128 devices in a mesh: rep: 16 (over y, x_lo, core), shard: 8 (over x_hi, z).
Axes of the slice: x: 4 (x_hi: 2, x_lo: 2; x = x_hi * 2 + x_lo), y: 4, z: 4, core: 2. Of those that a mesh axis runs over, the one named last changes fastest.
Arguments:
- tokens: bfloat16 [32768, 1024], P(('rep', 'shard')), may hold values from -6 to 6
- out_grad: bfloat16 [32768, 1024], P(('rep', 'shard')), may hold values from -6 to 6
- segments: int32 [32768], P(('rep', 'shard')), may hold values from 0 to 4, as said below
- w_qkv: float32 [1024, 3072], P('shard'), may hold values from -0.1875 to 0.1875
- w_proj: float32 [1024, 1024], P('shard'), may hold values from -0.5 to 0.5
- w_up: float32 [1024, 4096], P('shard'), may hold values from -0.1875 to 0.1875
- w_down: float32 [1024, 4096], P('shard'), may hold values from -0.09375 to 0.09375
- norm_params: float32 [4, 1024], P(None, 'shard'), may hold values from -1 to 1.4
- biases: float32 [9216], P('shard'), may hold values from -1.5 to 1.5
- prior_moment_qkv: float32 [1024, 3072], P('shard'), may hold values from -64 to 64
- prior_square_qkv: float32 [1024, 3072], P('shard'), may hold values from 425.984 to 1736.704
- prior_moment_proj: float32 [1024, 1024], P('shard'), may hold values from -24 to 24
- prior_square_proj: float32 [1024, 1024], P('shard'), may hold values from 68.8128 to 275.2512
- prior_moment_up: float32 [1024, 4096], P('shard'), may hold values from -32 to 32
- prior_square_up: float32 [1024, 4096], P('shard'), may hold values from 157.2864 to 622.592
- prior_moment_down: float32 [1024, 4096], P('shard'), may hold values from -64 to 64
- prior_square_down: float32 [1024, 4096], P('shard'), may hold values from 622.592 to 2490.368
- prior_moment_norm: float32 [4, 1024], P(None, 'shard'), may hold values from -64 to 64
- prior_square_norm: float32 [4, 1024], P(None, 'shard'), may hold values from 425.984 to 1736.704
- prior_moment_bias: float32 [9216], P('shard'), may hold values from -64 to 64
- prior_square_bias: float32 [9216], P('shard'), may hold values from 425.984 to 1736.704
Outputs:
- block_out: bfloat16 [32768, 1024], P(('rep', 'shard'))
- grad_tokens: float32 [32768, 1024], P(('rep', 'shard'))
- updated_qkv: float32 [1024, 3072], P('shard')
- moment_qkv: float32 [1024, 3072], P('shard')
- square_qkv: float32 [1024, 3072], P('shard')
- updated_proj: float32 [1024, 1024], P('shard')
- moment_proj: float32 [1024, 1024], P('shard')
- square_proj: float32 [1024, 1024], P('shard')
- updated_up: float32 [1024, 4096], P('shard')
- moment_up: float32 [1024, 4096], P('shard')
- square_up: float32 [1024, 4096], P('shard')
- updated_down: float32 [1024, 4096], P('shard')
- moment_down: float32 [1024, 4096], P('shard')
- square_down: float32 [1024, 4096], P('shard')
- updated_norm: float32 [4, 1024], P(None, 'shard')
- moment_norm: float32 [4, 1024], P(None, 'shard')
- square_norm: float32 [4, 1024], P(None, 'shard')
- updated_bias: float32 [9216], P('shard')
- moment_bias: float32 [9216], P('shard')
- square_bias: float32 [9216], P('shard')
The draws below stay inside these ranges and needn't reach their ends.
Inputs may be any that keep to these rules, and one draw needn't show every extreme that they name: `segments`: within each sequence of 2048 tokens the numbers never fall and run 0, 1, 2, 3, 4: five documents; the first two together, and the last two together, hold 64 to 128 tokens.
All inputs are finite; a program needn't handle non-finite values.
Results may differ from the reference program's by a relative error of at most 0.012.
Values may be sent and summed in bfloat16 or wider, within the bound.
No kernel may reach another device: no remote copies, remote signals or barrier semaphores. Data moves between devices by JAX's collectives and lax.ppermute only.
A program may use at most 320 MiB of HBM per device.

```python
import math
from functools import partial
import jax
import jax.numpy as jnp
from jax import lax

D = 1024
HEADS = 16
HEAD_DIM = 64
FF = 4096
ROT = 16
STEP = 10
ROWS = 256
SEQ = 2048
SEQS = 16
TOKENS = 32768


def draw_segments(key, part):
    key = jax.random.fold_in(key, 11)
    first_key, last_key, first_cut_key, last_cut_key = jax.random.split(key, 4)
    head_len = jax.random.randint(first_key, (SEQS, 1), ROWS // 4, ROWS // 2 + 1)
    tail_len = jax.random.randint(last_key, (SEQS, 1), ROWS // 4, ROWS // 2 + 1)
    head_cut = jax.random.randint(first_cut_key, (SEQS, 1), 1, head_len)
    tail_cut = jax.random.randint(last_cut_key, (SEQS, 1), 1, tail_len)
    token_ids = jnp.arange(SEQ, dtype=jnp.int32)[None, :]
    numbers = (token_ids >= head_cut).astype(jnp.int32) + (token_ids >= head_len).astype(jnp.int32) + (token_ids >= SEQ - tail_len).astype(jnp.int32) + (token_ids >= SEQ - tail_cut).astype(jnp.int32)
    return numbers.reshape(TOKENS)


def draw_norm_params(key, part):
    key = jax.random.fold_in(key, 7)
    gain_key, shift_key = jax.random.split(key)
    gains = jnp.clip(1.0 + 0.15 * jax.random.normal(gain_key, (2, D), jnp.float32), 0.6, 1.4)
    shifts = jnp.clip(0.3 * jax.random.normal(shift_key, (2, D), jnp.float32), -1.0, 1.0)
    return jnp.stack([gains[0], shifts[0], gains[1], shifts[1]], axis=0)


def block_levels(stream_key, extent, shards, smallest, largest):
    def one(dim, blocks):
        draws = jax.random.uniform(jax.random.fold_in(jax.random.fold_in(stream_key, 6), dim), (blocks,), jnp.float32, smallest / len(shards), largest / len(shards))
        return jnp.repeat(jnp.exp(draws), extent[dim] // blocks).reshape((-1,) + (1,) * (len(extent) - dim - 1))

    factor_of = one(*shards[0])
    for cut in shards[1:]:
        factor_of = factor_of * one(*cut)
    return factor_of


def gaussian(own_key, dims, width, limit, cuts=(), kind=jnp.bfloat16):
    drawn = width * jax.random.normal(own_key, dims, jnp.float32)
    if cuts:
        drawn = drawn * block_levels(own_key, dims, cuts, -0.22, 0.18)
    return jnp.clip(drawn, -limit, limit).astype(kind)


def setup_inputs(seed: int = 0) -> dict:
    seeds = jax.random.split(jax.random.key(seed), 22)
    tokens = gaussian(seeds[0], (TOKENS, D), 1.0, 6.0, ((0, 128),))
    out_grad = gaussian(seeds[1], (TOKENS, D), 1.0, 6.0, ((0, 128),))
    segments = draw_segments(jax.random.fold_in(seeds[21], 71), 0)
    w_qkv = gaussian(seeds[3], (D, 3 * D), D ** -0.5, 0.1875, ((0, 8),), jnp.float32)
    w_proj = gaussian(seeds[4], (D, D), (D // 8) ** -0.5, 0.5, ((0, 8),), jnp.float32)
    w_up = gaussian(seeds[5], (D, FF), D ** -0.5, 0.1875, ((0, 8),), jnp.float32)
    w_down = gaussian(seeds[6], (D, FF), FF ** -0.5, 0.09375, ((0, 8),), jnp.float32)
    norm_params = draw_norm_params(jax.random.fold_in(seeds[21], 71), 0)
    biases = gaussian(seeds[8], (5 * D + FF,), 0.3, 1.5, ((0, 8),), jnp.float32)
    prior_moment_qkv = gaussian(seeds[9], (D, 3 * D), (0.055 * TOKENS ** 0.5), 64.0, ((0, 8),), jnp.float32)
    prior_square_qkv = jnp.clip(jnp.exp(math.log(1736.704) - 1.40534252 * jax.random.uniform(seeds[10], (D, 3 * D), jnp.float32) ** block_levels(seeds[10], (D, 3 * D), ((0, 8),), -0.2, 0.2)), 425.984, 1736.704)
    prior_moment_proj = gaussian(seeds[11], (D, D), (0.022 * TOKENS ** 0.5), 24.0, ((0, 8),), jnp.float32)
    prior_square_proj = jnp.clip(jnp.exp(math.log(275.2512) - 1.3862944 * jax.random.uniform(seeds[12], (D, D), jnp.float32) ** block_levels(seeds[12], (D, D), ((0, 8),), -0.2, 0.2)), 68.8128, 275.2512)
    prior_moment_up = gaussian(seeds[13], (D, FF), (0.033 * TOKENS ** 0.5), 32.0, ((0, 8),), jnp.float32)
    prior_square_up = jnp.clip(jnp.exp(math.log(622.592) - 1.375823 * jax.random.uniform(seeds[14], (D, FF), jnp.float32) ** block_levels(seeds[14], (D, FF), ((0, 8),), -0.2, 0.2)), 157.2864, 622.592)
    prior_moment_down = gaussian(seeds[15], (D, FF), (0.066 * TOKENS ** 0.5), 64.0, ((0, 8),), jnp.float32)
    prior_square_down = jnp.clip(jnp.exp(math.log(2490.368) - 1.3862944 * jax.random.uniform(seeds[16], (D, FF), jnp.float32) ** block_levels(seeds[16], (D, FF), ((0, 8),), -0.2, 0.2)), 622.592, 2490.368)
    prior_moment_norm = gaussian(seeds[17], (4, D), (0.055 * TOKENS ** 0.5), 64.0, ((1, 8),), jnp.float32)
    prior_square_norm = jnp.clip(jnp.exp(math.log(1736.704) - 1.40534252 * jax.random.uniform(seeds[18], (4, D), jnp.float32) ** block_levels(seeds[18], (4, D), ((1, 8),), -0.2, 0.2)), 425.984, 1736.704)
    prior_moment_bias = gaussian(seeds[19], (5 * D + FF,), (0.055 * TOKENS ** 0.5), 64.0, ((0, 8),), jnp.float32)
    prior_square_bias = jnp.clip(jnp.exp(math.log(1736.704) - 1.40534252 * jax.random.uniform(seeds[20], (5 * D + FF,), jnp.float32) ** block_levels(seeds[20], (5 * D + FF,), ((0, 8),), -0.2, 0.2)), 425.984, 1736.704)
    return dict(tokens=tokens, out_grad=out_grad, segments=segments, w_qkv=w_qkv, w_proj=w_proj, w_up=w_up, w_down=w_down, norm_params=norm_params, biases=biases, prior_moment_qkv=prior_moment_qkv, prior_square_qkv=prior_square_qkv, prior_moment_proj=prior_moment_proj, prior_square_proj=prior_square_proj, prior_moment_up=prior_moment_up, prior_square_up=prior_square_up, prior_moment_down=prior_moment_down, prior_square_down=prior_square_down, prior_moment_norm=prior_moment_norm, prior_square_norm=prior_square_norm, prior_moment_bias=prior_moment_bias, prior_square_bias=prior_square_bias)


EPS_NORM = 1e-05
BETA_ONE = 0.9
BETA_TWO = 0.95
RATE_MATRIX = 0.05
RATE_VECTOR = 0.3
DECAY = 0.01
ADAM_EPS = 1e-08
NEGATIVE = -1e+30
HIGHEST = lax.Precision.HIGHEST

@jax.custom_vjp
def low(v):
    return lax.optimization_barrier(v.astype(jnp.bfloat16)).astype(jnp.float32)

@jax.custom_vjp
def low_back(v):
    return v

def low_keep(v):
    return (low(v), None)

def low_pass(kept, grad):
    return (grad,)

def back_keep(v):
    return (v, None)

def back_low(kept, grad):
    return (low(grad),)
low.defvjp(low_keep, low_pass)
low_back.defvjp(back_keep, back_low)

def matmul(left, right):
    return jnp.dot(left, right, precision=HIGHEST, preferred_element_type=jnp.float32)

def layer_norm(values, norm_gain, norm_shift):
    centred = values - lax.optimization_barrier(jnp.mean(values, axis=-1, keepdims=True))
    spread = lax.optimization_barrier(jnp.mean(centred * centred, axis=-1, keepdims=True))
    return centred * lax.rsqrt(spread + EPS_NORM) * norm_gain + norm_shift

def gelu_exact(values):
    return jax.nn.gelu(values, approximate=False)

def rotary_tables(positions):
    rot_half = ROT // 2
    frequency = 10000.0 ** (-2.0 * jnp.arange(rot_half, dtype=jnp.float32) / ROT)
    angles = positions.astype(jnp.float32)[:, None] * frequency[None, :]
    angles = jnp.concatenate([angles, angles], axis=-1)
    return (jnp.cos(angles), jnp.sin(angles))

def rotate(values, cosine, sine):
    rot_half = ROT // 2
    rot_head = values[..., :ROT]
    turned = jnp.concatenate([-rot_head[..., rot_half:], rot_head[..., :rot_half]], axis=-1)
    rotated = rot_head * cosine[:, None, :] + turned * sine[:, None, :]
    return jnp.concatenate([rotated, values[..., ROT:]], axis=-1)

def attention(queries, key_heads, value_heads, token_ids, doc_ids):
    seq_rows = queries.shape[0]
    block_rows = min(512, seq_rows)
    block_count = seq_rows // block_rows

    def one_block(block):
        query_block, query_ids, query_docs = block
        scores = jnp.einsum('qhd,khd->hqk', query_block, key_heads, precision=HIGHEST) * 0.125
        scores = low_back(scores)
        allowed = (token_ids[None, :] <= query_ids[:, None]) & (doc_ids[None, :] == query_docs[:, None])
        top_score = lax.optimization_barrier(jnp.max(jnp.where(allowed[None], scores, NEGATIVE), axis=-1, keepdims=True))
        expo_vals = jnp.where(allowed[None], jnp.exp(scores - top_score), 0.0)
        row_total = lax.optimization_barrier(jnp.sum(expo_vals, axis=-1))
        merged = jnp.einsum('hqk,khd->qhd', low(expo_vals), value_heads, precision=HIGHEST)
        merged = low_back(merged)
        return merged / row_total.T[:, :, None]
    blocks = (queries.reshape(block_count, block_rows, HEADS, HEAD_DIM), token_ids.reshape(block_count, block_rows), doc_ids.reshape(block_count, block_rows))
    return lax.map(jax.checkpoint(one_block), blocks).reshape(seq_rows, HEADS, HEAD_DIM)

def block_forward(seq_input, w_qkv, w_proj, w_up, w_down, norm_params, biases, doc_ids):
    seq_rows = seq_input.shape[0]
    model_width = seq_input.shape[1]
    ffn_width = w_up.shape[1]
    token_ids = jnp.arange(seq_rows, dtype=jnp.int32)
    doc_start = lax.optimization_barrier(jnp.sum((doc_ids[None, :] < doc_ids[:, None]).astype(jnp.int32), axis=1))
    cosine, sine = rotary_tables(token_ids - doc_start)
    gains = low(norm_params)
    shifts = low(biases)
    normed_one = low(layer_norm(seq_input, gains[0], gains[1]))
    qkv_vals = low_back(matmul(normed_one, low(w_qkv)) + shifts[:3 * model_width])
    query_part = qkv_vals[:, :model_width].reshape(seq_rows, HEADS, HEAD_DIM)
    key_part = qkv_vals[:, model_width:2 * model_width].reshape(seq_rows, HEADS, HEAD_DIM)
    value_part = qkv_vals[:, 2 * model_width:].reshape(seq_rows, HEADS, HEAD_DIM)
    queries = low(rotate(query_part, cosine, sine))
    key_heads = low(rotate(key_part, cosine, sine))
    value_heads = low(value_part)
    context = attention(queries, key_heads, value_heads, token_ids, doc_ids)
    context = low(context.reshape(seq_rows, model_width))
    attn_out = matmul(context, low(w_proj)) + shifts[3 * model_width:4 * model_width]
    normed_two = low(layer_norm(seq_input, gains[2], gains[3]))
    pre_act = low_back(matmul(normed_two, low(w_up)) + shifts[4 * model_width:4 * model_width + ffn_width])
    hidden = low(gelu_exact(pre_act))
    down_out = matmul(hidden, low(w_down).T) + shifts[4 * model_width + ffn_width:]
    return seq_input + attn_out + down_out

def adam_step(weight, moment, square, gradient, rate, decay):
    moment_new = BETA_ONE * moment + (1.0 - BETA_ONE) * gradient
    square_new = BETA_TWO * square + (1.0 - BETA_TWO) * gradient * gradient
    fixed_moment = moment_new / (1.0 - BETA_ONE ** STEP)
    fixed_square = square_new / (1.0 - BETA_TWO ** STEP)
    weight_new = weight - rate * (fixed_moment / (jnp.sqrt(fixed_square) + ADAM_EPS) + decay * weight)
    return (weight_new, moment_new, square_new)

def reference(tokens, out_grad, segments, w_qkv, w_proj, w_up, w_down, norm_params, biases, prior_moment_qkv, prior_square_qkv, prior_moment_proj, prior_square_proj, prior_moment_up, prior_square_up, prior_moment_down, prior_square_down, prior_moment_norm, prior_square_norm, prior_moment_bias, prior_square_bias):
    inputs = tokens.astype(jnp.float32).reshape(SEQS, SEQ, D)
    cotangents = out_grad.astype(jnp.float32).reshape(SEQS, SEQ, D)
    documents = segments.reshape(SEQS, SEQ)
    params = (w_qkv, w_proj, w_up, w_down, norm_params, biases)

    def one_sequence(totals, sequence):
        seq_input, seq_cotangent, seq_docs = sequence
        primal, pullback = jax.vjp(partial(block_forward, doc_ids=seq_docs), seq_input, *params)
        gradients = pullback(seq_cotangent)
        totals = tuple((summed + gradient for summed, gradient in zip(totals, gradients[1:])))
        return (totals, (primal.astype(jnp.bfloat16), gradients[0]))
    zero_grads = tuple((jnp.zeros_like(param) for param in params))
    totals, (outputs, input_grads) = lax.scan(one_sequence, zero_grads, (inputs, cotangents, documents))
    block_out = outputs.reshape(TOKENS, D)
    grad_tokens = input_grads.reshape(TOKENS, D)
    new_qkv = adam_step(w_qkv, prior_moment_qkv, prior_square_qkv, totals[0], RATE_MATRIX, DECAY)
    new_proj = adam_step(w_proj, prior_moment_proj, prior_square_proj, totals[1], RATE_MATRIX, DECAY)
    new_up = adam_step(w_up, prior_moment_up, prior_square_up, totals[2], RATE_MATRIX, DECAY)
    new_down = adam_step(w_down, prior_moment_down, prior_square_down, totals[3], RATE_MATRIX, DECAY)
    new_norm = adam_step(norm_params, prior_moment_norm, prior_square_norm, totals[4], RATE_VECTOR, 0.0)
    new_bias = adam_step(biases, prior_moment_bias, prior_square_bias, totals[5], RATE_VECTOR, 0.0)
    return (block_out, grad_tokens, new_qkv[0], new_qkv[1], new_qkv[2], new_proj[0], new_proj[1], new_proj[2], new_up[0], new_up[1], new_up[2], new_down[0], new_down[1], new_down[2], new_norm[0], new_norm[1], new_norm[2], new_bias[0], new_bias[1], new_bias[2])
```

```python
import functools

import jax
import jax.numpy as jnp
import numpy as np
from jax import lax
from jax.experimental import pallas as pl
from jax.experimental.pallas import tpu as pltpu
from jax.sharding import PartitionSpec as P

HEAD_DIM = 64
ROT = 16
STEP = 10
EPS_NORM = 1e-05
BETA_ONE = 0.9
BETA_TWO = 0.95
RATE_MATRIX = 0.05
RATE_VECTOR = 0.3
DECAY = 0.01
ADAM_EPS = 1e-08
NEGATIVE = -1e30

NY, NXL, NC, NXH, NZ = 4, 2, 2, 2, 4
AXES = ("rep", "shard")
D = 1024
ROWS = 256
SEQ = 2048
FF = 4096
PAIR = 128
HID = 512
QB = 512
BF = jnp.bfloat16
F32 = jnp.float32


def device_pairs(move):
    pairs = []
    for y in range(NY):
        for xl in range(NXL):
            for c in range(NC):
                for h in range(NXH):
                    for z in range(NZ):
                        ty, txl, tc, th, tz = move(y, xl, c, h, z)
                        pairs.append(
                            (
                                ((y * NXL + xl) * NC + c) * 8 + h * NZ + z,
                                ((ty * NXL + txl) * NC + tc) * 8 + th * NZ + tz % NZ,
                            )
                        )
    return pairs


def spread_pairs(k):
    def move(y, xl, c, h, z):
        return (y, xl, h, c, z + k)

    return device_pairs(move)


SPREAD = [spread_pairs(k) for k in range(NZ)]
COLLECT = [[(t, s) for s, t in pairs] for pairs in SPREAD]
SIBLING = device_pairs(lambda y, xl, c, h, z: (y, xl, 1 - c, h, z))
ROUND_Z = [device_pairs(lambda y, xl, c, h, z, k=k: (y, xl, c, h, z + k)) for k in range(NZ)]


def device(y, xl, c, h, z):
    return ((y * NXL + xl) * NC + c) * 8 + h * NZ + z


RANGES = dict(y=range(NY), xl=range(NXL), c=range(NC), h=range(NXH), z=range(NZ))


def groups(*inner):
    outer = [name for name in RANGES if name not in inner]

    def walk(names, at):
        if not names:
            return [device(**at)]
        return [d for n in RANGES[names[0]] for d in walk(names[1:], dict(at, **{names[0]: n}))]

    def each(names, at):
        if not names:
            return [walk(inner, at)]
        return [g for n in RANGES[names[0]] for g in each(names[1:], dict(at, **{names[0]: n}))]

    return each(outer, {})


ALONG_Y = groups("y")
ALONG_Z = groups("z")
PLANE = groups("h", "y", "xl")
COPIES = groups("y", "xl")
SAME_CORE = groups("h", "z", "y", "xl")


def spread(blocks):
    return [lax.ppermute(b, AXES, SPREAD[k]) for k, b in enumerate(blocks)]


def collect(blocks):
    return [lax.ppermute(b, AXES, COLLECT[k]) for k, b in enumerate(blocks)]


def sibling(values):
    return lax.ppermute(values, AXES, SIBLING)


def exchange(values, members):
    return lax.all_to_all(values, AXES, 0, 0, axis_index_groups=members, tiled=True)


def dot(a, b, ca, cb):
    return lax.dot_general(a, b, (((ca,), (cb,)), ((), ())), preferred_element_type=F32)


def gelu_parts(values):
    cdf = 0.5 * (1.0 + lax.erf(values * np.float32(np.sqrt(0.5))))
    density = jnp.exp(-0.5 * values * values) * np.float32(1.0 / np.sqrt(2.0 * np.pi))
    return values * cdf, cdf + values * density


def adam_step(weight, moment, square, gradient, rate, decay):
    moment_new = BETA_ONE * moment + (1.0 - BETA_ONE) * gradient
    square_new = BETA_TWO * square + (1.0 - BETA_TWO) * gradient * gradient
    fixed_moment = moment_new / (1.0 - BETA_ONE**STEP)
    fixed_square = square_new / (1.0 - BETA_TWO**STEP)
    weight_new = weight - rate * (
        fixed_moment / (jnp.sqrt(fixed_square) + ADAM_EPS) + decay * weight
    )
    return (weight_new, moment_new, square_new)


SM = pl.BlockSpec(memory_space=pltpu.SMEM)
VM = pl.BlockSpec(memory_space=pltpu.VMEM)


def params(mib=16):
    return pltpu.CompilerParams(vmem_limit_bytes=mib * 2**20)


def cost(us):
    flops = int(us * 7e8)
    return pl.CostEstimate(flops=flops, bytes_accessed=int(us * 2e6), transcendentals=0)


def shape(dims, kind):
    return jax.ShapeDtypeStruct(dims, kind)


def send_weights_kernel(
    where_ref, w_ref, up_ref, down_ref, norm_ref, bias_ref, seg_ref, sib_ref, out_ref
):
    core = where_ref[0]
    misc = jnp.concatenate(
        [norm_ref[...], bias_ref[...], seg_ref[...].astype(F32), jnp.zeros((1, 128), F32)], axis=0
    ).astype(BF)
    theirs = jnp.concatenate([sib_ref[...].astype(F32), jnp.zeros((14, 128), F32)], axis=0).astype(BF)
    rows = pl.ds(pl.multiple_of(where_ref[2] * 32, 32), 32)
    for n in range(8):
        for part in range(3):
            source = pl.multiple_of(part * D + core * 512 + (n % NZ) * PAIR, PAIR)
            lanes = slice(part * PAIR, (part + 1) * PAIR)
            out_ref[n, 0:128, lanes] = w_ref[:, pl.ds(source, PAIR)].astype(BF)
        out_ref[n, 128:144, 0:128] = misc
        out_ref[n, 128:144, 128:256] = theirs
        out_ref[n, 128:144, 256:384] = jnp.zeros((16, 128), BF)
        for j in range(8):
            ref = (up_ref, down_ref)[j // 4]
            source = pl.multiple_of(core * 2048 + (n % NZ) * HID + (j % 4) * 128, 128)
            first = 144 + (j // 3) * 32
            out_ref[n, first : first + 32, (j % 3) * 128 : (j % 3 + 1) * 128] = ref[
                rows, pl.ds(source, 128)
            ].astype(BF)
        out_ref[n, 208:240, 256:384] = jnp.zeros((32, 128), BF)


def send_weights(where, w, up, down, norms, biases, segments, sibling_segments):
    return pl.pallas_call(
        send_weights_kernel,
        in_specs=[SM] + [VM] * 7,
        out_specs=VM,
        out_shape=shape((8, 240, 384), BF),
        compiler_params=params(),
        cost_estimate=cost(0),
        name="send_weights",
    )(where, w, up, down, norms, biases, segments, sibling_segments)


def join_kernel(*refs):
    for k in range(NZ):
        refs[NZ][k * ROWS : (k + 1) * ROWS, :] = refs[k][0:ROWS, :]


def join(blocks, us):
    return pl.pallas_call(
        join_kernel,
        in_specs=[VM] * NZ,
        out_specs=VM,
        out_shape=shape((SEQ // 2, D), BF),
        compiler_params=params(),
        cost_estimate=cost(us),
        name="join",
    )(*blocks)


def doc_start(ids, meta_ref):
    start = jnp.zeros_like(ids)
    for d in range(4):
        start = jnp.where(ids >= meta_ref[d], meta_ref[d], start)
    return start


def block_tables(where_ref, meta_ref):
    c, z = where_ref[0], where_ref[1]
    meta_ref[4] = c
    meta_ref[5] = z
    meta_ref[6] = c * NZ + z
    meta_ref[7] = where_ref[2]
    for j in range(2):
        half = c if j == 0 else 1 - c
        for k in range(NZ):
            meta_ref[8 + j * NZ + k] = half * NZ + jnp.bitwise_and(z + NZ - k, NZ - 1)
    for half in range(2):
        base = jnp.bitwise_xor(c, half) * NZ
        for ring in range(NZ):
            meta_ref[16 + half * NZ + ring] = base + jnp.bitwise_and(z + NZ - ring, NZ - 1)


def assemble_kernel(
    where_ref, in_ref, w_ref, norm_ref, bias_ref, ffn_ref, meta_ref
):
    block_tables(where_ref, meta_ref)
    counts = [jnp.zeros((1, 128), F32) for _ in range(4)]
    native = (where_ref[0] == where_ref[3]).astype(F32)
    for n in range(8):
        w_ref[n * 128 : (n + 1) * 128, :] = in_ref[n, 0:128, :]
        misc = in_ref[n, 128:144, 0:128].astype(F32)
        other = in_ref[n, 128:144, 128:256].astype(F32)
        norm_ref[:, n * 128 : (n + 1) * 128] = misc[0:4]
        bias_ref[n * 9 : (n + 1) * 9, :] = misc[4:13]
        docs = misc[13:15] * native + other[0:2] * (1.0 - native)
        for d in range(4):
            below = jnp.where(docs < d + 0.5, 1.0, 0.0)
            counts[d] = counts[d] + below[0:1] + below[1:2]
        for j in range(8):
            first = 144 + (j // 3) * 32
            block = in_ref[n, first : first + 32, (j % 3) * 128 : (j % 3 + 1) * 128]
            for y in range(NY):
                ffn_ref[y, n * 32 : (n + 1) * 32, j * 128 : (j + 1) * 128] = block
    for d in range(4):
        meta_ref[d] = jnp.sum(counts[d]).astype(jnp.int32)


def rotary_tables():
    lane = np.arange(PAIR) % HEAD_DIM
    freq = 10000.0 ** (-2.0 * (lane % (ROT // 2)) / ROT)
    angles = np.arange(SEQ)[:, None] * np.where(lane < ROT, freq, 0.0)[None, :]
    return jnp.asarray(np.cos(angles), F32), jnp.asarray(np.sin(angles), F32)


def assemble(where, received):
    return pl.pallas_call(
        assemble_kernel,
        in_specs=[SM, VM],
        out_specs=[VM] * 4 + [SM],
        out_shape=[
            shape((D, 3 * PAIR), BF),
            shape((4, D), F32),
            shape((72, 128), F32),
            shape((NY, ROWS, 2 * HID), BF),
            shape((24,), jnp.int32),
        ],
        compiler_params=params(),
        cost_estimate=cost(0),
        name="assemble",
    )(where, received)


def assemble_ffn_kernel(in_ref, up_ref, down_ref):
    for y in range(NY):
        for n in range(8):
            rows = slice(n * 128 + y * 32, n * 128 + (y + 1) * 32)
            up_ref[rows, :] = in_ref[y, n * 32 : (n + 1) * 32, 0:HID]
            down_ref[rows, :] = in_ref[y, n * 32 : (n + 1) * 32, HID:]


def assemble_ffn(parts):
    return pl.pallas_call(
        assemble_ffn_kernel,
        in_specs=[VM],
        out_specs=[VM] * 2,
        out_shape=[shape((D, HID), BF)] * 2,
        compiler_params=params(),
        cost_estimate=cost(0),
        name="assemble_ffn",
    )(parts)


def turn(u, cosine, sine):
    lane = lax.broadcasted_iota(jnp.int32, u.shape, 1) % HEAD_DIM
    left = pltpu.roll(u, PAIR - ROT // 2, 1)
    right = pltpu.roll(u, ROT // 2, 1)
    return u * cosine + jnp.where(lane < ROT // 2, -left, right) * sine


def qkv_kernel(meta_ref, x_ref, w_ref, bias_ref, norm_ref, cos_ref, sin_ref, *refs):
    n2_ref, xh_ref, q_ref, k_ref, v_ref = refs[-5:]
    x = x_ref[...].astype(F32)
    centred = x - jnp.mean(x, axis=-1, keepdims=True)
    variance = jnp.mean(centred * centred, axis=-1, keepdims=True)
    xh = centred * lax.rsqrt(variance + EPS_NORM)
    n1 = (xh * norm_ref[0:1, :] + norm_ref[1:2, :]).astype(BF)
    xh_ref[...] = xh.astype(BF)
    n2_ref[...] = (xh * norm_ref[2:3, :] + norm_ref[3:4, :]).astype(BF)
    part = meta_ref[6]
    cosine, sine = cos_ref[...], sin_ref[...]
    qkv = dot(n1, w_ref[...], 1, 0)
    q = qkv[:, 0:PAIR] + bias_ref[pl.ds(part, 1), :]
    k = qkv[:, PAIR : 2 * PAIR] + bias_ref[pl.ds(8 + part, 1), :]
    v = qkv[:, 2 * PAIR :] + bias_ref[pl.ds(16 + part, 1), :]
    q_ref[...] = (turn(q, cosine, sine).astype(BF) * 0.125).astype(BF)
    k_ref[...] = turn(k, cosine, sine).astype(BF)
    v_ref[...] = v.astype(BF)


def project_qkv(meta, x, w, bias, norms, cosine, sine, before, us):
    base = 0 if before is None else NZ
    moving = lambda i, meta: (i, 0)
    physical = lambda i, meta: (base + i, 0)
    logical = lambda i, meta: (meta[8 + base + i], 0)
    fixed = lambda i, meta: (0, 0)
    extra = [] if before is None else list(before)
    return pl.pallas_call(
        qkv_kernel,
        grid_spec=pltpu.PrefetchScalarGridSpec(
            num_scalar_prefetch=1,
            grid=(NZ,),
            in_specs=[
                pl.BlockSpec((ROWS, D), moving),
                pl.BlockSpec((D, 3 * PAIR), fixed),
                pl.BlockSpec((72, 128), fixed),
                pl.BlockSpec((4, D), fixed),
                pl.BlockSpec((ROWS, PAIR), logical),
                pl.BlockSpec((ROWS, PAIR), logical),
            ]
            + [pl.BlockSpec(memory_space=pl.ANY)] * len(extra),
            out_specs=[pl.BlockSpec((ROWS, D), physical)] * 2
            + [pl.BlockSpec((ROWS, PAIR), logical)] * 3,
        ),
        out_shape=[shape((SEQ, D), BF)] * 2 + [shape((SEQ, PAIR), BF)] * 3,
        input_output_aliases={7 + n: n for n in range(len(extra))},
        compiler_params=params(),
        cost_estimate=cost(us),
        name="project_qkv",
    )(meta, x, w, bias, norms, cosine, sine, *extra)


def head_only(values, h):
    lane = lax.broadcasted_iota(jnp.int32, values.shape, 1)
    return jnp.where((lane // HEAD_DIM) == h, values, jnp.zeros_like(values))


def tile_mask(meta_ref, i, j):
    keys = j * QB + lax.broadcasted_iota(jnp.int32, (QB, QB), 0)
    query_row = i * QB + lax.broadcasted_iota(jnp.int32, (1, QB), 1)
    start = doc_start(query_row, meta_ref)
    return (keys <= query_row) & (keys >= start)


def attn_forward_kernel(meta_ref, q_ref, k_ref, v_ref, ctx_ref, ctxt_ref, stat_ref, vt_ref):
    i = pl.program_id(0)

    @pl.when(i == 0)
    def _():
        for b in range(SEQ // QB):
            vt_ref[:, b * QB : (b + 1) * QB] = v_ref[b * QB : (b + 1) * QB, :].T

    q = q_ref[pl.ds(pl.multiple_of(i * QB, QB), QB), :]
    heads = [head_only(q, h) for h in range(2)]

    def step(j, carry):
        mask = tile_mask(meta_ref, i, j)
        row = pl.multiple_of(j * QB, QB)
        keys = k_ref[pl.ds(row, QB), :]
        out = []
        for h in range(2):
            m, l, acc = carry[h]
            scores = dot(keys, heads[h], 1, 1)
            scores = jnp.where(mask, scores, NEGATIVE)
            top = jnp.maximum(m, jnp.max(scores, axis=0, keepdims=True))
            expo = jnp.exp(scores - top)
            fade = jnp.exp(m - top)
            l = l * fade + jnp.sum(expo, axis=0, keepdims=True)
            values = vt_ref[h * HEAD_DIM : (h + 1) * HEAD_DIM, pl.ds(row, QB)]
            acc = acc * fade + dot(values, expo.astype(BF), 1, 0)
            out.append((top, l, acc))
        return tuple(out)

    zero = (
        jnp.full((1, QB), NEGATIVE, F32),
        jnp.zeros((1, QB), F32),
        jnp.zeros((HEAD_DIM, QB), F32),
    )
    result = lax.fori_loop(0, i + 1, step, (zero, zero))
    column = pl.multiple_of(i * QB, QB)
    parts = []
    for h in range(2):
        m, l, acc = result[h]
        parts.append(acc / l)
        stat_ref[h : h + 1, pl.ds(column, QB)] = m
        stat_ref[2 + h : 3 + h, pl.ds(column, QB)] = 1.0 / l
    ctxt = jnp.concatenate(parts, axis=0)
    ctxt_ref[:, pl.ds(column, QB)] = ctxt
    low = ctxt.astype(BF).T
    for b in range(QB // ROWS):
        row = pl.multiple_of(meta_ref[16 + i * (QB // ROWS) + b] * ROWS, ROWS)
        ctx_ref[pl.ds(row, ROWS), :] = low[b * ROWS : (b + 1) * ROWS]


def attn_forward(meta, q, k, v):
    return pl.pallas_call(
        attn_forward_kernel,
        grid=(SEQ // QB,),
        in_specs=[SM, VM, VM, VM],
        out_specs=[VM, VM, VM],
        out_shape=[shape((SEQ, PAIR), BF), shape((PAIR, SEQ), F32), shape((8, SEQ), F32)],
        scratch_shapes=[pltpu.VMEM((PAIR, SEQ), BF)],
        compiler_params=params(),
        cost_estimate=cost(0),
        name="attn_forward",
    )(meta, q, k, v)


def attn_prepare_kernel(
    q_ref, k_ref, dctx_ref, ctxt_ref, stat_ref, kt_ref, du_ref, dut_ref, qh_ref, c_ref
):
    c_ref[...] = jnp.zeros_like(c_ref)
    for b in range(SEQ // QB):
        cols = slice(b * QB, (b + 1) * QB)
        kt_ref[:, cols] = k_ref[cols, :].T
        dctxt = dctx_ref[cols, :].T
        prod = dctxt * ctxt_ref[:, cols]
        for h in range(2):
            rows = slice(h * HEAD_DIM, (h + 1) * HEAD_DIM)
            inverse = stat_ref[2 + h : 3 + h, cols]
            c_ref[h : h + 1, cols] = jnp.sum(prod[rows], axis=0, keepdims=True) * inverse
            dut = (dctxt[rows] * inverse).astype(BF)
            dut_ref[h, rows, cols] = dut
            dut_ref[h, (1 - h) * HEAD_DIM : (2 - h) * HEAD_DIM, cols] = jnp.zeros_like(dut)
        for h in range(2):
            du_ref[h, cols, :] = dut_ref[h, :, cols].T
            qh_ref[h, cols, :] = head_only(q_ref[cols, :], h)


def attn_prepare(q, k, dctx, ctxt, stat):
    return pl.pallas_call(
        attn_prepare_kernel,
        in_specs=[VM] * 5,
        out_specs=[VM] * 5,
        out_shape=[
            shape((PAIR, SEQ), BF),
            shape((2, SEQ, PAIR), BF),
            shape((2, PAIR, SEQ), BF),
            shape((2, SEQ, PAIR), BF),
            shape((8, SEQ), F32),
        ],
        compiler_params=params(),
        cost_estimate=cost(60),
        name="attn_prepare",
    )(q, k, dctx, ctxt, stat)


def attn_backward_kernel(
    meta_ref, k_ref, v_ref, stat_ref, cos_ref, sin_ref, kt_ref, du_ref, dut_ref, qh_ref, c_ref,
    out_ref,
    dqt_ref, dk_ref, dv_ref,
):
    j = pl.program_id(0)
    blocks = SEQ // QB

    @pl.when(j == 0)
    def _():
        dqt_ref[...] = jnp.zeros_like(dqt_ref)

    row = pl.multiple_of(j * QB, QB)
    keys = k_ref[pl.ds(row, QB), :]
    values = v_ref[pl.ds(row, QB), :]

    def step(i, carry):
        dk, dv = carry
        mask = tile_mask(meta_ref, i, j)
        col = pl.multiple_of(i * QB, QB)
        for h in range(2):
            qh = qh_ref[h, pl.ds(col, QB), :]
            scores = dot(keys, qh, 1, 1)
            m = stat_ref[h : h + 1, pl.ds(col, QB)]
            expo = jnp.where(mask, jnp.exp(scores - m), 0.0)
            dexpo = dot(values, dut_ref[h, :, pl.ds(col, QB)], 1, 0)
            dscore = (expo * (dexpo - c_ref[h : h + 1, pl.ds(col, QB)])).astype(BF)
            dv = dv + dot(expo.astype(BF), du_ref[h, pl.ds(col, QB), :], 1, 0)
            dk = dk + dot(dscore, qh, 1, 0)
            rows = slice(h * HEAD_DIM, (h + 1) * HEAD_DIM)
            dqt_ref[rows, pl.ds(col, QB)] += dot(kt_ref[rows, pl.ds(row, QB)], dscore, 1, 0)
        return dk, dv

    zero = jnp.zeros((QB, PAIR), F32)
    dk, dv = lax.fori_loop(j, blocks, step, (zero, zero))
    dk_ref[pl.ds(row, QB), :] = dk
    dv_ref[pl.ds(row, QB), :] = dv

    @pl.when(j == blocks - 1)
    def _():
        for b in range(SEQ // ROWS):
            rows = slice(b * ROWS, (b + 1) * ROWS)
            place = pl.ds(pl.multiple_of(meta_ref[16 + b] * ROWS, ROWS), ROWS)
            cosine, sine = cos_ref[rows, :], -sin_ref[rows, :]
            dq = (dqt_ref[:, rows] * 0.125).T
            out_ref[place, 0:PAIR] = turn(dq, cosine, sine).astype(BF)
            out_ref[place, PAIR : 2 * PAIR] = turn(dk_ref[rows, :], cosine, sine).astype(BF)
            out_ref[place, 2 * PAIR :] = dv_ref[rows, :].astype(BF)


def attn_backward(meta, k, v, stat, cosine, sine, prepared):
    return pl.pallas_call(
        attn_backward_kernel,
        grid=(SEQ // QB,),
        in_specs=[SM] + [VM] * 10,
        out_specs=VM,
        out_shape=shape((SEQ, 3 * PAIR), BF),
        scratch_shapes=[
            pltpu.VMEM((PAIR, SEQ), F32),
            pltpu.VMEM((SEQ, PAIR), F32),
            pltpu.VMEM((SEQ, PAIR), F32),
        ],
        compiler_params=params(),
        cost_estimate=cost(100),
        name="attn_backward",
    )(meta, k, v, stat, cosine, sine, *prepared)


def lay_rows(ref, first, count):
    return jnp.concatenate([ref[pl.ds(first + r, 1), :] for r in range(count)], axis=1)


def by_half(double):
    return [
        pl.BlockSpec((double, D), lambda i, meta: (jnp.minimum(i, 1), 0)),
        pl.BlockSpec((double, D), lambda i, meta: (jnp.maximum(i - 2, 0), 0)),
    ]


def take_half(step, mine_ref, theirs_ref, now_ref):
    @pl.when(step < 2)
    def _():
        now_ref[...] = mine_ref[...]

    @pl.when(step >= 2)
    def _():
        now_ref[...] = theirs_ref[...]


def ffn_kernel(meta_ref, *refs):
    mine_ref, theirs_ref = refs[:2]
    n2_ref, xh_ref, ctx_ref, up_ref, down_ref, proj_ref, bias_ref, norm_ref = refs[2:10]
    out_mine_ref, out_theirs_ref, back_ref, dctx_ref, vec_ref, grad_ref = refs[10:16]
    dy_now, gup, gdown, gproj, total = refs[16:]
    step = pl.program_id(0)
    part = meta_ref[6]

    @pl.when(step == 0)
    def _():
        gup[...] = jnp.zeros_like(gup)
        gdown[...] = jnp.zeros_like(gdown)
        gproj[...] = jnp.zeros_like(gproj)
        total[...] = jnp.zeros_like(total)

    take_half(step, mine_ref, theirs_ref, dy_now)
    dy = dy_now[...]
    ctx = ctx_ref[...]
    dctx = dot(dy, proj_ref[...], 1, 1)
    for b in range(2):
        row = pl.multiple_of(meta_ref[8 + 2 * step + b] * ROWS, ROWS)
        dctx_ref[pl.ds(row, ROWS), :] = dctx[b * ROWS : (b + 1) * ROWS]
    gproj[...] += dot(ctx, dy, 0, 0)
    bias_up = lay_rows(bias_ref, 32 + 4 * part, 4)
    pre = dot(n2_ref[...], up_ref[...], 1, 0) + bias_up
    hidden, slope = gelu_parts(pre)
    hidden = hidden.astype(BF)
    dpre = (dot(dy, down_ref[...], 1, 0) * slope).astype(BF)
    out = (dot(ctx, proj_ref[...], 1, 0) + dot(hidden, down_ref[...], 1, 1)).astype(BF)

    @pl.when(step < 2)
    def _():
        out_mine_ref[...] = out

    @pl.when(step >= 2)
    def _():
        out_theirs_ref[...] = out

    back_ref[...] = (dot(dpre, up_ref[...], 1, 1) * norm_ref[2:3, :]).astype(BF)
    gdown[...] += dot(dy, hidden, 0, 0)
    gup[...] += dot(xh_ref[...], dpre, 0, 0)
    total[...] += jnp.broadcast_to(jnp.sum(dpre.astype(F32), axis=0, keepdims=True), total.shape)

    @pl.when(step == 3)
    def _():
        sums = total[...]
        raw = gup[...]
        gain = jnp.transpose(jnp.broadcast_to(norm_ref[2:3, :], (8, D)))[:, 0:1]
        shift = jnp.transpose(jnp.broadcast_to(norm_ref[3:4, :], (8, D)))[:, 0:1]
        product = (raw * up_ref[...].astype(F32)).astype(BF)
        gup[...] = raw * gain + shift * sums[0:1, :]
        for h in range(NXH):
            for p in range(8):
                for ring in range(NZ):
                    first = h * 512 + ring * 128 + p * 16
                    here = slice(ring * 16, (ring + 1) * 16)
                    grad_ref[h * 8 + p, here, 0:HID] = gup[first : first + 16, :].astype(BF)
                    grad_ref[h * 8 + p, here, HID:] = gdown[first : first + 16, :].astype(BF)
                grad_ref[h * 8 + p, 64:80, :] = gproj[p * 16 : (p + 1) * 16, :].astype(BF)
        vec_ref[0:8, :] = dot(jnp.ones((8, HID), BF), product, 1, 1)
        vec_ref[8:16, :] = dot(sums.astype(BF), up_ref[...], 1, 1)
        vec_ref[16:24, 0:HID] = sums
        vec_ref[16:24, HID:] = jnp.zeros((8, D - HID), F32)


def feed_forward(meta, mine, theirs, n2, xh, ctx, up, down, proj, bias, norms):
    double = 2 * ROWS
    moving = lambda i, meta: (i, 0)
    fixed = lambda i, meta: (0, 0)
    once = pl.Buffered(1)
    return pl.pallas_call(
        ffn_kernel,
        grid_spec=pltpu.PrefetchScalarGridSpec(
            num_scalar_prefetch=1,
            grid=(4,),
            in_specs=by_half(double)
            + [
                pl.BlockSpec((double, D), moving),
                pl.BlockSpec((double, D), moving),
                pl.BlockSpec((double, PAIR), moving),
                pl.BlockSpec((D, HID), fixed, pipeline_mode=once),
                pl.BlockSpec((D, HID), fixed, pipeline_mode=once),
                pl.BlockSpec((PAIR, D), lambda i, meta: (2, 0), pipeline_mode=once),
                pl.BlockSpec((72, 128), fixed, pipeline_mode=once),
                pl.BlockSpec((4, D), fixed, pipeline_mode=once),
            ],
            out_specs=by_half(double)
            + [
                pl.BlockSpec((double, D), moving),
                VM,
                VM,
                VM,
            ],
            scratch_shapes=[
                pltpu.VMEM((double, D), BF),
                pltpu.VMEM((D, HID), F32),
                pltpu.VMEM((D, HID), F32),
                pltpu.VMEM((PAIR, D), F32),
                pltpu.VMEM((8, HID), F32),
            ],
        ),
        out_shape=[
            shape((SEQ // 2, D), BF),
            shape((SEQ // 2, D), BF),
            shape((SEQ, D), BF),
            shape((SEQ, PAIR), F32),
            shape((24, D), F32),
            shape((16, 80, 2 * HID), BF),
        ],
        compiler_params=params(32),
        cost_estimate=cost(60),
        name="feed_forward",
    )(meta, mine, theirs, n2, xh, ctx, up, down, proj, bias, norms)


def core_sum_kernel(mine_ref, theirs_ref, *sent_refs):
    step = pl.program_id(0)
    total = (mine_ref[...].astype(F32) + theirs_ref[...].astype(F32)).astype(BF)
    for k in range(NZ):

        @pl.when(step == k)
        def _():
            sent_refs[k][...] = total


def core_sum(mine, theirs):
    moving = lambda i: (i, 0)
    return pl.pallas_call(
        core_sum_kernel,
        grid=(NZ,),
        in_specs=[pl.BlockSpec((ROWS, D), moving)] * 2,
        out_specs=[pl.BlockSpec((ROWS, D), lambda i: (0, 0))] * NZ,
        out_shape=[shape((ROWS, D), BF)] * NZ,
        compiler_params=params(),
        cost_estimate=cost(0),
        name="core_sum",
    )(mine, theirs)


def finish_out_kernel(x_ref, bias_ref, *refs):
    bias = lay_rows(bias_ref, 24, 8) + lay_rows(bias_ref, 64, 8)
    total = refs[0][...].astype(F32)
    for k in range(1, NZ):
        total = total + refs[k][...].astype(F32)
    refs[NZ][...] = (x_ref[...].astype(F32) + total + bias).astype(BF)


def finish_out(x, bias, pieces):
    return pl.pallas_call(
        finish_out_kernel,
        in_specs=[VM] * (2 + NZ),
        out_specs=VM,
        out_shape=shape((ROWS, D), BF),
        compiler_params=params(),
        cost_estimate=cost(0),
        name="finish_out",
    )(x, bias, *pieces)


def finish_grad_kernel(x_ref, dy_ref, *refs):
    w = refs[0][...].astype(F32)
    for k in range(1, NZ):
        w = w + refs[k][...].astype(F32)
    x = x_ref[...].astype(F32)
    centred = x - jnp.mean(x, axis=-1, keepdims=True)
    rstd = lax.rsqrt(jnp.mean(centred * centred, axis=-1, keepdims=True) + EPS_NORM)
    xh = centred * rstd
    inner = w - jnp.mean(w, axis=-1, keepdims=True) - xh * jnp.mean(w * xh, axis=-1, keepdims=True)
    refs[NZ][...] = dy_ref[...].astype(F32) + rstd * inner


def finish_grad(x, dy, pieces):
    return pl.pallas_call(
        finish_grad_kernel,
        in_specs=[VM] * (2 + NZ),
        out_specs=VM,
        out_shape=shape((ROWS, D), F32),
        compiler_params=params(),
        cost_estimate=cost(0),
        name="finish_grad",
    )(x, dy, *pieces)


def ffn_reduce_kernel(where_ref, in_ref, own_ref, *sent_refs):
    z = where_ref[1]
    total = in_ref[0].astype(F32)
    for n in range(1, 16):
        total = total + in_ref[n].astype(F32)
    low = total.astype(BF)
    own_ref[16:32, :] = low[64:80]
    for n in range(NZ):
        step = jnp.bitwise_and(n + NZ - z, NZ - 1)

        @pl.when(step == 0)
        def _():
            own_ref[0:16, :] = low[n * 16 : (n + 1) * 16]

        for k in (1, 2, 3):

            @pl.when(step == k)
            def _():
                sent_refs[k - 1][...] = low[n * 16 : (n + 1) * 16]


def ffn_reduce(where, received):
    return pl.pallas_call(
        ffn_reduce_kernel,
        in_specs=[SM, VM],
        out_specs=[VM] * NZ,
        out_shape=[shape((32, 2 * HID), BF)] + [shape((16, 2 * HID), BF)] * 3,
        compiler_params=params(),
        cost_estimate=cost(0),
        name="ffn_reduce",
    )(where, received)


UP, DOWN, PROJ, QKV, SMALL, WIDE = 0, 2048, 4096, 5120, 6656, 6784


def pack_kernel(where_ref, own_ref, *refs):
    ffn_refs, qkv_ref, out_ref = refs[:3], refs[3], refs[4]
    z = where_ref[1]
    for k in range(NZ):
        ring = jnp.bitwise_and(z + NZ - k, NZ - 1)
        block = own_ref[0:16, :] if k == 0 else ffn_refs[k - 1][...]
        for n in range(8):
            out_ref[n, :, pl.ds(pl.multiple_of(UP + ring * HID, HID), HID)] = block[:, :HID]
            out_ref[n, :, pl.ds(pl.multiple_of(DOWN + ring * HID, HID), HID)] = block[:, HID:]
    small = jnp.zeros((16, 128), F32)
    for ring in range(NZ):
        total = jnp.zeros((16, 4 * PAIR), F32)
        for h in range(NXH):
            for n in range(8):
                total = total + qkv_ref[(h * NZ + ring) * 8 + n].astype(F32)
        small = small + total[:, 3 * PAIR :]
        low = total.astype(BF)
        for n in range(8):
            for part in range(3):
                first = QKV + part * 512 + ring * PAIR
                out_ref[n, :, first : first + PAIR] = low[:, part * PAIR : (part + 1) * PAIR]
    for n in range(8):
        out_ref[n, :, PROJ:QKV] = own_ref[16:32, :]
        out_ref[n, :, SMALL:WIDE] = small.astype(BF)


def pack(where, own, others, qkv):
    return pl.pallas_call(
        pack_kernel,
        in_specs=[SM] + [VM] * 5,
        out_specs=VM,
        out_shape=shape((8, 16, WIDE), BF),
        compiler_params=params(),
        cost_estimate=cost(0),
        name="pack",
    )(where, own, *others, qkv)


def merge_kernel(where_ref, mine_ref, theirs_ref, up_ref, down_ref, proj_ref, qkv_ref, small_ref):
    core = where_ref[0]
    native = where_ref[0] == where_ref[3]
    for side, ref in ((core, mine_ref), (1 - core, theirs_ref)):
        up_ref[:, pl.ds(pl.multiple_of(side * 2048, 2048), 2048)] = ref[:, UP:DOWN]
        down_ref[:, pl.ds(pl.multiple_of(side * 2048, 2048), 2048)] = ref[:, DOWN:PROJ]
        for part in range(3):
            place = pl.multiple_of(part * D + side * 512, 512)
            qkv_ref[:, pl.ds(place, 512)] = ref[:, QKV + part * 512 : QKV + (part + 1) * 512]

    @pl.when(native)
    def _():
        proj_ref[...] = mine_ref[:, PROJ:QKV]

    @pl.when(jnp.logical_not(native))
    def _():
        proj_ref[...] = theirs_ref[:, PROJ:QKV]

    for n in range(8):
        small_ref[2 * n : 2 * n + 2, :] = mine_ref[n * 16 : (n + 1) * 16, SMALL:WIDE].astype(F32)[
            0:2
        ] + theirs_ref[n * 16 : (n + 1) * 16, SMALL:WIDE].astype(F32)[0:2]


def merge(where, mine, theirs):
    return pl.pallas_call(
        merge_kernel,
        in_specs=[SM, VM, VM],
        out_specs=[VM] * 5,
        out_shape=[
            shape((128, FF), BF),
            shape((128, FF), BF),
            shape((128, D), BF),
            shape((128, 3 * D), BF),
            shape((16, 128), F32),
        ],
        compiler_params=params(),
        cost_estimate=cost(0),
        name="merge",
    )(where, mine, theirs)


def back_kernel(dqkv_ref, w_ref, ffn_ref, norm_ref, out_ref):
    dn1 = dot(dqkv_ref[...], w_ref[...], 1, 1)
    out_ref[...] = (dn1 * norm_ref[0:1, :] + ffn_ref[...].astype(F32)).astype(BF)


def back_half(dqkv, w, ffn_back, norms, base):
    moving = lambda i: (base + i, 0)
    fixed = lambda i: (0, 0)
    return pl.pallas_call(
        back_kernel,
        grid=(2,),
        in_specs=[
            pl.BlockSpec((2 * ROWS, 3 * PAIR), moving),
            pl.BlockSpec((D, 3 * PAIR), fixed),
            pl.BlockSpec((2 * ROWS, D), moving),
            pl.BlockSpec((4, D), fixed),
        ],
        out_specs=pl.BlockSpec((2 * ROWS, D), lambda i: (i, 0)),
        out_shape=shape((SEQ // 2, D), BF),
        compiler_params=params(),
        cost_estimate=cost(0),
        name="back_half",
    )(dqkv, w, ffn_back, norms)


def qkv_grad_kernel(meta_ref, xh_ref, dqkv_ref, w_ref, norm_ref, dy_ref, ffn_vec_ref, grad_ref, vec):
    part = meta_ref[6]
    dqkv = dqkv_ref[...]
    sums = jnp.broadcast_to(jnp.sum(dqkv.astype(F32), axis=0, keepdims=True), (8, 3 * PAIR))
    dy_sum = jnp.sum(dy_ref[...].astype(F32), axis=0, keepdims=True)
    raw = dot(xh_ref[...], dqkv, 0, 0)
    gain = jnp.transpose(jnp.broadcast_to(norm_ref[0:1, :], (8, D)))[:, 0:1]
    shift = jnp.transpose(jnp.broadcast_to(norm_ref[1:2, :], (8, D)))[:, 0:1]
    grad_ref[:, 0 : 3 * PAIR] = (raw * gain + shift * sums[0:1, :]).astype(BF)
    product = (raw * w_ref[...].astype(F32)).astype(BF)
    norm_rows = [
        dot(jnp.ones((8, 3 * PAIR), BF), product, 1, 1)[0:1],
        dot(sums.astype(BF), w_ref[...], 1, 1)[0:1],
        ffn_vec_ref[0:1, :],
        ffn_vec_ref[8:9, :],
    ]
    vec[...] = jnp.zeros_like(vec)

    def put(bias_row, values):
        place = bias_row + (bias_row // 9) * 7
        vec[pl.ds(place, 1), :] = values

    for n in range(3):
        put(n * 8 + part, sums[0:1, n * PAIR : (n + 1) * PAIR])
    for n in range(4):
        put(32 + part * 4 + n, ffn_vec_ref[16:17, n * 128 : (n + 1) * 128])
    for n in range(8):
        put(24 + n, dy_sum[:, n * 128 : (n + 1) * 128])
        put(64 + n, dy_sum[:, n * 128 : (n + 1) * 128])
        for r in range(4):
            vec[n * 16 + 9 + r : n * 16 + 10 + r, :] = norm_rows[r][:, n * 128 : (n + 1) * 128]
    grad_ref[:, 3 * PAIR :] = jnp.concatenate(
        [
            part for n in range(64) for part in (vec[2 * n : 2 * n + 2, :], jnp.zeros((14, 128), F32))
        ],
        axis=0,
    ).astype(BF)


def qkv_grad(meta, xh, dqkv, w, norms, dy, ffn_vec):
    return pl.pallas_call(
        qkv_grad_kernel,
        in_specs=[SM] + [VM] * 6,
        out_specs=VM,
        out_shape=shape((D, 4 * PAIR), BF),
        scratch_shapes=[pltpu.VMEM((128, 128), F32)],
        compiler_params=params(),
        cost_estimate=cost(0),
        name="qkv_grad",
    )(meta, xh, dqkv, w, norms, dy, ffn_vec)


def body(
    tokens, out_grad, segments, w_qkv, w_proj, w_up, w_down, norm_params, biases,
    prior_moment_qkv, prior_square_qkv, prior_moment_proj, prior_square_proj,
    prior_moment_up, prior_square_up, prior_moment_down, prior_square_down,
    prior_moment_norm, prior_square_norm, prior_moment_bias, prior_square_bias,
):
    rep, shard = lax.axis_index("rep"), lax.axis_index("shard")
    core, y = rep % NC, rep // (NC * NXL)
    where = jnp.stack([core, shard % NZ, y, shard // NZ]).astype(jnp.int32)

    x_mine = spread([tokens] * NZ)
    docs = segments.astype(BF).reshape(2, 128)
    sent = send_weights(
        where, w_qkv, w_up, w_down, norm_params, biases.reshape(9, 128), docs, sibling(docs)
    )
    received = lax.all_to_all(sent, "shard", 0, 0, tiled=True)
    w_qkv_t, norms, bias, ffn_part, meta = assemble(where, received)
    cosine, sine = rotary_tables()
    x_joined = join(x_mine, 200)
    half = project_qkv(meta, x_joined, w_qkv_t, bias, norms, cosine, sine, None, 100)
    x_other = sibling(x_joined)
    n2, xh, q, k, v = project_qkv(meta, x_other, w_qkv_t, bias, norms, cosine, sine, half, 0)

    ffn_part = exchange(ffn_part, ALONG_Y)
    w_up_t, w_down_t = assemble_ffn(ffn_part)
    dy_first = jnp.concatenate([out_grad, w_proj.astype(BF)], axis=0)
    dy_first, dy_own, _ = lax.optimization_barrier((dy_first, out_grad, x_joined))
    dy_mine = spread([dy_first, dy_own, dy_own, dy_own])

    ctx, ctxt, stat = attn_forward(meta, q, k, v)
    ctx, dy_mine, w_up_t, w_down_t = lax.optimization_barrier((ctx, dy_mine, w_up_t, w_down_t))
    dy_joined = join(dy_mine, 0)
    dy_other = sibling(dy_joined)
    out_mine, out_theirs, ffn_back, dctx, ffn_vec, ffn_sent = feed_forward(
        meta, dy_joined, dy_other, n2, xh, ctx, w_up_t, w_down_t, dy_mine[0], bias, norms
    )
    out_other = sibling(out_theirs)

    prepared = attn_prepare(q, k, dctx, ctxt, stat)
    dqkv = attn_backward(meta, k, v, stat, cosine, sine, prepared)
    qkv_sent = qkv_grad(meta, xh, dqkv, w_qkv_t, norms, out_grad, ffn_vec)
    out_pieces = collect(core_sum(out_mine, out_other))
    dqkv, qkv_sent = lax.optimization_barrier((dqkv, qkv_sent))
    back_theirs = back_half(dqkv, w_qkv_t, ffn_back, norms, 2)
    dqkv, back_theirs, out_pieces = lax.optimization_barrier((dqkv, back_theirs, out_pieces))
    back_mine = back_half(dqkv, w_qkv_t, ffn_back, norms, 0)

    block_out = finish_out(tokens, bias, out_pieces)
    ffn_received, back_mine = lax.optimization_barrier((exchange(ffn_sent, PLANE), back_mine))
    ffn_own, *ffn_others = ffn_reduce(where, ffn_received)
    ffn_others = [lax.ppermute(b, AXES, ROUND_Z[k + 1]) for k, b in enumerate(ffn_others)]
    qkv_rows = exchange(qkv_sent.reshape(64, 16, 4 * PAIR), SAME_CORE)
    back_pieces = collect(core_sum(back_mine, sibling(back_theirs)))
    grad_tokens = finish_grad(tokens, out_grad, back_pieces)
    ffn_own, grad_tokens = lax.optimization_barrier((ffn_own, grad_tokens))
    packed = pack(where, ffn_own, ffn_others, qkv_rows)
    mine_grad = exchange(packed, COPIES).reshape(128, WIDE)
    g_up, g_down, g_proj, g_qkv, small = merge(where, mine_grad, sibling(mine_grad))
    g_norm = small[9:13]
    g_bias = small[:9].reshape(1152)

    def matrix_step(weight, moment, square, grad):
        return adam_step(weight, moment, square, grad.astype(F32), RATE_MATRIX, DECAY)

    new_qkv = matrix_step(w_qkv, prior_moment_qkv, prior_square_qkv, g_qkv)
    new_proj = matrix_step(w_proj, prior_moment_proj, prior_square_proj, g_proj)
    new_up = matrix_step(w_up, prior_moment_up, prior_square_up, g_up)
    new_down = matrix_step(w_down, prior_moment_down, prior_square_down, g_down)
    new_norm = adam_step(norm_params, prior_moment_norm, prior_square_norm, g_norm, RATE_VECTOR, 0.0)
    new_bias = adam_step(biases, prior_moment_bias, prior_square_bias, g_bias, RATE_VECTOR, 0.0)
    return (block_out, grad_tokens, *new_qkv, *new_proj, *new_up, *new_down, *new_norm, *new_bias)


def solution(mesh):
    token = P(("rep", "shard"), None)
    row = P("shard", None)
    norm = P(None, "shard")
    flat = P("shard")
    in_specs = (
        (token, token, P(("rep", "shard")))
        + (row,) * 4
        + (norm, flat)
        + (row,) * 8
        + (norm, norm, flat, flat)
    )
    out_specs = (token, token) + (row,) * 12 + (norm,) * 3 + (flat,) * 3
    return jax.shard_map(body, mesh=mesh, in_specs=in_specs, out_specs=out_specs, check_vma=False)
```

```python
import functools

import jax
import jax.numpy as jnp
import numpy as np
from jax import lax
from jax.experimental import pallas as pl
from jax.experimental.pallas import tpu as pltpu
from jax.sharding import PartitionSpec as P

HEAD_DIM = 64
ROT = 16
STEP = 10
EPS_NORM = 1e-05
BETA_ONE = 0.9
BETA_TWO = 0.95
RATE_MATRIX = 0.05
RATE_VECTOR = 0.3
DECAY = 0.01
ADAM_EPS = 1e-08
NEGATIVE = -1e30

NY, NXL, NC, NXH, NZ = 4, 2, 2, 2, 4
AXES = ("rep", "shard")
D = 1024
ROWS = 256
SEQ = 2048
FF = 4096
PAIR = 128
HID = 512
QB = 512
BF = jnp.bfloat16
F32 = jnp.float32


def device_pairs(move):
    pairs = []
    for y in range(NY):
        for xl in range(NXL):
            for c in range(NC):
                for h in range(NXH):
                    for z in range(NZ):
                        ty, txl, tc, th, tz = move(y, xl, c, h, z)
                        pairs.append(
                            (
                                ((y * NXL + xl) * NC + c) * 8 + h * NZ + z,
                                ((ty * NXL + txl) * NC + tc) * 8 + th * NZ + tz % NZ,
                            )
                        )
    return pairs


SWAP = device_pairs(lambda y, xl, c, h, z: (y, xl, h, c, z))


SIBLING = device_pairs(lambda y, xl, c, h, z: (y, xl, 1 - c, h, z))
ROUND_X = [
    device_pairs(
        lambda y, xl, c, h, z, k=k: (y, (h * 2 + xl + k) % 4 % 2, c, (h * 2 + xl + k) % 4 // 2, z)
    )
    for k in range(4)
]
ROUND_Z = [device_pairs(lambda y, xl, c, h, z, k=k: (y, xl, c, h, z + k)) for k in range(NZ)]


def device(y, xl, c, h, z):
    return ((y * NXL + xl) * NC + c) * 8 + h * NZ + z


RANGES = dict(y=range(NY), xl=range(NXL), c=range(NC), h=range(NXH), z=range(NZ))


def groups(*inner):
    outer = [name for name in RANGES if name not in inner]

    def walk(names, at):
        if not names:
            return [device(**at)]
        return [d for n in RANGES[names[0]] for d in walk(names[1:], dict(at, **{names[0]: n}))]

    def each(names, at):
        if not names:
            return [walk(inner, at)]
        return [g for n in RANGES[names[0]] for g in each(names[1:], dict(at, **{names[0]: n}))]

    return each(outer, {})


ALONG_Y = groups("y")
ALONG_Z = groups("z")
PLANE = groups("h", "y", "xl")
COPIES = groups("y", "xl")


SPREAD = [device_pairs(lambda y, xl, c, h, z, k=k: (y, xl, h, c, z + k)) for k in range(NZ)]


def permute(values, pairs):
    return lax.ppermute(values, AXES, pairs)


def around(block):
    return [block] + [permute(block, ROUND_Z[k]) for k in (1, 2, 3)]


def back_around(blocks):
    return [blocks[0]] + [permute(blocks[k], ROUND_Z[NZ - k]) for k in (1, 2, 3)]


def sibling(values):
    return lax.ppermute(values, AXES, SIBLING)


def exchange(values, members):
    return lax.all_to_all(values, AXES, 0, 0, axis_index_groups=members, tiled=True)


def dot(a, b, ca, cb):
    return lax.dot_general(a, b, (((ca,), (cb,)), ((), ())), preferred_element_type=F32)


def gelu_parts(values):
    cdf = 0.5 * (1.0 + lax.erf(values * np.float32(np.sqrt(0.5))))
    density = jnp.exp(-0.5 * values * values) * np.float32(1.0 / np.sqrt(2.0 * np.pi))
    return values * cdf, cdf + values * density


def adam_step(weight, moment, square, gradient, rate, decay):
    moment_new = BETA_ONE * moment + (1.0 - BETA_ONE) * gradient
    square_new = BETA_TWO * square + (1.0 - BETA_TWO) * gradient * gradient
    fixed_moment = moment_new / (1.0 - BETA_ONE**STEP)
    fixed_square = square_new / (1.0 - BETA_TWO**STEP)
    weight_new = weight - rate * (
        fixed_moment / (jnp.sqrt(fixed_square) + ADAM_EPS) + decay * weight
    )
    return (weight_new, moment_new, square_new)


SM = pl.BlockSpec(memory_space=pltpu.SMEM)
VM = pl.BlockSpec(memory_space=pltpu.VMEM)


def full(*dims):
    return pl.BlockSpec(dims, lambda i: (0,) * len(dims))


WHOLE = pl.BlockSpec((SEQ, PAIR), lambda i: (0, 0))


def params(mib=16):
    return pltpu.CompilerParams(vmem_limit_bytes=mib * 2**20)


def cost(us):
    flops = int(us * 7e8)
    return pl.CostEstimate(flops=flops, bytes_accessed=int(us * 2e6), transcendentals=0)


def shape(dims, kind):
    return jax.ShapeDtypeStruct(dims, kind)


def far(dims, kind):
    return pltpu.HBM(dims, kind)


def keep_far(values):
    return pltpu.with_memory_space_constraint(values, pltpu.HBM)


def send_weights_kernel(
    where_ref, q_ref, k_ref, v_ref, up_ref, down_ref, norm_ref, bias_ref, seg_ref, sib_ref, out_ref
):
    misc = jnp.concatenate(
        [norm_ref[...], bias_ref[...], seg_ref[...].astype(F32), jnp.zeros((1, 128), F32)], axis=0
    ).astype(BF)
    theirs = jnp.concatenate([sib_ref[...].astype(F32), jnp.zeros((14, 128), F32)], axis=0).astype(BF)
    for n in range(8):
        for part, ref in enumerate((q_ref, k_ref, v_ref)):
            source = slice((n % NZ) * PAIR, (n % NZ + 1) * PAIR)
            out_ref[n, 0:128, part * PAIR : (part + 1) * PAIR] = ref[:, source].astype(BF)
        out_ref[n, 128:144, 0:128] = misc
        out_ref[n, 128:144, 128:256] = theirs
        out_ref[n, 128:144, 256:384] = jnp.zeros((16, 128), BF)
        for j in range(8):
            ref = (up_ref, down_ref)[j // 4]
            source = (n % NZ) * HID + (j % 4) * 128
            first = 144 + (j // 3) * 32
            out_ref[n, first : first + 32, (j % 3) * 128 : (j % 3 + 1) * 128] = ref[
                :, source : source + 128
            ].astype(BF)
        out_ref[n, 208:240, 256:384] = jnp.zeros((32, 128), BF)


def send_weights(where, w, up, down, norms, biases, segments, sibling_segments):
    third = lambda part: pl.BlockSpec((128, 512), lambda i, where: (0, part * 2 + where[0]))
    rows = pl.BlockSpec((32, 2048), lambda i, where: (where[2], where[0]))
    small = lambda count: pl.BlockSpec((count, 128), lambda i, where: (0, 0))
    return pl.pallas_call(
        send_weights_kernel,
        grid_spec=pltpu.PrefetchScalarGridSpec(
            num_scalar_prefetch=1,
            grid=(1,),
            in_specs=[third(0), third(1), third(2), rows, rows] + [small(4), small(9), small(2), small(2)],
            out_specs=pl.BlockSpec((8, 240, 384), lambda i, where: (0, 0, 0)),
        ),
        out_shape=far((8, 240, 384), BF),
        compiler_params=params(),
        cost_estimate=cost(0),
        name="send_weights",
    )(
        where, *[keep_far(w)] * 3, keep_far(up), keep_far(down),
        keep_far(norms), biases, segments, sibling_segments,
    )


def join_kernel(*refs):
    for k in range(NZ):
        refs[NZ][k * ROWS : (k + 1) * ROWS, :] = refs[k][...]


def join(blocks):
    return pl.pallas_call(
        join_kernel,
        in_specs=[VM] * NZ,
        out_specs=VM,
        out_shape=shape((SEQ // 2, D), BF),
        compiler_params=params(),
        cost_estimate=cost(0),
        name="join",
    )(*blocks)


def doc_start(ids, meta_ref):
    start = jnp.zeros_like(ids)
    for d in range(4):
        start = jnp.where(ids >= meta_ref[d], meta_ref[d], start)
    return start


def block_tables(where_ref, meta_ref):
    c, z = where_ref[0], where_ref[1]
    meta_ref[4] = c
    meta_ref[5] = z
    meta_ref[6] = c * NZ + z
    meta_ref[7] = where_ref[2]
    for j in range(2):
        half = c if j == 0 else 1 - c
        for k in range(NZ):
            meta_ref[8 + j * NZ + k] = half * NZ + jnp.bitwise_and(z + NZ - k, NZ - 1)
    for half in range(2):
        base = jnp.bitwise_xor(c, half) * NZ
        for ring in range(NZ):
            meta_ref[16 + half * NZ + ring] = base + jnp.bitwise_and(z + NZ - ring, NZ - 1)


def assemble_kernel(
    where_ref, in_ref, w_ref, norm_ref, bias_ref, ffn_ref, meta_ref
):
    block_tables(where_ref, meta_ref)
    counts = [jnp.zeros((1, 128), F32) for _ in range(4)]
    native = (where_ref[0] == where_ref[3]).astype(F32)
    for n in range(8):
        w_ref[n * 128 : (n + 1) * 128, :] = in_ref[n, 0:128, :]
        misc = in_ref[n, 128:144, 0:128].astype(F32)
        other = in_ref[n, 128:144, 128:256].astype(F32)
        norm_ref[:, n * 128 : (n + 1) * 128] = misc[0:4]
        bias_ref[n * 9 : (n + 1) * 9, :] = misc[4:13]
        docs = misc[13:15] * native + other[0:2] * (1.0 - native)
        for d in range(4):
            below = jnp.where(docs < d + 0.5, 1.0, 0.0)
            counts[d] = counts[d] + below[0:1] + below[1:2]
        for j in range(8):
            first = 144 + (j // 3) * 32
            block = in_ref[n, first : first + 32, (j % 3) * 128 : (j % 3 + 1) * 128]
            for y in range(NY):
                ffn_ref[y, n * 32 : (n + 1) * 32, j * 128 : (j + 1) * 128] = block
    for d in range(4):
        meta_ref[d] = jnp.sum(counts[d]).astype(jnp.int32)


def rotary_tables():
    lane = np.arange(PAIR) % HEAD_DIM
    freq = 10000.0 ** (-2.0 * (lane % (ROT // 2)) / ROT)
    angles = np.arange(SEQ)[:, None] * np.where(lane < ROT, freq, 0.0)[None, :]
    return jnp.asarray(np.where(np.arange(PAIR) < HEAD_DIM, np.cos(angles), np.sin(angles)), F32)


def both_heads(table):
    first = lax.broadcasted_iota(jnp.int32, table.shape, 1) < HEAD_DIM
    other = pltpu.roll(table, HEAD_DIM, 1)
    return jnp.where(first, table, other), jnp.where(first, other, table)


def assemble(where, received):
    return pl.pallas_call(
        assemble_kernel,
        grid=(1,),
        in_specs=[SM, VM],
        out_specs=[VM] * 3 + [pl.BlockSpec((NY, ROWS, 2 * HID), lambda i: (0, 0, 0)), SM],
        out_shape=[
            shape((D, 3 * PAIR), BF),
            shape((4, D), F32),
            shape((72, 128), F32),
            far((NY, ROWS, 2 * HID), BF),
            shape((24,), jnp.int32),
        ],
        compiler_params=params(),
        cost_estimate=cost(0),
        name="assemble",
    )(where, received)


def assemble_ffn_kernel(in_ref, up_ref, down_ref):
    for y in range(NY):
        for n in range(8):
            rows = slice(n * 128 + y * 32, n * 128 + (y + 1) * 32)
            up_ref[rows, :] = in_ref[y, n * 32 : (n + 1) * 32, 0:HID]
            down_ref[rows, :] = in_ref[y, n * 32 : (n + 1) * 32, HID:]


def assemble_ffn(parts):
    return pl.pallas_call(
        assemble_ffn_kernel,
        in_specs=[VM],
        out_specs=[VM] * 2,
        out_shape=[shape((D, HID), BF)] * 2,
        compiler_params=params(),
        cost_estimate=cost(0),
        name="assemble_ffn",
    )(parts)


def turn(u, cosine, sine):
    lane = lax.broadcasted_iota(jnp.int32, u.shape, 1) % HEAD_DIM
    left = pltpu.roll(u, PAIR - ROT // 2, 1)
    right = pltpu.roll(u, ROT // 2, 1)
    return u * cosine + jnp.where(lane < ROT // 2, -left, right) * sine


def qkv_kernel(meta_ref, x_ref, w_ref, bias_ref, norm_ref, turn_ref, *refs):
    n2_ref, xh_ref, q_ref, k_ref, v_ref = refs[-5:]
    x = x_ref[...].astype(F32)
    centred = x - jnp.mean(x, axis=-1, keepdims=True)
    variance = jnp.mean(centred * centred, axis=-1, keepdims=True)
    xh = centred * lax.rsqrt(variance + EPS_NORM)
    n1 = (xh * norm_ref[0:1, :] + norm_ref[1:2, :]).astype(BF)
    xh_ref[...] = xh.astype(BF)
    n2_ref[...] = (xh * norm_ref[2:3, :] + norm_ref[3:4, :]).astype(BF)
    part = meta_ref[6]
    cosine, sine = both_heads(turn_ref[...])
    qkv = dot(n1, w_ref[...], 1, 0)
    q = qkv[:, 0:PAIR] + bias_ref[pl.ds(part, 1), :]
    k = qkv[:, PAIR : 2 * PAIR] + bias_ref[pl.ds(8 + part, 1), :]
    v = qkv[:, 2 * PAIR :] + bias_ref[pl.ds(16 + part, 1), :]
    q_ref[...] = (turn(q, cosine, sine).astype(BF) * 0.125).astype(BF)
    k_ref[...] = turn(k, cosine, sine).astype(BF)
    v_ref[...] = v.astype(BF)


def project_qkv(meta, x, w, bias, norms, turns, before, us):
    base = 0 if before is None else NZ
    moving = lambda i, meta: (i, 0)
    physical = lambda i, meta: (base + i, 0)
    logical = lambda i, meta: (meta[8 + base + i], 0)
    fixed = lambda i, meta: (0, 0)
    extra = [] if before is None else list(before)
    return pl.pallas_call(
        qkv_kernel,
        grid_spec=pltpu.PrefetchScalarGridSpec(
            num_scalar_prefetch=1,
            grid=(NZ,),
            in_specs=[
                pl.BlockSpec((ROWS, D), moving),
                pl.BlockSpec((D, 3 * PAIR), fixed),
                pl.BlockSpec((72, 128), fixed),
                pl.BlockSpec((4, D), fixed),
                pl.BlockSpec((ROWS, PAIR), logical),
            ]
            + [pl.BlockSpec(memory_space=pl.ANY)] * len(extra),
            out_specs=[pl.BlockSpec((ROWS, D), physical)] * 2
            + [pl.BlockSpec((ROWS, PAIR), logical)] * 3,
        ),
        out_shape=[far((SEQ, D), BF)] * 2 + [far((SEQ, PAIR), BF)] * 3,
        input_output_aliases={6 + n: n for n in range(len(extra))},
        compiler_params=params(),
        cost_estimate=cost(us),
        name="project_qkv",
    )(meta, x, w, bias, norms, keep_far(turns), *extra)


def head_only(values, h):
    lane = lax.broadcasted_iota(jnp.int32, values.shape, 1)
    return jnp.where((lane // HEAD_DIM) == h, values, jnp.zeros_like(values))


def tile_mask(meta_ref, i, j):
    keys = j * QB + lax.broadcasted_iota(jnp.int32, (QB, QB), 0)
    query_row = i * QB + lax.broadcasted_iota(jnp.int32, (1, QB), 1)
    start = doc_start(query_row, meta_ref)
    return (keys <= query_row) & (keys >= start)


def attn_forward_kernel(meta_ref, q_ref, k_ref, v_ref, ctx_ref, ctxt_ref, stat_ref, vt_ref):
    i = pl.program_id(0)

    @pl.when(i == 0)
    def _():
        for b in range(SEQ // QB):
            vt_ref[:, b * QB : (b + 1) * QB] = v_ref[b * QB : (b + 1) * QB, :].T

    q = q_ref[pl.ds(pl.multiple_of(i * QB, QB), QB), :]
    heads = [head_only(q, h) for h in range(2)]

    def step(j, carry):
        mask = tile_mask(meta_ref, i, j)
        row = pl.multiple_of(j * QB, QB)
        keys = k_ref[pl.ds(row, QB), :]
        out = []
        for h in range(2):
            m, l, acc = carry[h]
            scores = dot(keys, heads[h], 1, 1)
            scores = jnp.where(mask, scores, NEGATIVE)
            top = jnp.maximum(m, jnp.max(scores, axis=0, keepdims=True))
            expo = jnp.exp(scores - top)
            fade = jnp.exp(m - top)
            l = l * fade + jnp.sum(expo, axis=0, keepdims=True)
            values = vt_ref[h * HEAD_DIM : (h + 1) * HEAD_DIM, pl.ds(row, QB)]
            acc = acc * fade + dot(values, expo.astype(BF), 1, 0)
            out.append((top, l, acc))
        return tuple(out)

    zero = (
        jnp.full((1, QB), NEGATIVE, F32),
        jnp.zeros((1, QB), F32),
        jnp.zeros((HEAD_DIM, QB), F32),
    )
    result = lax.fori_loop(0, i + 1, step, (zero, zero))
    column = pl.multiple_of(i * QB, QB)
    parts = []
    for h in range(2):
        m, l, acc = result[h]
        parts.append(acc / l)
        stat_ref[h : h + 1, pl.ds(column, QB)] = m
        stat_ref[2 + h : 3 + h, pl.ds(column, QB)] = 1.0 / l
    ctxt = jnp.concatenate(parts, axis=0)
    ctxt_ref[:, pl.ds(column, QB)] = ctxt
    low = ctxt.astype(BF).T
    for b in range(QB // ROWS):
        row = pl.multiple_of(meta_ref[16 + i * (QB // ROWS) + b] * ROWS, ROWS)
        ctx_ref[pl.ds(row, ROWS), :] = low[b * ROWS : (b + 1) * ROWS]


def attn_forward(meta, q, k, v):
    return pl.pallas_call(
        attn_forward_kernel,
        grid=(SEQ // QB,),
        in_specs=[SM, WHOLE, WHOLE, WHOLE],
        out_specs=[WHOLE, pl.BlockSpec((PAIR, SEQ), lambda i: (0, 0)), VM],
        out_shape=[far((SEQ, PAIR), BF), far((PAIR, SEQ), F32), shape((8, SEQ), F32)],
        scratch_shapes=[pltpu.VMEM((PAIR, SEQ), BF)],
        compiler_params=params(),
        cost_estimate=cost(0),
        name="attn_forward",
    )(meta, keep_far(q), keep_far(k), keep_far(v))


def attn_prepare_kernel(
    q_ref, k_ref, dctx_ref, ctxt_ref, stat_ref, kt_ref, du_ref, dut_ref, qh_ref, c_ref
):
    kt_ref[...] = k_ref[...].T
    dctxt = dctx_ref[...].T
    prod = dctxt * ctxt_ref[...]
    c_ref[...] = jnp.zeros_like(c_ref)
    for h in range(2):
        rows = slice(h * HEAD_DIM, (h + 1) * HEAD_DIM)
        inverse = stat_ref[2 + h : 3 + h, :]
        c_ref[h : h + 1, :] = jnp.sum(prod[rows], axis=0, keepdims=True) * inverse
        dut = (dctxt[rows] * inverse).astype(BF)
        dut_ref[h, rows, :] = dut
        dut_ref[h, (1 - h) * HEAD_DIM : (2 - h) * HEAD_DIM, :] = jnp.zeros_like(dut)
        du_ref[h] = dut_ref[h].T
        qh_ref[h] = head_only(q_ref[...], h)


def attn_prepare(q, k, dctx, ctxt, stat):
    down = pl.BlockSpec((QB, PAIR), lambda i: (i, 0))
    across = lambda rows: pl.BlockSpec((rows, QB), lambda i: (0, i))
    down_heads = pl.BlockSpec((2, QB, PAIR), lambda i: (0, i, 0))
    across_heads = pl.BlockSpec((2, PAIR, QB), lambda i: (0, 0, i))
    return pl.pallas_call(
        attn_prepare_kernel,
        grid=(SEQ // QB,),
        in_specs=[down, down, down, across(PAIR), across(8)],
        out_specs=[across(PAIR), down_heads, across_heads, down_heads, across(8)],
        out_shape=[
            shape((PAIR, SEQ), BF),
            shape((2, SEQ, PAIR), BF),
            shape((2, PAIR, SEQ), BF),
            shape((2, SEQ, PAIR), BF),
            shape((8, SEQ), F32),
        ],
        compiler_params=params(),
        cost_estimate=cost(60),
        name="attn_prepare",
    )(keep_far(q), keep_far(k), keep_far(dctx), keep_far(ctxt), stat)


def attn_backward_kernel(
    meta_ref, k_ref, v_ref, stat_ref, turn_ref, kt_ref, du_ref, dut_ref, qh_ref, c_ref,
    out_ref,
    dqt_ref, dk_ref, dv_ref,
):
    j = pl.program_id(0)
    blocks = SEQ // QB

    @pl.when(j == 0)
    def _():
        dqt_ref[...] = jnp.zeros_like(dqt_ref)

    row = pl.multiple_of(j * QB, QB)
    keys = k_ref[pl.ds(row, QB), :]
    values = v_ref[pl.ds(row, QB), :]

    def step(i, carry):
        dk, dv = carry
        mask = tile_mask(meta_ref, i, j)
        col = pl.multiple_of(i * QB, QB)
        for h in range(2):
            qh = qh_ref[h, pl.ds(col, QB), :]
            scores = dot(keys, qh, 1, 1)
            m = stat_ref[h : h + 1, pl.ds(col, QB)]
            expo = jnp.where(mask, jnp.exp(scores - m), 0.0)
            dexpo = dot(values, dut_ref[h, :, pl.ds(col, QB)], 1, 0)
            dscore = (expo * (dexpo - c_ref[h : h + 1, pl.ds(col, QB)])).astype(BF)
            dv = dv + dot(expo.astype(BF), du_ref[h, pl.ds(col, QB), :], 1, 0)
            dk = dk + dot(dscore, qh, 1, 0)
            rows = slice(h * HEAD_DIM, (h + 1) * HEAD_DIM)
            dqt_ref[rows, pl.ds(col, QB)] += dot(kt_ref[rows, pl.ds(row, QB)], dscore, 1, 0)
        return dk, dv

    zero = jnp.zeros((QB, PAIR), F32)
    dk, dv = lax.fori_loop(j, blocks, step, (zero, zero))
    dk_ref[pl.ds(row, QB), :] = dk
    dv_ref[pl.ds(row, QB), :] = dv

    @pl.when(j == blocks - 1)
    def _():
        for b in range(SEQ // ROWS):
            rows = slice(b * ROWS, (b + 1) * ROWS)
            place = pl.ds(pl.multiple_of(meta_ref[16 + b] * ROWS, ROWS), ROWS)
            cosine, sine = both_heads(turn_ref[rows, :])
            sine = -sine
            dq = (dqt_ref[:, rows] * 0.125).T
            out_ref[place, 0:PAIR] = turn(dq, cosine, sine).astype(BF)
            out_ref[place, PAIR : 2 * PAIR] = turn(dk_ref[rows, :], cosine, sine).astype(BF)
            out_ref[place, 2 * PAIR :] = dv_ref[rows, :].astype(BF)


def attn_backward(meta, k, v, stat, turns, prepared):
    return pl.pallas_call(
        attn_backward_kernel,
        grid=(SEQ // QB,),
        in_specs=[SM, WHOLE, WHOLE, VM, WHOLE] + [VM] * 5,
        out_specs=VM,
        out_shape=shape((SEQ, 3 * PAIR), BF),
        scratch_shapes=[
            pltpu.VMEM((PAIR, SEQ), F32),
            pltpu.VMEM((SEQ, PAIR), F32),
            pltpu.VMEM((SEQ, PAIR), F32),
        ],
        compiler_params=params(),
        cost_estimate=cost(100),
        name="attn_backward",
    )(meta, keep_far(k), keep_far(v), stat, keep_far(turns), *prepared)


def lay_rows(ref, first, count):
    return jnp.concatenate([ref[pl.ds(first + r, 1), :] for r in range(count)], axis=1)


def by_half(double):
    return [
        pl.BlockSpec((double, D), lambda i, meta: (jnp.minimum(i, 1), 0)),
        pl.BlockSpec((double, D), lambda i, meta: (jnp.maximum(i - 2, 0), 0)),
    ]


def take_half(step, mine_ref, theirs_ref, now_ref):
    @pl.when(step < 2)
    def _():
        now_ref[...] = mine_ref[...]

    @pl.when(step >= 2)
    def _():
        now_ref[...] = theirs_ref[...]


def ffn_kernel(meta_ref, *refs):
    mine_ref, theirs_ref = refs[:2]
    n2_ref, xh_ref, ctx_ref, up_ref, down_ref, proj_ref, bias_ref, norm_ref = refs[2:10]
    out_mine_ref, out_theirs_ref, back_ref, dctx_ref, vec_ref, grad_ref = refs[10:16]
    dy_now, gup, gdown, gproj, total = refs[16:]
    step = pl.program_id(0)
    part = meta_ref[6]

    @pl.when(step == 0)
    def _():
        gup[...] = jnp.zeros_like(gup)
        gdown[...] = jnp.zeros_like(gdown)
        gproj[...] = jnp.zeros_like(gproj)
        total[...] = jnp.zeros_like(total)

    take_half(step, mine_ref, theirs_ref, dy_now)
    dy = dy_now[...]
    ctx = ctx_ref[...]
    dctx = dot(dy, proj_ref[...], 1, 1)
    for b in range(2):
        row = pl.multiple_of(meta_ref[8 + 2 * step + b] * ROWS, ROWS)
        dctx_ref[pl.ds(row, ROWS), :] = dctx[b * ROWS : (b + 1) * ROWS]
    gproj[...] += dot(ctx, dy, 0, 0)
    bias_up = lay_rows(bias_ref, 32 + 4 * part, 4)
    pre = dot(n2_ref[...], up_ref[...], 1, 0) + bias_up
    hidden, slope = gelu_parts(pre)
    hidden = hidden.astype(BF)
    dpre = (dot(dy, down_ref[...], 1, 0) * slope).astype(BF)
    out = (dot(ctx, proj_ref[...], 1, 0) + dot(hidden, down_ref[...], 1, 1)).astype(BF)

    @pl.when(step < 2)
    def _():
        out_mine_ref[...] = out

    @pl.when(step >= 2)
    def _():
        out_theirs_ref[...] = out

    back_ref[...] = (dot(dpre, up_ref[...], 1, 1) * norm_ref[2:3, :]).astype(BF)
    gdown[...] += dot(dy, hidden, 0, 0)
    gup[...] += dot(xh_ref[...], dpre, 0, 0)
    total[...] += jnp.broadcast_to(jnp.sum(dpre.astype(F32), axis=0, keepdims=True), total.shape)

    @pl.when(step == 3)
    def _():
        sums = total[...]
        raw = gup[...]
        gain = jnp.transpose(jnp.broadcast_to(norm_ref[2:3, :], (8, D)))[:, 0:1]
        shift = jnp.transpose(jnp.broadcast_to(norm_ref[3:4, :], (8, D)))[:, 0:1]
        product = (raw * up_ref[...].astype(F32)).astype(BF)
        gup[...] = raw * gain + shift * sums[0:1, :]
        for y in range(NY):
            for n in range(8):
                here = slice(n * 32, (n + 1) * 32)
                rows = slice(n * 128 + y * 32, n * 128 + (y + 1) * 32)
                grad_ref[y, here, 0:HID] = gup[rows, :].astype(BF)
                grad_ref[y, here, HID:] = gdown[rows, :].astype(BF)
            grad_ref[y, 256:288, :] = gproj[y * 32 : (y + 1) * 32, :].astype(BF)
        vec_ref[0:8, :] = dot(jnp.ones((8, HID), BF), product, 1, 1)
        vec_ref[8:16, :] = dot(sums.astype(BF), up_ref[...], 1, 1)
        vec_ref[16:24, 0:HID] = sums
        vec_ref[16:24, HID:] = jnp.zeros((8, D - HID), F32)


def feed_forward(meta, mine, theirs, n2, xh, ctx, up, down, proj, bias, norms):
    double = 2 * ROWS
    moving = lambda i, meta: (i, 0)
    fixed = lambda i, meta: (0, 0)
    once = pl.Buffered(1)
    return pl.pallas_call(
        ffn_kernel,
        grid_spec=pltpu.PrefetchScalarGridSpec(
            num_scalar_prefetch=1,
            grid=(4,),
            in_specs=by_half(double)
            + [
                pl.BlockSpec((double, D), moving),
                pl.BlockSpec((double, D), moving),
                pl.BlockSpec((double, PAIR), moving),
                pl.BlockSpec((D, HID), fixed, pipeline_mode=once),
                pl.BlockSpec((D, HID), fixed, pipeline_mode=once),
                pl.BlockSpec((PAIR, D), lambda i, meta: (2, 0), pipeline_mode=once),
                pl.BlockSpec((72, 128), fixed, pipeline_mode=once),
                pl.BlockSpec((4, D), fixed, pipeline_mode=once),
            ],
            out_specs=by_half(double)
            + [
                pl.BlockSpec((double, D), moving),
                pl.BlockSpec((SEQ, PAIR), fixed),
                VM,
                pl.BlockSpec((NY, 288, D), lambda i, meta: (0, 0, 0)),
            ],
            scratch_shapes=[
                pltpu.VMEM((double, D), BF),
                pltpu.VMEM((D, HID), F32),
                pltpu.VMEM((D, HID), F32),
                pltpu.VMEM((PAIR, D), F32),
                pltpu.VMEM((8, HID), F32),
            ],
        ),
        out_shape=[
            far((SEQ // 2, D), BF),
            far((SEQ // 2, D), BF),
            far((SEQ, D), BF),
            far((SEQ, PAIR), F32),
            shape((24, D), F32),
            far((NY, 288, D), BF),
        ],
        compiler_params=params(40),
        cost_estimate=cost(60),
        name="feed_forward",
    )(meta, mine, theirs, keep_far(n2), keep_far(xh), keep_far(ctx), up, down, proj, bias, norms)


def core_sum_kernel(mine_ref, theirs_ref, *sent_refs):
    step = pl.program_id(0)
    total = (mine_ref[...].astype(F32) + theirs_ref[...].astype(F32)).astype(BF)
    for k in range(NZ):

        @pl.when(step == k)
        def _():
            sent_refs[k][...] = total


def core_sum(mine, theirs):
    moving = lambda i: (i, 0)
    return pl.pallas_call(
        core_sum_kernel,
        grid=(NZ,),
        in_specs=[pl.BlockSpec((ROWS, D), moving)] * 2,
        out_specs=[pl.BlockSpec((ROWS, D), lambda i: (0, 0))] * NZ,
        out_shape=[shape((ROWS, D), BF)] * NZ,
        compiler_params=params(),
        cost_estimate=cost(0),
        name="core_sum",
    )(mine, theirs)


def fold_kernel(*refs):
    total = refs[0][...].astype(F32)
    for k in range(1, NZ):
        total = total + refs[k][...].astype(F32)
    refs[NZ][...] = total.astype(BF)


def fold(pieces):
    return pl.pallas_call(
        fold_kernel,
        in_specs=[VM] * NZ,
        out_specs=VM,
        out_shape=shape((ROWS, D), BF),
        compiler_params=params(),
        cost_estimate=cost(0),
        name="fold",
    )(*pieces)


def finish_out_kernel(x_ref, bias_ref, sum_ref, out_ref):
    bias = lay_rows(bias_ref, 24, 8) + lay_rows(bias_ref, 64, 8)
    out_ref[...] = (x_ref[...].astype(F32) + sum_ref[...].astype(F32) + bias).astype(BF)


def finish_out(x, bias, total):
    half = pl.BlockSpec((ROWS // 2, D), lambda i: (i, 0))
    return pl.pallas_call(
        finish_out_kernel,
        grid=(2,),
        in_specs=[half, pl.BlockSpec((72, 128), lambda i: (0, 0)), half],
        out_specs=half,
        out_shape=shape((ROWS, D), BF),
        compiler_params=params(),
        cost_estimate=cost(0),
        name="finish_out",
    )(keep_far(x), bias, total)


def finish_grad_kernel(x_ref, dy_ref, sum_ref, out_ref):
    w = sum_ref[...].astype(F32)
    x = x_ref[...].astype(F32)
    centred = x - jnp.mean(x, axis=-1, keepdims=True)
    rstd = lax.rsqrt(jnp.mean(centred * centred, axis=-1, keepdims=True) + EPS_NORM)
    xh = centred * rstd
    inner = w - jnp.mean(w, axis=-1, keepdims=True) - xh * jnp.mean(w * xh, axis=-1, keepdims=True)
    out_ref[...] = dy_ref[...].astype(F32) + rstd * inner


def finish_grad(x, dy, total):
    half = pl.BlockSpec((ROWS // 2, D), lambda i: (i, 0))
    return pl.pallas_call(
        finish_grad_kernel,
        grid=(2,),
        in_specs=[half] * 3,
        out_specs=half,
        out_shape=shape((ROWS, D), F32),
        compiler_params=params(),
        cost_estimate=cost(0),
        name="finish_grad",
    )(keep_far(x), keep_far(dy), total)


def reduce_y_kernel(where_ref, ffn_ref, *refs):
    low_ref = refs[4]
    total = ffn_ref[0].astype(F32)
    for n in range(1, NY):
        total = total + ffn_ref[n].astype(F32)
    low_ref[...] = total.astype(BF)
    x = where_ref[3] * NXL + where_ref[4]
    for k in range(4):
        target = jnp.bitwise_and(x + k, 3)
        half, low_x = target // 2, jnp.bitwise_and(target, 1)
        for ring in range(NZ):
            rows = pl.ds(pl.multiple_of((half * NZ + ring) * 32 + low_x * 16, 16), 16)
            refs[k][ring * 16 : (ring + 1) * 16, :] = low_ref[rows, :]
        refs[k][64:80, :] = low_ref[pl.ds(pl.multiple_of(256 + low_x * 16, 16), 16), :]


def reduce_y(where, ffn):
    return pl.pallas_call(
        reduce_y_kernel,
        grid=(1,),
        in_specs=[SM, full(NY, 288, D)],
        out_specs=[VM] * 4,
        out_shape=[shape((80, D), BF)] * 4,
        scratch_shapes=[pltpu.VMEM((288, D), BF)],
        compiler_params=params(),
        cost_estimate=cost(0),
        name="reduce_y",
    )(where, keep_far(ffn))


def reduce_x_kernel(where_ref, *refs):
    ffn_refs, qkv_ref, own_ref, sent_refs = refs[:4], refs[4], refs[5], refs[6:9]
    low_ref, low_qkv_ref = refs[9:]
    z = where_ref[1]
    total, total_qkv = ffn_refs[0][...].astype(F32), qkv_ref[0].astype(F32)
    for n in range(1, 4):
        total = total + ffn_refs[n][...].astype(F32)
    for n in range(1, 16):
        total_qkv = total_qkv + qkv_ref[n].astype(F32)
    low_ref[...] = total.astype(BF)
    low_qkv_ref[...] = total_qkv.astype(BF)
    for k in range(NZ):
        out_ref = own_ref if k == 0 else sent_refs[k - 1]
        rows = pl.ds(pl.multiple_of(jnp.bitwise_and(z + k, NZ - 1) * 16, 16), 16)
        out_ref[0:16, :] = low_ref[rows, :]
        out_ref[16:32, 0:512] = low_qkv_ref[rows, :]
        out_ref[16:32, 512:] = jnp.zeros((16, 512), BF)
    own_ref[32:48, :] = low_ref[64:80, :]


def reduce_x(where, ffn, qkv):
    return pl.pallas_call(
        reduce_x_kernel,
        grid=(1,),
        in_specs=[SM] + [VM] * 4 + [full(16, 64, 4 * PAIR)],
        out_specs=[VM] * 4,
        out_shape=[shape((48, D), BF)] + [shape((32, D), BF)] * 3,
        scratch_shapes=[pltpu.VMEM((80, D), BF), pltpu.VMEM((64, 4 * PAIR), BF)],
        compiler_params=params(),
        cost_estimate=cost(0),
        name="reduce_x",
    )(where, *ffn, keep_far(qkv))


UP, DOWN, PROJ, QKV, SMALL, WIDE = 0, 2048, 4096, 5120, 6656, 6784


def pack_kernel(where_ref, *refs):
    out_ref = refs[NZ]
    z = where_ref[1]
    small = jnp.zeros((16, 128), F32)
    for k in range(NZ):
        ring = jnp.bitwise_and(z + NZ - k, NZ - 1)
        ffn, qkv = refs[k][0:16, :], refs[k][16:32, :]
        small = small + qkv[:, 3 * PAIR : 4 * PAIR].astype(F32)
        for n in range(8):
            out_ref[n, :, pl.ds(pl.multiple_of(UP + ring * HID, HID), HID)] = ffn[:, :HID]
            out_ref[n, :, pl.ds(pl.multiple_of(DOWN + ring * HID, HID), HID)] = ffn[:, HID:]
            for part in range(3):
                place = pl.ds(pl.multiple_of(QKV + part * 512 + ring * PAIR, PAIR), PAIR)
                out_ref[n, :, place] = qkv[:, part * PAIR : (part + 1) * PAIR]
    for n in range(8):
        out_ref[n, :, PROJ:QKV] = refs[0][32:48, :]
        out_ref[n, :, SMALL:WIDE] = small.astype(BF)


def pack(where, own, others):
    return pl.pallas_call(
        pack_kernel,
        grid=(1,),
        in_specs=[SM] + [VM] * 4,
        out_specs=full(8, 16, WIDE),
        out_shape=far((8, 16, WIDE), BF),
        compiler_params=params(),
        cost_estimate=cost(0),
        name="pack",
    )(where, own, *others)


def merge_kernel(where_ref, mine_ref, theirs_ref, up_ref, down_ref, proj_ref, qkv_ref, small_ref):
    core = where_ref[0]
    native = where_ref[0] == where_ref[3]
    for side, ref in ((core, mine_ref), (1 - core, theirs_ref)):
        up_ref[:, pl.ds(pl.multiple_of(side * 2048, 2048), 2048)] = ref[:, UP:DOWN]
        down_ref[:, pl.ds(pl.multiple_of(side * 2048, 2048), 2048)] = ref[:, DOWN:PROJ]
        for part in range(3):
            place = pl.multiple_of(part * D + side * 512, 512)
            qkv_ref[:, pl.ds(place, 512)] = ref[:, QKV + part * 512 : QKV + (part + 1) * 512]

    @pl.when(native)
    def _():
        proj_ref[...] = mine_ref[:, PROJ:QKV]

    @pl.when(jnp.logical_not(native))
    def _():
        proj_ref[...] = theirs_ref[:, PROJ:QKV]

    for n in range(8):
        small_ref[2 * n : 2 * n + 2, :] = mine_ref[n * 16 : (n + 1) * 16, SMALL:WIDE].astype(F32)[
            0:2
        ] + theirs_ref[n * 16 : (n + 1) * 16, SMALL:WIDE].astype(F32)[0:2]


def merge(where, mine, theirs):
    return pl.pallas_call(
        merge_kernel,
        in_specs=[SM, VM, VM],
        out_specs=[VM] * 5,
        out_shape=[
            shape((128, FF), BF),
            shape((128, FF), BF),
            shape((128, D), BF),
            shape((128, 3 * D), BF),
            shape((16, 128), F32),
        ],
        compiler_params=params(),
        cost_estimate=cost(0),
        name="merge",
    )(where, mine, theirs)


def back_kernel(dqkv_ref, w_ref, ffn_ref, norm_ref, out_ref):
    dn1 = dot(dqkv_ref[...], w_ref[...], 1, 1)
    out_ref[...] = (dn1 * norm_ref[0:1, :] + ffn_ref[...].astype(F32)).astype(BF)


def back_theirs(dqkv, w, ffn_back, norms):
    moving = lambda i: (2 + i, 0)
    fixed = lambda i: (0, 0)
    return pl.pallas_call(
        back_kernel,
        grid=(2,),
        in_specs=[
            pl.BlockSpec((2 * ROWS, 3 * PAIR), moving),
            pl.BlockSpec((D, 3 * PAIR), fixed),
            pl.BlockSpec((2 * ROWS, D), moving),
            pl.BlockSpec((4, D), fixed),
        ],
        out_specs=pl.BlockSpec((2 * ROWS, D), lambda i: (i, 0)),
        out_shape=shape((SEQ // 2, D), BF),
        compiler_params=params(),
        cost_estimate=cost(0),
        name="back_theirs",
    )(dqkv, w, keep_far(ffn_back), norms)


def back_sum_kernel(dqkv_ref, w_ref, ffn_ref, norm_ref, other_ref, *out_refs):
    step = pl.program_id(0)
    dn1 = dot(dqkv_ref[...], w_ref[...], 1, 1)
    mine = (dn1 * norm_ref[0:1, :] + ffn_ref[...].astype(F32)).astype(BF)
    total = (mine.astype(F32) + other_ref[...].astype(F32)).astype(BF)
    for n in range(2):

        @pl.when(step == n)
        def _():
            out_refs[2 * n][...] = total[0:ROWS]
            out_refs[2 * n + 1][...] = total[ROWS:]


def back_sum(dqkv, w, ffn_back, norms, other):
    moving = lambda i: (i, 0)
    fixed = lambda i: (0, 0)
    return pl.pallas_call(
        back_sum_kernel,
        grid=(2,),
        in_specs=[
            pl.BlockSpec((2 * ROWS, 3 * PAIR), moving),
            pl.BlockSpec((D, 3 * PAIR), fixed),
            pl.BlockSpec((2 * ROWS, D), moving),
            pl.BlockSpec((4, D), fixed),
            pl.BlockSpec((2 * ROWS, D), moving),
        ],
        out_specs=[pl.BlockSpec((ROWS, D), fixed)] * NZ,
        out_shape=[far((ROWS, D), BF)] * NZ,
        compiler_params=params(),
        cost_estimate=cost(0),
        name="back_sum",
    )(dqkv, w, keep_far(ffn_back), norms, other)


def qkv_grad_kernel(meta_ref, xh_ref, dqkv_ref, w_ref, norm_ref, dy_ref, ffn_vec_ref, grad_ref, vec):
    part = meta_ref[6]
    dqkv = dqkv_ref[...]
    sums = jnp.broadcast_to(jnp.sum(dqkv.astype(F32), axis=0, keepdims=True), (8, 3 * PAIR))
    dy_sum = jnp.sum(dy_ref[...].astype(F32), axis=0, keepdims=True)
    raw = dot(xh_ref[...], dqkv, 0, 0)
    gain = jnp.transpose(jnp.broadcast_to(norm_ref[0:1, :], (8, D)))[:, 0:1]
    shift = jnp.transpose(jnp.broadcast_to(norm_ref[1:2, :], (8, D)))[:, 0:1]
    grad = (raw * gain + shift * sums[0:1, :]).astype(BF)
    for h in range(NXH):
        for p in range(8):
            for ring in range(NZ):
                first = (h * NZ + ring) * 128 + p * 16
                grad_ref[h * 8 + p, ring * 16 : (ring + 1) * 16, 0 : 3 * PAIR] = grad[first : first + 16]
    product = (raw * w_ref[...].astype(F32)).astype(BF)
    norm_rows = [
        dot(jnp.ones((8, 3 * PAIR), BF), product, 1, 1)[0:1],
        dot(sums.astype(BF), w_ref[...], 1, 1)[0:1],
        ffn_vec_ref[0:1, :],
        ffn_vec_ref[8:9, :],
    ]
    vec[...] = jnp.zeros_like(vec)

    def put(bias_row, values):
        place = bias_row + (bias_row // 9) * 7
        vec[pl.ds(place, 1), :] = values

    for n in range(3):
        put(n * 8 + part, sums[0:1, n * PAIR : (n + 1) * PAIR])
    for n in range(4):
        put(32 + part * 4 + n, ffn_vec_ref[16:17, n * 128 : (n + 1) * 128])
    for n in range(8):
        put(24 + n, dy_sum[:, n * 128 : (n + 1) * 128])
        put(64 + n, dy_sum[:, n * 128 : (n + 1) * 128])
        for r in range(4):
            vec[n * 16 + 9 + r : n * 16 + 10 + r, :] = norm_rows[r][:, n * 128 : (n + 1) * 128]
    for h in range(NXH):
        for p in range(8):
            for ring in range(NZ):
                first = (h * NZ + ring) * 16 + 2 * p
                grad_ref[h * 8 + p, ring * 16 : (ring + 1) * 16, 3 * PAIR :] = jnp.concatenate(
                    [vec[first : first + 2, :], jnp.zeros((14, 128), F32)], axis=0
                ).astype(BF)


def qkv_grad(meta, xh, dqkv, w, norms, dy, ffn_vec):
    return pl.pallas_call(
        qkv_grad_kernel,
        in_specs=[SM] + [VM] * 6,
        grid=(1,),
        out_specs=full(16, 64, 4 * PAIR),
        out_shape=far((16, 64, 4 * PAIR), BF),
        scratch_shapes=[pltpu.VMEM((128, 128), F32)],
        compiler_params=params(),
        cost_estimate=cost(0),
        name="qkv_grad",
    )(meta, xh, dqkv, w, norms, dy, ffn_vec)


def body(
    tokens, out_grad, segments, w_qkv, w_proj, w_up, w_down, norm_params, biases,
    prior_moment_qkv, prior_square_qkv, prior_moment_proj, prior_square_proj,
    prior_moment_up, prior_square_up, prior_moment_down, prior_square_down,
    prior_moment_norm, prior_square_norm, prior_moment_bias, prior_square_bias,
):
    rep, shard = lax.axis_index("rep"), lax.axis_index("shard")
    core, y = rep % NC, rep // (NC * NXL)
    where = jnp.stack([core, shard % NZ, y, shard // NZ, rep // NC % NXL]).astype(jnp.int32)

    x_mine = [permute(tokens, SPREAD[k]) for k in range(NZ)]
    docs = segments.astype(BF).reshape(2, 128)
    sent = send_weights(
        where, w_qkv, w_up, w_down, norm_params, biases.reshape(9, 128), docs, sibling(docs)
    )
    received = lax.all_to_all(sent, "shard", 0, 0, tiled=True)
    w_qkv_t, norms, bias, ffn_part, meta = assemble(where, received)
    turns = rotary_tables()
    x_joined = join(x_mine)
    dy_wide, _ = lax.optimization_barrier(
        (jnp.concatenate([out_grad, w_proj.astype(BF)], axis=0), x_joined)
    )
    dy_first = permute(dy_wide, SWAP)
    half = project_qkv(meta, x_joined, w_qkv_t, bias, norms, turns, None, 100)
    x_other = sibling(x_joined)
    n2, xh, q, k, v = project_qkv(meta, x_other, w_qkv_t, bias, norms, turns, half, 0)

    ffn_part = exchange(ffn_part, ALONG_Y)
    dy_block, _ = lax.optimization_barrier((dy_first[:ROWS], x_joined))
    dy_mine = around(dy_block)

    ctx, ctxt, stat = attn_forward(meta, q, k, v)
    ctx, dy_mine = lax.optimization_barrier((ctx, dy_mine))
    dy_joined = join(dy_mine)
    dy_joined, ffn_part = lax.optimization_barrier((dy_joined, ffn_part))
    w_up_t, w_down_t = assemble_ffn(ffn_part)
    dy_other = sibling(dy_joined)
    out_mine, out_theirs, ffn_back, dctx, ffn_vec, ffn_sent = feed_forward(
        meta, dy_joined, dy_other, n2, xh, ctx, w_up_t, w_down_t, dy_first, bias, norms
    )
    out_other = sibling(out_theirs)

    prepared = attn_prepare(q, k, dctx, ctxt, stat)
    dqkv = attn_backward(meta, k, v, stat, turns, prepared)
    qkv_sent = qkv_grad(meta, xh, dqkv, w_qkv_t, norms, out_grad, ffn_vec)
    out_pieces = back_around(core_sum(out_mine, out_other))
    out_sum = fold(out_pieces)
    dqkv, qkv_sent, out_sum, ffn_received = lax.optimization_barrier(
        (dqkv, qkv_sent, out_sum, exchange(ffn_sent, ALONG_Y))
    )
    w_theirs = back_theirs(dqkv, w_qkv_t, ffn_back, norms)
    block_out = finish_out(tokens, bias, permute(out_sum, SWAP))
    w_pieces = back_sum(dqkv, w_qkv_t, ffn_back, norms, sibling(w_theirs))

    qkv_received = exchange(qkv_sent, PLANE)
    ffn_parts = reduce_y(where, ffn_received)
    ffn_parts = [ffn_parts[0]] + [permute(ffn_parts[k], ROUND_X[k]) for k in (1, 2, 3)]
    qkv_received, w_pieces = lax.optimization_barrier((qkv_received, w_pieces))
    ffn_own, *ffn_others = reduce_x(where, ffn_parts, qkv_received)
    ffn_others = [permute(b, ROUND_Z[k + 1]) for k, b in enumerate(ffn_others)]
    ffn_own, block_out = lax.optimization_barrier((ffn_own, block_out))
    mine_grad = exchange(pack(where, ffn_own, ffn_others), COPIES)
    mine_grad, w_sum = lax.optimization_barrier((mine_grad, fold(back_around(w_pieces))))
    mine_grad = mine_grad.reshape(128, WIDE)
    their_grad = sibling(mine_grad)
    g_up, g_down, g_proj, g_qkv, small = merge(where, mine_grad, their_grad)
    w_sum = permute(w_sum, SWAP)
    g_norm = small[9:13]
    g_bias = small[:9].reshape(1152)

    def matrix_step(weight, moment, square, grad):
        return adam_step(weight, moment, square, grad.astype(F32), RATE_MATRIX, DECAY)

    new_qkv = matrix_step(w_qkv, prior_moment_qkv, prior_square_qkv, g_qkv)
    new_proj = matrix_step(w_proj, prior_moment_proj, prior_square_proj, g_proj)
    new_up = matrix_step(w_up, prior_moment_up, prior_square_up, g_up)
    new_down = matrix_step(w_down, prior_moment_down, prior_square_down, g_down)
    w_sum, new_qkv = lax.optimization_barrier((w_sum, new_qkv))
    grad_tokens = finish_grad(tokens, out_grad, w_sum)
    new_norm = adam_step(norm_params, prior_moment_norm, prior_square_norm, g_norm, RATE_VECTOR, 0.0)
    new_bias = adam_step(biases, prior_moment_bias, prior_square_bias, g_bias, RATE_VECTOR, 0.0)
    return (block_out, grad_tokens, *new_qkv, *new_proj, *new_up, *new_down, *new_norm, *new_bias)


def solution(mesh):
    token = P(("rep", "shard"), None)
    row = P("shard", None)
    norm = P(None, "shard")
    flat = P("shard")
    in_specs = (
        (token, token, P(("rep", "shard")))
        + (row,) * 4
        + (norm, flat)
        + (row,) * 8
        + (norm, norm, flat, flat)
    )
    out_specs = (token, token) + (row,) * 12 + (norm,) * 3 + (flat,) * 3
    return jax.shard_map(body, mesh=mesh, in_specs=in_specs, out_specs=out_specs, check_vma=False)
```

```python
import functools

import jax
import jax.numpy as jnp
import numpy as np
from jax import lax
from jax.experimental import pallas as pl
from jax.experimental.pallas import tpu as pltpu
from jax.sharding import PartitionSpec as P

HEAD_DIM = 64
ROT = 16
STEP = 10
EPS_NORM = 1e-05
BETA_ONE = 0.9
BETA_TWO = 0.95
RATE_MATRIX = 0.05
RATE_VECTOR = 0.3
DECAY = 0.01
ADAM_EPS = 1e-08
NEGATIVE = -1e30

NY, NXL, NC, NXH, NZ = 4, 2, 2, 2, 4
AXES = ("rep", "shard")
D = 1024
ROWS = 256
SEQ = 2048
FF = 4096
PAIR = 128
HID = 512
QB = 512
BF = jnp.bfloat16
F32 = jnp.float32


def device_pairs(move):
    pairs = []
    for y in range(NY):
        for xl in range(NXL):
            for c in range(NC):
                for h in range(NXH):
                    for z in range(NZ):
                        ty, txl, tc, th, tz = move(y, xl, c, h, z)
                        pairs.append(
                            (
                                ((y * NXL + xl) * NC + c) * 8 + h * NZ + z,
                                ((ty * NXL + txl) * NC + tc) * 8 + th * NZ + tz % NZ,
                            )
                        )
    return pairs


SWAP = device_pairs(lambda y, xl, c, h, z: (y, xl, h, c, z))


SIBLING = device_pairs(lambda y, xl, c, h, z: (y, xl, 1 - c, h, z))
ROUND_X = [
    device_pairs(
        lambda y, xl, c, h, z, k=k: (y, (h * 2 + xl + k) % 4 % 2, c, (h * 2 + xl + k) % 4 // 2, z)
    )
    for k in range(4)
]
ROUND_Z = [device_pairs(lambda y, xl, c, h, z, k=k: (y, xl, c, h, z + k)) for k in range(NZ)]


def device(y, xl, c, h, z):
    return ((y * NXL + xl) * NC + c) * 8 + h * NZ + z


RANGES = dict(y=range(NY), xl=range(NXL), c=range(NC), h=range(NXH), z=range(NZ))


def groups(*inner):
    outer = [name for name in RANGES if name not in inner]

    def walk(names, at):
        if not names:
            return [device(**at)]
        return [d for n in RANGES[names[0]] for d in walk(names[1:], dict(at, **{names[0]: n}))]

    def each(names, at):
        if not names:
            return [walk(inner, at)]
        return [g for n in RANGES[names[0]] for g in each(names[1:], dict(at, **{names[0]: n}))]

    return each(outer, {})


ALONG_Y = groups("y")
ALONG_Z = groups("z")
PLANE = groups("h", "y", "xl")
COPIES = groups("y", "xl")


SPREAD = [device_pairs(lambda y, xl, c, h, z, k=k: (y, xl, h, c, z + k)) for k in range(NZ)]


def permute(values, pairs):
    return lax.ppermute(values, AXES, pairs)


def around(block):
    return [block] + [permute(block, ROUND_Z[k]) for k in (1, 2, 3)]


def back_around(blocks):
    return [blocks[0]] + [permute(blocks[k], ROUND_Z[NZ - k]) for k in (1, 2, 3)]


def sibling(values):
    return lax.ppermute(values, AXES, SIBLING)


def exchange(values, members):
    return lax.all_to_all(values, AXES, 0, 0, axis_index_groups=members, tiled=True)


def dot(a, b, ca, cb):
    return lax.dot_general(a, b, (((ca,), (cb,)), ((), ())), preferred_element_type=F32)


def gelu_parts(values):
    cdf = 0.5 * (1.0 + lax.erf(values * np.float32(np.sqrt(0.5))))
    density = jnp.exp(-0.5 * values * values) * np.float32(1.0 / np.sqrt(2.0 * np.pi))
    return values * cdf, cdf + values * density


def adam_step(weight, moment, square, gradient, rate, decay):
    moment_new = BETA_ONE * moment + (1.0 - BETA_ONE) * gradient
    square_new = BETA_TWO * square + (1.0 - BETA_TWO) * gradient * gradient
    fixed_moment = moment_new / (1.0 - BETA_ONE**STEP)
    fixed_square = square_new / (1.0 - BETA_TWO**STEP)
    weight_new = weight - rate * (
        fixed_moment / (jnp.sqrt(fixed_square) + ADAM_EPS) + decay * weight
    )
    return (weight_new, moment_new, square_new)


SM = pl.BlockSpec(memory_space=pltpu.SMEM)
VM = pl.BlockSpec(memory_space=pltpu.VMEM)


def full(*dims):
    return pl.BlockSpec(dims, lambda i: (0,) * len(dims))


WHOLE = pl.BlockSpec((SEQ, PAIR), lambda i: (0, 0))


def params(mib=16):
    return pltpu.CompilerParams(vmem_limit_bytes=mib * 2**20)


def cost(us):
    flops = int(us * 7e8)
    return pl.CostEstimate(flops=flops, bytes_accessed=int(us * 2e6), transcendentals=0)


def shape(dims, kind):
    return jax.ShapeDtypeStruct(dims, kind)


def far(dims, kind):
    return pltpu.HBM(dims, kind)


def keep_far(values):
    return pltpu.with_memory_space_constraint(values, pltpu.HBM)


def send_weights_kernel(
    where_ref, q_ref, k_ref, v_ref, up_ref, down_ref, norm_ref, bias_ref, seg_ref, sib_ref, out_ref
):
    misc = jnp.concatenate(
        [norm_ref[...], bias_ref[...], seg_ref[...].astype(F32), jnp.zeros((1, 128), F32)], axis=0
    ).astype(BF)
    theirs = jnp.concatenate([sib_ref[...].astype(F32), jnp.zeros((14, 128), F32)], axis=0).astype(BF)
    for n in range(8):
        for part, ref in enumerate((q_ref, k_ref, v_ref)):
            source = slice((n % NZ) * PAIR, (n % NZ + 1) * PAIR)
            out_ref[n, 0:128, part * PAIR : (part + 1) * PAIR] = ref[:, source].astype(BF)
        out_ref[n, 128:144, 0:128] = misc
        out_ref[n, 128:144, 128:256] = theirs
        out_ref[n, 128:144, 256:384] = jnp.zeros((16, 128), BF)
        for j in range(8):
            ref = (up_ref, down_ref)[j // 4]
            source = (n % NZ) * HID + (j % 4) * 128
            first = 144 + (j // 3) * 32
            out_ref[n, first : first + 32, (j % 3) * 128 : (j % 3 + 1) * 128] = ref[
                :, source : source + 128
            ].astype(BF)
        out_ref[n, 208:240, 256:384] = jnp.zeros((32, 128), BF)


def send_weights(where, w, up, down, norms, biases, segments, sibling_segments):
    third = lambda part: pl.BlockSpec((128, 512), lambda i, where: (0, part * 2 + where[0]))
    rows = pl.BlockSpec((32, 2048), lambda i, where: (where[2], where[0]))
    small = lambda count: pl.BlockSpec((count, 128), lambda i, where: (0, 0))
    return pl.pallas_call(
        send_weights_kernel,
        grid_spec=pltpu.PrefetchScalarGridSpec(
            num_scalar_prefetch=1,
            grid=(1,),
            in_specs=[third(0), third(1), third(2), rows, rows] + [small(4), small(9), small(2), small(2)],
            out_specs=pl.BlockSpec((8, 240, 384), lambda i, where: (0, 0, 0)),
        ),
        out_shape=far((8, 240, 384), BF),
        compiler_params=params(),
        cost_estimate=cost(0),
        name="send_weights",
    )(
        where, *[keep_far(w)] * 3, keep_far(up), keep_far(down),
        keep_far(norms), biases, segments, sibling_segments,
    )


def join_kernel(*refs):
    for k in range(NZ):
        refs[NZ][k * ROWS : (k + 1) * ROWS, :] = refs[k][...]


def join(blocks):
    return pl.pallas_call(
        join_kernel,
        in_specs=[VM] * NZ,
        out_specs=VM,
        out_shape=shape((SEQ // 2, D), BF),
        compiler_params=params(),
        cost_estimate=cost(0),
        name="join",
    )(*blocks)


def doc_start(ids, meta_ref):
    start = jnp.zeros_like(ids)
    for d in range(4):
        start = jnp.where(ids >= meta_ref[d], meta_ref[d], start)
    return start


def block_tables(where_ref, meta_ref):
    c, z = where_ref[0], where_ref[1]
    meta_ref[4] = c
    meta_ref[5] = z
    meta_ref[6] = c * NZ + z
    meta_ref[7] = where_ref[2]
    for j in range(2):
        half = c if j == 0 else 1 - c
        for k in range(NZ):
            meta_ref[8 + j * NZ + k] = half * NZ + jnp.bitwise_and(z + NZ - k, NZ - 1)
    for half in range(2):
        base = jnp.bitwise_xor(c, half) * NZ
        for ring in range(NZ):
            meta_ref[16 + half * NZ + ring] = base + jnp.bitwise_and(z + NZ - ring, NZ - 1)


def assemble_kernel(
    where_ref, in_ref, w_ref, norm_ref, bias_ref, ffn_ref, meta_ref
):
    block_tables(where_ref, meta_ref)
    counts = [jnp.zeros((1, 128), F32) for _ in range(4)]
    native = (where_ref[0] == where_ref[3]).astype(F32)
    for n in range(8):
        w_ref[n * 128 : (n + 1) * 128, :] = in_ref[n, 0:128, :]
        misc = in_ref[n, 128:144, 0:128].astype(F32)
        other = in_ref[n, 128:144, 128:256].astype(F32)
        norm_ref[:, n * 128 : (n + 1) * 128] = misc[0:4]
        bias_ref[n * 9 : (n + 1) * 9, :] = misc[4:13]
        docs = misc[13:15] * native + other[0:2] * (1.0 - native)
        for d in range(4):
            below = jnp.where(docs < d + 0.5, 1.0, 0.0)
            counts[d] = counts[d] + below[0:1] + below[1:2]
        for j in range(8):
            first = 144 + (j // 3) * 32
            block = in_ref[n, first : first + 32, (j % 3) * 128 : (j % 3 + 1) * 128]
            for y in range(NY):
                ffn_ref[y, n * 32 : (n + 1) * 32, j * 128 : (j + 1) * 128] = block
    for d in range(4):
        meta_ref[d] = jnp.sum(counts[d]).astype(jnp.int32)


def rotary_tables():
    lane = np.arange(PAIR) % HEAD_DIM
    freq = 10000.0 ** (-2.0 * (lane % (ROT // 2)) / ROT)
    angles = np.arange(SEQ)[:, None] * np.where(lane < ROT, freq, 0.0)[None, :]
    return jnp.asarray(np.where(np.arange(PAIR) < HEAD_DIM, np.cos(angles), np.sin(angles)), F32)


def both_heads(table):
    first = lax.broadcasted_iota(jnp.int32, table.shape, 1) < HEAD_DIM
    other = pltpu.roll(table, HEAD_DIM, 1)
    return jnp.where(first, table, other), jnp.where(first, other, table)


def assemble(where, received):
    return pl.pallas_call(
        assemble_kernel,
        grid=(1,),
        in_specs=[SM, VM],
        out_specs=[VM] * 3 + [pl.BlockSpec((NY, ROWS, 2 * HID), lambda i: (0, 0, 0)), SM],
        out_shape=[
            shape((D, 3 * PAIR), BF),
            shape((4, D), F32),
            shape((72, 128), F32),
            far((NY, ROWS, 2 * HID), BF),
            shape((24,), jnp.int32),
        ],
        compiler_params=params(),
        cost_estimate=cost(0),
        name="assemble",
    )(where, received)


def assemble_ffn_kernel(in_ref, up_ref, down_ref):
    for y in range(NY):
        for n in range(8):
            rows = slice(n * 128 + y * 32, n * 128 + (y + 1) * 32)
            up_ref[rows, :] = in_ref[y, n * 32 : (n + 1) * 32, 0:HID]
            down_ref[rows, :] = in_ref[y, n * 32 : (n + 1) * 32, HID:]


def assemble_ffn(parts):
    return pl.pallas_call(
        assemble_ffn_kernel,
        in_specs=[VM],
        out_specs=[VM] * 2,
        out_shape=[shape((D, HID), BF)] * 2,
        compiler_params=params(),
        cost_estimate=cost(0),
        name="assemble_ffn",
    )(parts)


def turn(u, cosine, sine):
    lane = lax.broadcasted_iota(jnp.int32, u.shape, 1) % HEAD_DIM
    left = pltpu.roll(u, PAIR - ROT // 2, 1)
    right = pltpu.roll(u, ROT // 2, 1)
    return u * cosine + jnp.where(lane < ROT // 2, -left, right) * sine


def qkv_kernel(meta_ref, x_ref, w_ref, bias_ref, norm_ref, turn_ref, *refs):
    n2_ref, xh_ref, q_ref, k_ref, v_ref = refs[-5:]
    x = x_ref[...].astype(F32)
    centred = x - jnp.mean(x, axis=-1, keepdims=True)
    variance = jnp.mean(centred * centred, axis=-1, keepdims=True)
    xh = centred * lax.rsqrt(variance + EPS_NORM)
    n1 = (xh * norm_ref[0:1, :] + norm_ref[1:2, :]).astype(BF)
    xh_ref[...] = xh.astype(BF)
    n2_ref[...] = (xh * norm_ref[2:3, :] + norm_ref[3:4, :]).astype(BF)
    part = meta_ref[6]
    cosine, sine = both_heads(turn_ref[...])
    qkv = dot(n1, w_ref[...], 1, 0)
    q = qkv[:, 0:PAIR] + bias_ref[pl.ds(part, 1), :]
    k = qkv[:, PAIR : 2 * PAIR] + bias_ref[pl.ds(8 + part, 1), :]
    v = qkv[:, 2 * PAIR :] + bias_ref[pl.ds(16 + part, 1), :]
    q_ref[...] = (turn(q, cosine, sine).astype(BF) * 0.125).astype(BF)
    k_ref[...] = turn(k, cosine, sine).astype(BF)
    v_ref[...] = v.astype(BF)


def project_qkv(meta, x, w, bias, norms, turns, before, us):
    base = 0 if before is None else NZ
    moving = lambda i, meta: (i, 0)
    physical = lambda i, meta: (base + i, 0)
    logical = lambda i, meta: (meta[8 + base + i], 0)
    fixed = lambda i, meta: (0, 0)
    extra = [] if before is None else list(before)
    return pl.pallas_call(
        qkv_kernel,
        grid_spec=pltpu.PrefetchScalarGridSpec(
            num_scalar_prefetch=1,
            grid=(NZ,),
            in_specs=[
                pl.BlockSpec((ROWS, D), moving),
                pl.BlockSpec((D, 3 * PAIR), fixed),
                pl.BlockSpec((72, 128), fixed),
                pl.BlockSpec((4, D), fixed),
                pl.BlockSpec((ROWS, PAIR), logical),
            ]
            + [pl.BlockSpec(memory_space=pl.ANY)] * len(extra),
            out_specs=[pl.BlockSpec((ROWS, D), physical)] * 2
            + [pl.BlockSpec((ROWS, PAIR), logical)] * 3,
        ),
        out_shape=[far((SEQ, D), BF)] * 2 + [far((SEQ, PAIR), BF)] * 3,
        input_output_aliases={6 + n: n for n in range(len(extra))},
        compiler_params=params(),
        cost_estimate=cost(us),
        name="project_qkv",
    )(meta, x, w, bias, norms, keep_far(turns), *extra)


def head_only(values, h):
    lane = lax.broadcasted_iota(jnp.int32, values.shape, 1)
    return jnp.where((lane // HEAD_DIM) == h, values, jnp.zeros_like(values))


def keep_allowed(meta_ref, i, j, values, other):
    keys = j * QB + lax.broadcasted_iota(jnp.int32, (QB, QB), 0)
    queries = i * QB + lax.broadcasted_iota(jnp.int32, (1, QB), 1)
    allowed = None
    if i == j:
        allowed = keys <= queries
    if j == 0 or i == SEQ // QB - 1:
        same = keys >= doc_start(queries, meta_ref)
        allowed = same if allowed is None else allowed & same
    return values if allowed is None else jnp.where(allowed, values, other)


def attn_forward_kernel(meta_ref, q_ref, k_ref, v_ref, ctx_ref, ctxt_ref, stat_ref, vt_ref):
    for b in range(SEQ // QB):
        vt_ref[:, b * QB : (b + 1) * QB] = v_ref[b * QB : (b + 1) * QB, :].T
    for i in range(SEQ // QB):
        here = slice(i * QB, (i + 1) * QB)
        parts = []
        for h in range(2):
            q = head_only(q_ref[here, :], h)
            m = l = acc = None
            for j in range(i + 1):
                there = slice(j * QB, (j + 1) * QB)
                scores = keep_allowed(meta_ref, i, j, dot(k_ref[there, :], q, 1, 1), NEGATIVE)
                top = jnp.max(scores, axis=0, keepdims=True)
                if j > 0:
                    top = jnp.maximum(m, top)
                expo = jnp.exp(scores - top)
                total = jnp.sum(expo, axis=0, keepdims=True)
                values = vt_ref[h * HEAD_DIM : (h + 1) * HEAD_DIM, there]
                add = dot(values, expo.astype(BF), 1, 0)
                if j > 0:
                    fade = jnp.exp(m - top)
                    total, add = l * fade + total, acc * fade + add
                m, l, acc = top, total, add
            parts.append(acc / l)
            stat_ref[h : h + 1, here] = m
            stat_ref[2 + h : 3 + h, here] = 1.0 / l
        ctxt = jnp.concatenate(parts, axis=0)
        ctxt_ref[:, here] = ctxt
        low = ctxt.astype(BF).T
        for b in range(QB // ROWS):
            row = pl.multiple_of(meta_ref[16 + i * (QB // ROWS) + b] * ROWS, ROWS)
            ctx_ref[pl.ds(row, ROWS), :] = low[b * ROWS : (b + 1) * ROWS]


def attn_forward(meta, q, k, v):
    return pl.pallas_call(
        attn_forward_kernel,
        grid=(1,),
        in_specs=[SM, WHOLE, WHOLE, WHOLE],
        out_specs=[WHOLE, pl.BlockSpec((PAIR, SEQ), lambda i: (0, 0)), VM],
        out_shape=[far((SEQ, PAIR), BF), far((PAIR, SEQ), F32), shape((8, SEQ), F32)],
        scratch_shapes=[pltpu.VMEM((PAIR, SEQ), BF)],
        compiler_params=params(),
        cost_estimate=cost(0),
        name="attn_forward",
    )(meta, keep_far(q), keep_far(k), keep_far(v))


def attn_prepare_kernel(
    q_ref, k_ref, dctx_ref, ctxt_ref, stat_ref, kt_ref, du_ref, dut_ref, qh_ref, c_ref
):
    kt_ref[...] = k_ref[...].T
    dctxt = dctx_ref[...].T
    prod = dctxt * ctxt_ref[...]
    c_ref[...] = jnp.zeros_like(c_ref)
    for h in range(2):
        rows = slice(h * HEAD_DIM, (h + 1) * HEAD_DIM)
        inverse = stat_ref[2 + h : 3 + h, :]
        c_ref[h : h + 1, :] = jnp.sum(prod[rows], axis=0, keepdims=True) * inverse
        dut = (dctxt[rows] * inverse).astype(BF)
        dut_ref[h, rows, :] = dut
        dut_ref[h, (1 - h) * HEAD_DIM : (2 - h) * HEAD_DIM, :] = jnp.zeros_like(dut)
        du_ref[h] = dut_ref[h].T
        qh_ref[h] = head_only(q_ref[...], h)


def attn_prepare(q, k, dctx, ctxt, stat):
    down = pl.BlockSpec((QB, PAIR), lambda i: (i, 0))
    across = lambda rows: pl.BlockSpec((rows, QB), lambda i: (0, i))
    down_heads = pl.BlockSpec((2, QB, PAIR), lambda i: (0, i, 0))
    across_heads = pl.BlockSpec((2, PAIR, QB), lambda i: (0, 0, i))
    return pl.pallas_call(
        attn_prepare_kernel,
        grid=(SEQ // QB,),
        in_specs=[down, down, down, across(PAIR), across(8)],
        out_specs=[across(PAIR), down_heads, across_heads, down_heads, across(8)],
        out_shape=[
            shape((PAIR, SEQ), BF),
            shape((2, SEQ, PAIR), BF),
            shape((2, PAIR, SEQ), BF),
            shape((2, SEQ, PAIR), BF),
            shape((8, SEQ), F32),
        ],
        compiler_params=params(),
        cost_estimate=cost(60),
        name="attn_prepare",
    )(keep_far(q), keep_far(k), keep_far(dctx), keep_far(ctxt), stat)


def attn_backward_kernel(
    meta_ref, k_ref, v_ref, stat_ref, turn_ref, kt_ref, du_ref, dut_ref, qh_ref, c_ref,
    out_ref,
    dqt_ref,
):
    blocks = SEQ // QB

    def put(b, lanes, values):
        for n in range(QB // ROWS):
            place = pl.multiple_of(meta_ref[16 + b * (QB // ROWS) + n] * ROWS, ROWS)
            out_ref[pl.ds(place, ROWS), lanes] = values[n * ROWS : (n + 1) * ROWS].astype(BF)

    for j in range(blocks):
        there = slice(j * QB, (j + 1) * QB)
        keys, values = k_ref[there, :], v_ref[there, :]
        dk = dv = None
        for i in range(j, blocks):
            here = slice(i * QB, (i + 1) * QB)
            for h in range(2):
                qh = qh_ref[h, here, :]
                scores = dot(keys, qh, 1, 1)
                expo = jnp.exp(scores - stat_ref[h : h + 1, here])
                expo = keep_allowed(meta_ref, i, j, expo, 0.0)
                dexpo = dot(values, dut_ref[h, :, here], 1, 0)
                dscore = (expo * (dexpo - c_ref[h : h + 1, here])).astype(BF)
                dv_add = dot(expo.astype(BF), du_ref[h, here, :], 1, 0)
                dk_add = dot(dscore, qh, 1, 0)
                dk = dk_add if dk is None else dk + dk_add
                dv = dv_add if dv is None else dv + dv_add
                rows = slice(h * HEAD_DIM, (h + 1) * HEAD_DIM)
                dq_add = dot(kt_ref[rows, there], dscore, 1, 0)
                dqt_ref[rows, here] = dq_add if j == 0 else dqt_ref[rows, here] + dq_add
        cosine, sine = both_heads(turn_ref[there, :])
        dq = (dqt_ref[:, there] * 0.125).T
        put(j, slice(0, PAIR), turn(dq, cosine, -sine))
        put(j, slice(PAIR, 2 * PAIR), turn(dk, cosine, -sine))
        put(j, slice(2 * PAIR, 3 * PAIR), dv)


def attn_backward(meta, k, v, stat, turns, prepared):
    return pl.pallas_call(
        attn_backward_kernel,
        grid=(1,),
        in_specs=[SM, WHOLE, WHOLE, VM, WHOLE] + [VM] * 5,
        out_specs=VM,
        out_shape=shape((SEQ, 3 * PAIR), BF),
        scratch_shapes=[
            pltpu.VMEM((PAIR, SEQ), F32),
        ],
        compiler_params=params(),
        cost_estimate=cost(100),
        name="attn_backward",
    )(meta, keep_far(k), keep_far(v), stat, keep_far(turns), *prepared)


def lay_rows(ref, first, count):
    return jnp.concatenate([ref[pl.ds(first + r, 1), :] for r in range(count)], axis=1)


def by_half(double):
    return [
        pl.BlockSpec((double, D), lambda i, meta: (jnp.minimum(i, 1), 0)),
        pl.BlockSpec((double, D), lambda i, meta: (jnp.maximum(i - 2, 0), 0)),
    ]


def take_half(step, mine_ref, theirs_ref, now_ref):
    @pl.when(step < 2)
    def _():
        now_ref[...] = mine_ref[...]

    @pl.when(step >= 2)
    def _():
        now_ref[...] = theirs_ref[...]


def ffn_kernel(meta_ref, *refs):
    mine_ref, theirs_ref = refs[:2]
    n2_ref, xh_ref, ctx_ref, up_ref, down_ref, proj_ref, bias_ref, norm_ref = refs[2:10]
    out_mine_ref, out_theirs_ref, back_ref, dctx_ref, vec_ref, grad_ref = refs[10:16]
    dy_now, gup, gdown, gproj, total = refs[16:]
    step = pl.program_id(0)
    part = meta_ref[6]

    @pl.when(step == 0)
    def _():
        gup[...] = jnp.zeros_like(gup)
        gdown[...] = jnp.zeros_like(gdown)
        gproj[...] = jnp.zeros_like(gproj)
        total[...] = jnp.zeros_like(total)

    take_half(step, mine_ref, theirs_ref, dy_now)
    dy = dy_now[...]
    ctx = ctx_ref[...]
    dctx = dot(dy, proj_ref[...], 1, 1)
    for b in range(2):
        row = pl.multiple_of(meta_ref[8 + 2 * step + b] * ROWS, ROWS)
        dctx_ref[pl.ds(row, ROWS), :] = dctx[b * ROWS : (b + 1) * ROWS]
    gproj[...] += dot(ctx, dy, 0, 0)
    bias_up = lay_rows(bias_ref, 32 + 4 * part, 4)
    pre = dot(n2_ref[...], up_ref[...], 1, 0) + bias_up
    hidden, slope = gelu_parts(pre)
    hidden = hidden.astype(BF)
    dpre = (dot(dy, down_ref[...], 1, 0) * slope).astype(BF)
    out = (dot(ctx, proj_ref[...], 1, 0) + dot(hidden, down_ref[...], 1, 1)).astype(BF)

    @pl.when(step < 2)
    def _():
        out_mine_ref[...] = out

    @pl.when(step >= 2)
    def _():
        out_theirs_ref[...] = out

    back_ref[...] = (dot(dpre, up_ref[...], 1, 1) * norm_ref[2:3, :]).astype(BF)
    gdown[...] += dot(dy, hidden, 0, 0)
    gup[...] += dot(xh_ref[...], dpre, 0, 0)
    total[...] += jnp.broadcast_to(jnp.sum(dpre.astype(F32), axis=0, keepdims=True), total.shape)

    @pl.when(step == 3)
    def _():
        sums = total[...]
        raw = gup[...]
        gain = jnp.transpose(jnp.broadcast_to(norm_ref[2:3, :], (8, D)))[:, 0:1]
        shift = jnp.transpose(jnp.broadcast_to(norm_ref[3:4, :], (8, D)))[:, 0:1]
        product = (raw * up_ref[...].astype(F32)).astype(BF)
        gup[...] = raw * gain + shift * sums[0:1, :]
        for y in range(NY):
            for n in range(8):
                here = slice(n * 32, (n + 1) * 32)
                rows = slice(n * 128 + y * 32, n * 128 + (y + 1) * 32)
                grad_ref[y, here, 0:HID] = gup[rows, :].astype(BF)
                grad_ref[y, here, HID:] = gdown[rows, :].astype(BF)
            grad_ref[y, 256:288, :] = gproj[y * 32 : (y + 1) * 32, :].astype(BF)
        vec_ref[0:8, :] = dot(jnp.ones((8, HID), BF), product, 1, 1)
        vec_ref[8:16, :] = dot(sums.astype(BF), up_ref[...], 1, 1)
        vec_ref[16:24, 0:HID] = sums
        vec_ref[16:24, HID:] = jnp.zeros((8, D - HID), F32)


def feed_forward(meta, mine, theirs, n2, xh, ctx, up, down, proj, bias, norms):
    double = 2 * ROWS
    moving = lambda i, meta: (i, 0)
    fixed = lambda i, meta: (0, 0)
    once = pl.Buffered(1)
    return pl.pallas_call(
        ffn_kernel,
        grid_spec=pltpu.PrefetchScalarGridSpec(
            num_scalar_prefetch=1,
            grid=(4,),
            in_specs=by_half(double)
            + [
                pl.BlockSpec((double, D), moving),
                pl.BlockSpec((double, D), moving),
                pl.BlockSpec((double, PAIR), moving),
                pl.BlockSpec((D, HID), fixed, pipeline_mode=once),
                pl.BlockSpec((D, HID), fixed, pipeline_mode=once),
                pl.BlockSpec((PAIR, D), lambda i, meta: (2, 0), pipeline_mode=once),
                pl.BlockSpec((72, 128), fixed, pipeline_mode=once),
                pl.BlockSpec((4, D), fixed, pipeline_mode=once),
            ],
            out_specs=by_half(double)
            + [
                pl.BlockSpec((double, D), moving),
                pl.BlockSpec((SEQ, PAIR), fixed),
                VM,
                pl.BlockSpec((NY, 288, D), lambda i, meta: (0, 0, 0)),
            ],
            scratch_shapes=[
                pltpu.VMEM((double, D), BF),
                pltpu.VMEM((D, HID), F32),
                pltpu.VMEM((D, HID), F32),
                pltpu.VMEM((PAIR, D), F32),
                pltpu.VMEM((8, HID), F32),
            ],
        ),
        out_shape=[
            far((SEQ // 2, D), BF),
            far((SEQ // 2, D), BF),
            far((SEQ, D), BF),
            far((SEQ, PAIR), F32),
            shape((24, D), F32),
            far((NY, 288, D), BF),
        ],
        compiler_params=params(40),
        cost_estimate=cost(60),
        name="feed_forward",
    )(meta, mine, theirs, keep_far(n2), keep_far(xh), keep_far(ctx), up, down, proj, bias, norms)


def core_sum_kernel(mine_ref, theirs_ref, *sent_refs):
    step = pl.program_id(0)
    total = (mine_ref[...].astype(F32) + theirs_ref[...].astype(F32)).astype(BF)
    for k in range(NZ):

        @pl.when(step == k)
        def _():
            sent_refs[k][...] = total


def core_sum(mine, theirs):
    moving = lambda i: (i, 0)
    return pl.pallas_call(
        core_sum_kernel,
        grid=(NZ,),
        in_specs=[pl.BlockSpec((ROWS, D), moving)] * 2,
        out_specs=[pl.BlockSpec((ROWS, D), lambda i: (0, 0))] * NZ,
        out_shape=[shape((ROWS, D), BF)] * NZ,
        compiler_params=params(),
        cost_estimate=cost(0),
        name="core_sum",
    )(mine, theirs)


def fold_kernel(*refs):
    total = refs[0][...].astype(F32)
    for k in range(1, NZ):
        total = total + refs[k][...].astype(F32)
    refs[NZ][...] = total.astype(BF)


def fold(pieces):
    return pl.pallas_call(
        fold_kernel,
        in_specs=[VM] * NZ,
        out_specs=VM,
        out_shape=shape((ROWS, D), BF),
        compiler_params=params(),
        cost_estimate=cost(0),
        name="fold",
    )(*pieces)


def finish_out_kernel(x_ref, bias_ref, sum_ref, out_ref):
    bias = lay_rows(bias_ref, 24, 8) + lay_rows(bias_ref, 64, 8)
    out_ref[...] = (x_ref[...].astype(F32) + sum_ref[...].astype(F32) + bias).astype(BF)


def finish_out(x, bias, total):
    half = pl.BlockSpec((ROWS // 2, D), lambda i: (i, 0))
    return pl.pallas_call(
        finish_out_kernel,
        grid=(2,),
        in_specs=[half, pl.BlockSpec((72, 128), lambda i: (0, 0)), half],
        out_specs=half,
        out_shape=shape((ROWS, D), BF),
        compiler_params=params(),
        cost_estimate=cost(0),
        name="finish_out",
    )(keep_far(x), bias, total)


def finish_grad_kernel(x_ref, dy_ref, sum_ref, out_ref):
    w = sum_ref[...].astype(F32)
    x = x_ref[...].astype(F32)
    centred = x - jnp.mean(x, axis=-1, keepdims=True)
    rstd = lax.rsqrt(jnp.mean(centred * centred, axis=-1, keepdims=True) + EPS_NORM)
    xh = centred * rstd
    inner = w - jnp.mean(w, axis=-1, keepdims=True) - xh * jnp.mean(w * xh, axis=-1, keepdims=True)
    out_ref[...] = dy_ref[...].astype(F32) + rstd * inner


def finish_grad(x, dy, total):
    half = pl.BlockSpec((ROWS // 2, D), lambda i: (i, 0))
    return pl.pallas_call(
        finish_grad_kernel,
        grid=(2,),
        in_specs=[half] * 3,
        out_specs=half,
        out_shape=shape((ROWS, D), F32),
        compiler_params=params(),
        cost_estimate=cost(0),
        name="finish_grad",
    )(keep_far(x), keep_far(dy), total)


def reduce_y_kernel(where_ref, ffn_ref, *refs):
    low_ref = refs[4]
    total = ffn_ref[0].astype(F32)
    for n in range(1, NY):
        total = total + ffn_ref[n].astype(F32)
    low_ref[...] = total.astype(BF)
    x = where_ref[3] * NXL + where_ref[4]
    for k in range(4):
        target = jnp.bitwise_and(x + k, 3)
        half, low_x = target // 2, jnp.bitwise_and(target, 1)
        for ring in range(NZ):
            rows = pl.ds(pl.multiple_of((half * NZ + ring) * 32 + low_x * 16, 16), 16)
            refs[k][ring * 16 : (ring + 1) * 16, :] = low_ref[rows, :]
        refs[k][64:80, :] = low_ref[pl.ds(pl.multiple_of(256 + low_x * 16, 16), 16), :]


def reduce_y(where, ffn):
    return pl.pallas_call(
        reduce_y_kernel,
        grid=(1,),
        in_specs=[SM, full(NY, 288, D)],
        out_specs=[VM] * 4,
        out_shape=[shape((80, D), BF)] * 4,
        scratch_shapes=[pltpu.VMEM((288, D), BF)],
        compiler_params=params(),
        cost_estimate=cost(0),
        name="reduce_y",
    )(where, keep_far(ffn))


def reduce_x_kernel(where_ref, *refs):
    ffn_refs, qkv_ref, own_ref, sent_refs = refs[:4], refs[4], refs[5], refs[6:9]
    low_ref, low_qkv_ref = refs[9:]
    z = where_ref[1]
    total, total_qkv = ffn_refs[0][...].astype(F32), qkv_ref[0].astype(F32)
    for n in range(1, 4):
        total = total + ffn_refs[n][...].astype(F32)
    for n in range(1, 16):
        total_qkv = total_qkv + qkv_ref[n].astype(F32)
    low_ref[...] = total.astype(BF)
    low_qkv_ref[...] = total_qkv.astype(BF)
    for k in range(NZ):
        out_ref = own_ref if k == 0 else sent_refs[k - 1]
        rows = pl.ds(pl.multiple_of(jnp.bitwise_and(z + k, NZ - 1) * 16, 16), 16)
        out_ref[0:16, :] = low_ref[rows, :]
        out_ref[16:32, 0:512] = low_qkv_ref[rows, :]
        out_ref[16:32, 512:] = jnp.zeros((16, 512), BF)
    own_ref[32:48, :] = low_ref[64:80, :]


def reduce_x(where, ffn, qkv):
    return pl.pallas_call(
        reduce_x_kernel,
        grid=(1,),
        in_specs=[SM] + [VM] * 4 + [full(16, 64, 4 * PAIR)],
        out_specs=[VM] * 4,
        out_shape=[shape((48, D), BF)] + [shape((32, D), BF)] * 3,
        scratch_shapes=[pltpu.VMEM((80, D), BF), pltpu.VMEM((64, 4 * PAIR), BF)],
        compiler_params=params(),
        cost_estimate=cost(0),
        name="reduce_x",
    )(where, *ffn, keep_far(qkv))


UP, DOWN, PROJ, QKV, SMALL, WIDE = 0, 2048, 4096, 5120, 6656, 6784


def pack_kernel(where_ref, *refs):
    out_ref = refs[NZ]
    z = where_ref[1]
    small = jnp.zeros((16, 128), F32)
    for k in range(NZ):
        ring = jnp.bitwise_and(z + NZ - k, NZ - 1)
        ffn, qkv = refs[k][0:16, :], refs[k][16:32, :]
        small = small + qkv[:, 3 * PAIR : 4 * PAIR].astype(F32)
        for n in range(8):
            out_ref[n, :, pl.ds(pl.multiple_of(UP + ring * HID, HID), HID)] = ffn[:, :HID]
            out_ref[n, :, pl.ds(pl.multiple_of(DOWN + ring * HID, HID), HID)] = ffn[:, HID:]
            for part in range(3):
                place = pl.ds(pl.multiple_of(QKV + part * 512 + ring * PAIR, PAIR), PAIR)
                out_ref[n, :, place] = qkv[:, part * PAIR : (part + 1) * PAIR]
    for n in range(8):
        out_ref[n, :, PROJ:QKV] = refs[0][32:48, :]
        out_ref[n, :, SMALL:WIDE] = small.astype(BF)


def pack(where, own, others):
    return pl.pallas_call(
        pack_kernel,
        grid=(1,),
        in_specs=[SM] + [VM] * 4,
        out_specs=full(8, 16, WIDE),
        out_shape=far((8, 16, WIDE), BF),
        compiler_params=params(),
        cost_estimate=cost(0),
        name="pack",
    )(where, own, *others)


def merge_kernel(where_ref, mine_ref, theirs_ref, up_ref, down_ref, proj_ref, qkv_ref, small_ref):
    core = where_ref[0]
    native = where_ref[0] == where_ref[3]
    for side, ref in ((core, mine_ref), (1 - core, theirs_ref)):
        up_ref[:, pl.ds(pl.multiple_of(side * 2048, 2048), 2048)] = ref[:, UP:DOWN]
        down_ref[:, pl.ds(pl.multiple_of(side * 2048, 2048), 2048)] = ref[:, DOWN:PROJ]
        for part in range(3):
            place = pl.multiple_of(part * D + side * 512, 512)
            qkv_ref[:, pl.ds(place, 512)] = ref[:, QKV + part * 512 : QKV + (part + 1) * 512]

    @pl.when(native)
    def _():
        proj_ref[...] = mine_ref[:, PROJ:QKV]

    @pl.when(jnp.logical_not(native))
    def _():
        proj_ref[...] = theirs_ref[:, PROJ:QKV]

    for n in range(8):
        small_ref[2 * n : 2 * n + 2, :] = mine_ref[n * 16 : (n + 1) * 16, SMALL:WIDE].astype(F32)[
            0:2
        ] + theirs_ref[n * 16 : (n + 1) * 16, SMALL:WIDE].astype(F32)[0:2]


def merge(where, mine, theirs):
    return pl.pallas_call(
        merge_kernel,
        in_specs=[SM, VM, VM],
        out_specs=[VM] * 5,
        out_shape=[
            shape((128, FF), BF),
            shape((128, FF), BF),
            shape((128, D), BF),
            shape((128, 3 * D), BF),
            shape((16, 128), F32),
        ],
        compiler_params=params(),
        cost_estimate=cost(0),
        name="merge",
    )(where, mine, theirs)


def back_kernel(dqkv_ref, w_ref, ffn_ref, norm_ref, out_ref):
    dn1 = dot(dqkv_ref[...], w_ref[...], 1, 1)
    out_ref[...] = (dn1 * norm_ref[0:1, :] + ffn_ref[...].astype(F32)).astype(BF)


def back_theirs(dqkv, w, ffn_back, norms):
    moving = lambda i: (2 + i, 0)
    fixed = lambda i: (0, 0)
    return pl.pallas_call(
        back_kernel,
        grid=(2,),
        in_specs=[
            pl.BlockSpec((2 * ROWS, 3 * PAIR), moving),
            pl.BlockSpec((D, 3 * PAIR), fixed),
            pl.BlockSpec((2 * ROWS, D), moving),
            pl.BlockSpec((4, D), fixed),
        ],
        out_specs=pl.BlockSpec((2 * ROWS, D), lambda i: (i, 0)),
        out_shape=shape((SEQ // 2, D), BF),
        compiler_params=params(),
        cost_estimate=cost(0),
        name="back_theirs",
    )(dqkv, w, keep_far(ffn_back), norms)


def back_sum_kernel(dqkv_ref, w_ref, ffn_ref, norm_ref, other_ref, *out_refs):
    step = pl.program_id(0)
    dn1 = dot(dqkv_ref[...], w_ref[...], 1, 1)
    mine = (dn1 * norm_ref[0:1, :] + ffn_ref[...].astype(F32)).astype(BF)
    total = (mine.astype(F32) + other_ref[...].astype(F32)).astype(BF)
    for n in range(2):

        @pl.when(step == n)
        def _():
            out_refs[2 * n][...] = total[0:ROWS]
            out_refs[2 * n + 1][...] = total[ROWS:]


def back_sum(dqkv, w, ffn_back, norms, other):
    moving = lambda i: (i, 0)
    fixed = lambda i: (0, 0)
    return pl.pallas_call(
        back_sum_kernel,
        grid=(2,),
        in_specs=[
            pl.BlockSpec((2 * ROWS, 3 * PAIR), moving),
            pl.BlockSpec((D, 3 * PAIR), fixed),
            pl.BlockSpec((2 * ROWS, D), moving),
            pl.BlockSpec((4, D), fixed),
            pl.BlockSpec((2 * ROWS, D), moving),
        ],
        out_specs=[pl.BlockSpec((ROWS, D), fixed)] * NZ,
        out_shape=[far((ROWS, D), BF)] * NZ,
        compiler_params=params(),
        cost_estimate=cost(0),
        name="back_sum",
    )(dqkv, w, keep_far(ffn_back), norms, other)


def qkv_grad_kernel(meta_ref, xh_ref, dqkv_ref, w_ref, norm_ref, dy_ref, ffn_vec_ref, grad_ref, vec):
    part = meta_ref[6]
    dqkv = dqkv_ref[...]
    sums = jnp.broadcast_to(jnp.sum(dqkv.astype(F32), axis=0, keepdims=True), (8, 3 * PAIR))
    dy_sum = jnp.sum(dy_ref[...].astype(F32), axis=0, keepdims=True)
    raw = dot(xh_ref[...], dqkv, 0, 0)
    gain = jnp.transpose(jnp.broadcast_to(norm_ref[0:1, :], (8, D)))[:, 0:1]
    shift = jnp.transpose(jnp.broadcast_to(norm_ref[1:2, :], (8, D)))[:, 0:1]
    grad = (raw * gain + shift * sums[0:1, :]).astype(BF)
    for h in range(NXH):
        for p in range(8):
            for ring in range(NZ):
                first = (h * NZ + ring) * 128 + p * 16
                grad_ref[h * 8 + p, ring * 16 : (ring + 1) * 16, 0 : 3 * PAIR] = grad[first : first + 16]
    product = (raw * w_ref[...].astype(F32)).astype(BF)
    norm_rows = [
        dot(jnp.ones((8, 3 * PAIR), BF), product, 1, 1)[0:1],
        dot(sums.astype(BF), w_ref[...], 1, 1)[0:1],
        ffn_vec_ref[0:1, :],
        ffn_vec_ref[8:9, :],
    ]
    vec[...] = jnp.zeros_like(vec)

    def put(bias_row, values):
        place = bias_row + (bias_row // 9) * 7
        vec[pl.ds(place, 1), :] = values

    for n in range(3):
        put(n * 8 + part, sums[0:1, n * PAIR : (n + 1) * PAIR])
    for n in range(4):
        put(32 + part * 4 + n, ffn_vec_ref[16:17, n * 128 : (n + 1) * 128])
    for n in range(8):
        put(24 + n, dy_sum[:, n * 128 : (n + 1) * 128])
        put(64 + n, dy_sum[:, n * 128 : (n + 1) * 128])
        for r in range(4):
            vec[n * 16 + 9 + r : n * 16 + 10 + r, :] = norm_rows[r][:, n * 128 : (n + 1) * 128]
    for h in range(NXH):
        for p in range(8):
            for ring in range(NZ):
                first = (h * NZ + ring) * 16 + 2 * p
                grad_ref[h * 8 + p, ring * 16 : (ring + 1) * 16, 3 * PAIR :] = jnp.concatenate(
                    [vec[first : first + 2, :], jnp.zeros((14, 128), F32)], axis=0
                ).astype(BF)


def qkv_grad(meta, xh, dqkv, w, norms, dy, ffn_vec):
    return pl.pallas_call(
        qkv_grad_kernel,
        in_specs=[SM] + [VM] * 6,
        grid=(1,),
        out_specs=full(16, 64, 4 * PAIR),
        out_shape=far((16, 64, 4 * PAIR), BF),
        scratch_shapes=[pltpu.VMEM((128, 128), F32)],
        compiler_params=params(),
        cost_estimate=cost(0),
        name="qkv_grad",
    )(meta, xh, dqkv, w, norms, dy, ffn_vec)


def body(
    tokens, out_grad, segments, w_qkv, w_proj, w_up, w_down, norm_params, biases,
    prior_moment_qkv, prior_square_qkv, prior_moment_proj, prior_square_proj,
    prior_moment_up, prior_square_up, prior_moment_down, prior_square_down,
    prior_moment_norm, prior_square_norm, prior_moment_bias, prior_square_bias,
):
    rep, shard = lax.axis_index("rep"), lax.axis_index("shard")
    core, y = rep % NC, rep // (NC * NXL)
    where = jnp.stack([core, shard % NZ, y, shard // NZ, rep // NC % NXL]).astype(jnp.int32)

    x_mine = [permute(tokens, SPREAD[k]) for k in range(NZ)]
    docs = segments.astype(BF).reshape(2, 128)
    sent = send_weights(
        where, w_qkv, w_up, w_down, norm_params, biases.reshape(9, 128), docs, sibling(docs)
    )
    received = lax.all_to_all(sent, "shard", 0, 0, tiled=True)
    w_qkv_t, norms, bias, ffn_part, meta = assemble(where, received)
    turns = rotary_tables()
    x_joined = join(x_mine)
    dy_wide, _ = lax.optimization_barrier(
        (jnp.concatenate([out_grad, w_proj.astype(BF)], axis=0), x_joined)
    )
    dy_first = permute(dy_wide, SWAP)
    half = project_qkv(meta, x_joined, w_qkv_t, bias, norms, turns, None, 100)
    x_other = sibling(x_joined)
    n2, xh, q, k, v = project_qkv(meta, x_other, w_qkv_t, bias, norms, turns, half, 0)

    ffn_part = exchange(ffn_part, ALONG_Y)
    dy_block, _ = lax.optimization_barrier((dy_first[:ROWS], x_joined))
    dy_mine = around(dy_block)

    ctx, ctxt, stat = attn_forward(meta, q, k, v)
    ctx, dy_mine = lax.optimization_barrier((ctx, dy_mine))
    dy_joined = join(dy_mine)
    dy_joined, ffn_part = lax.optimization_barrier((dy_joined, ffn_part))
    w_up_t, w_down_t = assemble_ffn(ffn_part)
    dy_other = sibling(dy_joined)
    out_mine, out_theirs, ffn_back, dctx, ffn_vec, ffn_sent = feed_forward(
        meta, dy_joined, dy_other, n2, xh, ctx, w_up_t, w_down_t, dy_first, bias, norms
    )
    out_other = sibling(out_theirs)

    prepared = attn_prepare(q, k, dctx, ctxt, stat)
    dqkv = attn_backward(meta, k, v, stat, turns, prepared)
    qkv_sent = qkv_grad(meta, xh, dqkv, w_qkv_t, norms, out_grad, ffn_vec)
    out_pieces = back_around(core_sum(out_mine, out_other))
    out_sum = fold(out_pieces)
    dqkv, qkv_sent, out_sum, ffn_received = lax.optimization_barrier(
        (dqkv, qkv_sent, out_sum, exchange(ffn_sent, ALONG_Y))
    )

    ffn_parts = reduce_y(where, ffn_received)
    ffn_parts = [ffn_parts[0]] + [permute(ffn_parts[k], ROUND_X[k]) for k in (1, 2, 3)]
    qkv_received = exchange(qkv_sent, PLANE)
    dqkv, ffn_parts, qkv_received = lax.optimization_barrier((dqkv, ffn_parts, qkv_received))
    ffn_own, *ffn_others = reduce_x(where, ffn_parts, qkv_received)
    dqkv, ffn_own = lax.optimization_barrier((dqkv, ffn_own))
    w_theirs = back_theirs(dqkv, w_qkv_t, ffn_back, norms)
    block_out = finish_out(tokens, bias, permute(out_sum, SWAP))
    w_pieces = back_sum(dqkv, w_qkv_t, ffn_back, norms, sibling(w_theirs))
    ffn_others = [permute(b, ROUND_Z[k + 1]) for k, b in enumerate(ffn_others)]
    ffn_own, block_out, w_pieces = lax.optimization_barrier((ffn_own, block_out, w_pieces))
    mine_grad = exchange(pack(where, ffn_own, ffn_others), COPIES)
    mine_grad, w_sum = lax.optimization_barrier((mine_grad, fold(back_around(w_pieces))))
    mine_grad = mine_grad.reshape(128, WIDE)
    their_grad = sibling(mine_grad)
    g_up, g_down, g_proj, g_qkv, small = merge(where, mine_grad, their_grad)
    w_sum = permute(w_sum, SWAP)
    g_norm = small[9:13]
    g_bias = small[:9].reshape(1152)

    def matrix_step(weight, moment, square, grad):
        return adam_step(weight, moment, square, grad.astype(F32), RATE_MATRIX, DECAY)

    new_qkv = matrix_step(w_qkv, prior_moment_qkv, prior_square_qkv, g_qkv)
    new_proj = matrix_step(w_proj, prior_moment_proj, prior_square_proj, g_proj)
    new_up = matrix_step(w_up, prior_moment_up, prior_square_up, g_up)
    new_down = matrix_step(w_down, prior_moment_down, prior_square_down, g_down)
    w_sum, new_qkv = lax.optimization_barrier((w_sum, new_qkv))
    grad_tokens = finish_grad(tokens, out_grad, w_sum)
    new_norm = adam_step(norm_params, prior_moment_norm, prior_square_norm, g_norm, RATE_VECTOR, 0.0)
    new_bias = adam_step(biases, prior_moment_bias, prior_square_bias, g_bias, RATE_VECTOR, 0.0)
    return (block_out, grad_tokens, *new_qkv, *new_proj, *new_up, *new_down, *new_norm, *new_bias)


def solution(mesh):
    token = P(("rep", "shard"), None)
    row = P("shard", None)
    norm = P(None, "shard")
    flat = P("shard")
    in_specs = (
        (token, token, P(("rep", "shard")))
        + (row,) * 4
        + (norm, flat)
        + (row,) * 8
        + (norm, norm, flat, flat)
    )
    out_specs = (token, token) + (row,) * 12 + (norm,) * 3 + (flat,) * 3
    return jax.shard_map(body, mesh=mesh, in_specs=in_specs, out_specs=out_specs, check_vma=False)
```

```python
import functools

import jax
import jax.numpy as jnp
import numpy as np
from jax import lax
from jax.experimental import pallas as pl
from jax.experimental.pallas import tpu as pltpu
from jax.sharding import PartitionSpec as P

HEAD_DIM = 64
ROT = 16
STEP = 10
EPS_NORM = 1e-05
BETA_ONE = 0.9
BETA_TWO = 0.95
RATE_MATRIX = 0.05
RATE_VECTOR = 0.3
DECAY = 0.01
ADAM_EPS = 1e-08
NEGATIVE = -1e30

NY, NXL, NC, NXH, NZ = 4, 2, 2, 2, 4
AXES = ("rep", "shard")
D = 1024
ROWS = 256
SEQ = 2048
FF = 4096
PAIR = 128
HID = 512
QB = 512
BF = jnp.bfloat16
F32 = jnp.float32


def device_pairs(move):
    pairs = []
    for y in range(NY):
        for xl in range(NXL):
            for c in range(NC):
                for h in range(NXH):
                    for z in range(NZ):
                        ty, txl, tc, th, tz = move(y, xl, c, h, z)
                        pairs.append(
                            (
                                ((y * NXL + xl) * NC + c) * 8 + h * NZ + z,
                                ((ty * NXL + txl) * NC + tc) * 8 + th * NZ + tz % NZ,
                            )
                        )
    return pairs


SWAP = device_pairs(lambda y, xl, c, h, z: (y, xl, h, c, z))


SIBLING = device_pairs(lambda y, xl, c, h, z: (y, xl, 1 - c, h, z))
ROUND_X = [
    device_pairs(
        lambda y, xl, c, h, z, k=k: (y, (h * 2 + xl + k) % 4 % 2, c, (h * 2 + xl + k) % 4 // 2, z)
    )
    for k in range(4)
]
ROUND_Z = [device_pairs(lambda y, xl, c, h, z, k=k: (y, xl, c, h, z + k)) for k in range(NZ)]


def device(y, xl, c, h, z):
    return ((y * NXL + xl) * NC + c) * 8 + h * NZ + z


RANGES = dict(y=range(NY), xl=range(NXL), c=range(NC), h=range(NXH), z=range(NZ))


def groups(*inner):
    outer = [name for name in RANGES if name not in inner]

    def walk(names, at):
        if not names:
            return [device(**at)]
        return [d for n in RANGES[names[0]] for d in walk(names[1:], dict(at, **{names[0]: n}))]

    def each(names, at):
        if not names:
            return [walk(inner, at)]
        return [g for n in RANGES[names[0]] for g in each(names[1:], dict(at, **{names[0]: n}))]

    return each(outer, {})


ALONG_Y = groups("y")
ALONG_Z = groups("z")
PLANE = groups("h", "y", "xl")
COPIES = groups("y", "xl")


SPREAD = [device_pairs(lambda y, xl, c, h, z, k=k: (y, xl, h, c, z + k)) for k in range(NZ)]


def permute(values, pairs):
    return lax.ppermute(values, AXES, pairs)


def around(block):
    return [block] + [permute(block, ROUND_Z[k]) for k in (1, 2, 3)]


def back_around(blocks):
    return [blocks[0]] + [permute(blocks[k], ROUND_Z[NZ - k]) for k in (1, 2, 3)]


def sibling(values):
    return lax.ppermute(values, AXES, SIBLING)


def exchange(values, members):
    return lax.all_to_all(values, AXES, 0, 0, axis_index_groups=members, tiled=True)


def dot(a, b, ca, cb):
    return lax.dot_general(a, b, (((ca,), (cb,)), ((), ())), preferred_element_type=F32)


def gelu_parts(values):
    cdf = 0.5 * (1.0 + lax.erf(values * np.float32(np.sqrt(0.5))))
    density = jnp.exp(-0.5 * values * values) * np.float32(1.0 / np.sqrt(2.0 * np.pi))
    return values * cdf, cdf + values * density


def adam_step(weight, moment, square, gradient, rate, decay):
    moment_new = BETA_ONE * moment + (1.0 - BETA_ONE) * gradient
    square_new = BETA_TWO * square + (1.0 - BETA_TWO) * gradient * gradient
    fixed_moment = moment_new / (1.0 - BETA_ONE**STEP)
    fixed_square = square_new / (1.0 - BETA_TWO**STEP)
    weight_new = weight - rate * (
        fixed_moment / (jnp.sqrt(fixed_square) + ADAM_EPS) + decay * weight
    )
    return (weight_new, moment_new, square_new)


SM = pl.BlockSpec(memory_space=pltpu.SMEM)
VM = pl.BlockSpec(memory_space=pltpu.VMEM)


def full(*dims):
    return pl.BlockSpec(dims, lambda i: (0,) * len(dims))


WHOLE = pl.BlockSpec((SEQ, PAIR), lambda i: (0, 0))


def params(mib=16):
    return pltpu.CompilerParams(vmem_limit_bytes=mib * 2**20)


def cost(us):
    flops = int(us * 7e8)
    return pl.CostEstimate(flops=flops, bytes_accessed=int(us * 2e6), transcendentals=0)


def shape(dims, kind):
    return jax.ShapeDtypeStruct(dims, kind)


def far(dims, kind):
    return pltpu.HBM(dims, kind)


def keep_far(values):
    return pltpu.with_memory_space_constraint(values, pltpu.HBM)


def send_weights_kernel(
    where_ref, q_ref, k_ref, v_ref, up_ref, down_ref, norm_ref, bias_ref, seg_ref, sib_ref, out_ref
):
    misc = jnp.concatenate(
        [norm_ref[...], bias_ref[...], seg_ref[...].astype(F32), jnp.zeros((1, 128), F32)], axis=0
    ).astype(BF)
    theirs = jnp.concatenate([sib_ref[...].astype(F32), jnp.zeros((14, 128), F32)], axis=0).astype(BF)
    for n in range(8):
        for part, ref in enumerate((q_ref, k_ref, v_ref)):
            source = slice((n % NZ) * PAIR, (n % NZ + 1) * PAIR)
            out_ref[n, 0:128, part * PAIR : (part + 1) * PAIR] = ref[:, source].astype(BF)
        out_ref[n, 128:144, 0:128] = misc
        out_ref[n, 128:144, 128:256] = theirs
        out_ref[n, 128:144, 256:384] = jnp.zeros((16, 128), BF)
        for j in range(8):
            ref = (up_ref, down_ref)[j // 4]
            source = (n % NZ) * HID + (j % 4) * 128
            first = 144 + (j // 3) * 32
            out_ref[n, first : first + 32, (j % 3) * 128 : (j % 3 + 1) * 128] = ref[
                :, source : source + 128
            ].astype(BF)
        out_ref[n, 208:240, 256:384] = jnp.zeros((32, 128), BF)


def send_weights(where, w, up, down, norms, biases, segments, sibling_segments):
    third = lambda part: pl.BlockSpec((128, 512), lambda i, where: (0, part * 2 + where[0]))
    rows = pl.BlockSpec((32, 2048), lambda i, where: (where[2], where[0]))
    small = lambda count: pl.BlockSpec((count, 128), lambda i, where: (0, 0))
    return pl.pallas_call(
        send_weights_kernel,
        grid_spec=pltpu.PrefetchScalarGridSpec(
            num_scalar_prefetch=1,
            grid=(1,),
            in_specs=[third(0), third(1), third(2), rows, rows] + [small(4), small(9), small(2), small(2)],
            out_specs=pl.BlockSpec((8, 240, 384), lambda i, where: (0, 0, 0)),
        ),
        out_shape=far((8, 240, 384), BF),
        compiler_params=params(),
        cost_estimate=cost(0),
        name="send_weights",
    )(
        where, *[keep_far(w)] * 3, keep_far(up), keep_far(down),
        keep_far(norms), biases, segments, sibling_segments,
    )


def join_kernel(*refs):
    for k in range(NZ):
        refs[NZ][k * ROWS : (k + 1) * ROWS, :] = refs[k][...]


def join(blocks):
    return pl.pallas_call(
        join_kernel,
        in_specs=[VM] * NZ,
        out_specs=VM,
        out_shape=shape((SEQ // 2, D), BF),
        compiler_params=params(),
        cost_estimate=cost(0),
        name="join",
    )(*blocks)


def doc_start(ids, meta_ref):
    start = jnp.zeros_like(ids)
    for d in range(4):
        start = jnp.where(ids >= meta_ref[d], meta_ref[d], start)
    return start


def block_tables(where_ref, meta_ref):
    c, z = where_ref[0], where_ref[1]
    meta_ref[4] = c
    meta_ref[5] = z
    meta_ref[6] = c * NZ + z
    meta_ref[7] = where_ref[2]
    for j in range(2):
        half = c if j == 0 else 1 - c
        for k in range(NZ):
            meta_ref[8 + j * NZ + k] = half * NZ + jnp.bitwise_and(z + NZ - k, NZ - 1)
    for half in range(2):
        base = jnp.bitwise_xor(c, half) * NZ
        for ring in range(NZ):
            meta_ref[16 + half * NZ + ring] = base + jnp.bitwise_and(z + NZ - ring, NZ - 1)


def assemble_kernel(
    where_ref, in_ref, w_ref, norm_ref, bias_ref, ffn_ref, meta_ref
):
    block_tables(where_ref, meta_ref)
    counts = [jnp.zeros((1, 128), F32) for _ in range(4)]
    native = (where_ref[0] == where_ref[3]).astype(F32)
    for n in range(8):
        w_ref[n * 128 : (n + 1) * 128, :] = in_ref[n, 0:128, :]
        misc = in_ref[n, 128:144, 0:128].astype(F32)
        other = in_ref[n, 128:144, 128:256].astype(F32)
        norm_ref[:, n * 128 : (n + 1) * 128] = misc[0:4]
        bias_ref[n * 9 : (n + 1) * 9, :] = misc[4:13]
        docs = misc[13:15] * native + other[0:2] * (1.0 - native)
        for d in range(4):
            below = jnp.where(docs < d + 0.5, 1.0, 0.0)
            counts[d] = counts[d] + below[0:1] + below[1:2]
        for j in range(8):
            first = 144 + (j // 3) * 32
            block = in_ref[n, first : first + 32, (j % 3) * 128 : (j % 3 + 1) * 128]
            for y in range(NY):
                ffn_ref[y, n * 32 : (n + 1) * 32, j * 128 : (j + 1) * 128] = block
    for d in range(4):
        meta_ref[d] = jnp.sum(counts[d]).astype(jnp.int32)


def rotary_tables():
    lane = np.arange(PAIR) % HEAD_DIM
    freq = 10000.0 ** (-2.0 * (lane % (ROT // 2)) / ROT)
    angles = np.arange(SEQ)[:, None] * np.where(lane < ROT, freq, 0.0)[None, :]
    return jnp.asarray(np.where(np.arange(PAIR) < HEAD_DIM, np.cos(angles), np.sin(angles)), F32)


def both_heads(table):
    first = lax.broadcasted_iota(jnp.int32, table.shape, 1) < HEAD_DIM
    other = pltpu.roll(table, HEAD_DIM, 1)
    return jnp.where(first, table, other), jnp.where(first, other, table)


def assemble(where, received):
    return pl.pallas_call(
        assemble_kernel,
        grid=(1,),
        in_specs=[SM, VM],
        out_specs=[VM] * 3 + [pl.BlockSpec((NY, ROWS, 2 * HID), lambda i: (0, 0, 0)), SM],
        out_shape=[
            shape((D, 3 * PAIR), BF),
            shape((4, D), F32),
            shape((72, 128), F32),
            far((NY, ROWS, 2 * HID), BF),
            shape((24,), jnp.int32),
        ],
        compiler_params=params(),
        cost_estimate=cost(0),
        name="assemble",
    )(where, received)


def assemble_ffn_kernel(in_ref, up_ref, down_ref):
    for y in range(NY):
        for n in range(8):
            rows = slice(n * 128 + y * 32, n * 128 + (y + 1) * 32)
            up_ref[rows, :] = in_ref[y, n * 32 : (n + 1) * 32, 0:HID]
            down_ref[rows, :] = in_ref[y, n * 32 : (n + 1) * 32, HID:]


def assemble_ffn(parts):
    return pl.pallas_call(
        assemble_ffn_kernel,
        in_specs=[VM],
        out_specs=[VM] * 2,
        out_shape=[shape((D, HID), BF)] * 2,
        compiler_params=params(),
        cost_estimate=cost(0),
        name="assemble_ffn",
    )(parts)


def turn(u, cosine, sine):
    lane = lax.broadcasted_iota(jnp.int32, u.shape, 1) % HEAD_DIM
    left = pltpu.roll(u, PAIR - ROT // 2, 1)
    right = pltpu.roll(u, ROT // 2, 1)
    return u * cosine + jnp.where(lane < ROT // 2, -left, right) * sine


def qkv_kernel(meta_ref, x_ref, w_ref, bias_ref, norm_ref, turn_ref, *refs):
    n2_ref, xh_ref, q_ref, k_ref, v_ref = refs[-5:]
    x = x_ref[...].astype(F32)
    centred = x - jnp.mean(x, axis=-1, keepdims=True)
    variance = jnp.mean(centred * centred, axis=-1, keepdims=True)
    xh = centred * lax.rsqrt(variance + EPS_NORM)
    n1 = (xh * norm_ref[0:1, :] + norm_ref[1:2, :]).astype(BF)
    xh_ref[...] = xh.astype(BF)
    n2_ref[...] = (xh * norm_ref[2:3, :] + norm_ref[3:4, :]).astype(BF)
    part = meta_ref[6]
    cosine, sine = both_heads(turn_ref[...])
    qkv = dot(n1, w_ref[...], 1, 0)
    q = qkv[:, 0:PAIR] + bias_ref[pl.ds(part, 1), :]
    k = qkv[:, PAIR : 2 * PAIR] + bias_ref[pl.ds(8 + part, 1), :]
    v = qkv[:, 2 * PAIR :] + bias_ref[pl.ds(16 + part, 1), :]
    q_ref[...] = (turn(q, cosine, sine).astype(BF) * 0.125).astype(BF)
    k_ref[...] = turn(k, cosine, sine).astype(BF)
    v_ref[...] = v.astype(BF)


def project_qkv(meta, x, w, bias, norms, turns, before, us):
    base = 0 if before is None else NZ
    moving = lambda i, meta: (i, 0)
    physical = lambda i, meta: (base + i, 0)
    logical = lambda i, meta: (meta[8 + base + i], 0)
    fixed = lambda i, meta: (0, 0)
    extra = [] if before is None else list(before)
    return pl.pallas_call(
        qkv_kernel,
        grid_spec=pltpu.PrefetchScalarGridSpec(
            num_scalar_prefetch=1,
            grid=(NZ,),
            in_specs=[
                pl.BlockSpec((ROWS, D), moving),
                pl.BlockSpec((D, 3 * PAIR), fixed),
                pl.BlockSpec((72, 128), fixed),
                pl.BlockSpec((4, D), fixed),
                pl.BlockSpec((ROWS, PAIR), logical),
            ]
            + [pl.BlockSpec(memory_space=pl.ANY)] * len(extra),
            out_specs=[pl.BlockSpec((ROWS, D), physical)] * 2
            + [pl.BlockSpec((ROWS, PAIR), logical)] * 3,
        ),
        out_shape=[far((SEQ, D), BF)] * 2 + [far((SEQ, PAIR), BF)] * 3,
        input_output_aliases={6 + n: n for n in range(len(extra))},
        compiler_params=params(),
        cost_estimate=cost(us),
        name="project_qkv",
    )(meta, x, w, bias, norms, keep_far(turns), *extra)


def head_only(values, h):
    lane = lax.broadcasted_iota(jnp.int32, values.shape, 1)
    return jnp.where((lane // HEAD_DIM) == h, values, jnp.zeros_like(values))


def keep_allowed(meta_ref, i, j, values, other):
    keys = j * QB + lax.broadcasted_iota(jnp.int32, (QB, QB), 0)
    queries = i * QB + lax.broadcasted_iota(jnp.int32, (1, QB), 1)
    allowed = None
    if i == j:
        allowed = keys <= queries
    if j == 0 or i == SEQ // QB - 1:
        same = keys >= doc_start(queries, meta_ref)
        allowed = same if allowed is None else allowed & same
    return values if allowed is None else jnp.where(allowed, values, other)


def attn_forward_kernel(meta_ref, q_ref, k_ref, v_ref, ctx_ref, ctxt_ref, stat_ref, vt_ref):
    for b in range(SEQ // QB):
        vt_ref[:, b * QB : (b + 1) * QB] = v_ref[b * QB : (b + 1) * QB, :].T
    for i in range(SEQ // QB):
        here = slice(i * QB, (i + 1) * QB)
        parts = []
        for h in range(2):
            q = head_only(q_ref[here, :], h)
            m = l = acc = None
            for j in range(i + 1):
                there = slice(j * QB, (j + 1) * QB)
                scores = keep_allowed(meta_ref, i, j, dot(k_ref[there, :], q, 1, 1), NEGATIVE)
                top = jnp.max(scores, axis=0, keepdims=True)
                if j > 0:
                    top = jnp.maximum(m, top)
                expo = jnp.exp(scores - top)
                total = jnp.sum(expo, axis=0, keepdims=True)
                values = vt_ref[h * HEAD_DIM : (h + 1) * HEAD_DIM, there]
                add = dot(values, expo.astype(BF), 1, 0)
                if j > 0:
                    fade = jnp.exp(m - top)
                    total, add = l * fade + total, acc * fade + add
                m, l, acc = top, total, add
            parts.append(acc / l)
            stat_ref[h : h + 1, here] = m
            stat_ref[2 + h : 3 + h, here] = 1.0 / l
        ctxt = jnp.concatenate(parts, axis=0)
        ctxt_ref[:, here] = ctxt
        low = ctxt.astype(BF).T
        for b in range(QB // ROWS):
            row = pl.multiple_of(meta_ref[16 + i * (QB // ROWS) + b] * ROWS, ROWS)
            ctx_ref[pl.ds(row, ROWS), :] = low[b * ROWS : (b + 1) * ROWS]


def attn_forward(meta, q, k, v):
    return pl.pallas_call(
        attn_forward_kernel,
        grid=(1,),
        in_specs=[SM, WHOLE, WHOLE, WHOLE],
        out_specs=[WHOLE, pl.BlockSpec((PAIR, SEQ), lambda i: (0, 0)), VM],
        out_shape=[far((SEQ, PAIR), BF), far((PAIR, SEQ), F32), shape((8, SEQ), F32)],
        scratch_shapes=[pltpu.VMEM((PAIR, SEQ), BF)],
        compiler_params=params(),
        cost_estimate=cost(0),
        name="attn_forward",
    )(meta, keep_far(q), keep_far(k), keep_far(v))


def attn_backward_kernel(
    meta_ref, q_ref, k_ref, v_ref, dctx_ref, ctxt_ref, stat_ref, turn_ref,
    out_ref,
    dqt_ref, kt_ref, du_ref, dut_ref, qh_ref, c_ref,
):
    blocks = SEQ // QB
    for b in range(blocks):
        here = slice(b * QB, (b + 1) * QB)
        kt_ref[:, here] = k_ref[here, :].T
        dctxt = dctx_ref[here, :].T
        prod = dctxt * ctxt_ref[:, here]
        for h in range(2):
            rows = slice(h * HEAD_DIM, (h + 1) * HEAD_DIM)
            inverse = stat_ref[2 + h : 3 + h, here]
            c_ref[h : h + 1, here] = jnp.sum(prod[rows], axis=0, keepdims=True) * inverse
            dut = (dctxt[rows] * inverse).astype(BF)
            zero = jnp.zeros_like(dut)
            whole = jnp.concatenate([dut, zero] if h == 0 else [zero, dut], axis=0)
            dut_ref[h, :, here] = whole
            du_ref[h, here, :] = whole.T
            qh_ref[h, here, :] = head_only(q_ref[here, :], h)


    def put(b, lanes, values):
        for n in range(QB // ROWS):
            place = pl.multiple_of(meta_ref[16 + b * (QB // ROWS) + n] * ROWS, ROWS)
            out_ref[pl.ds(place, ROWS), lanes] = values[n * ROWS : (n + 1) * ROWS].astype(BF)

    for j in range(blocks):
        there = slice(j * QB, (j + 1) * QB)
        keys, values = k_ref[there, :], v_ref[there, :]
        dk = dv = None
        for i in range(j, blocks):
            here = slice(i * QB, (i + 1) * QB)
            for h in range(2):
                qh = qh_ref[h, here, :]
                scores = dot(keys, qh, 1, 1)
                expo = jnp.exp(scores - stat_ref[h : h + 1, here])
                expo = keep_allowed(meta_ref, i, j, expo, 0.0)
                dexpo = dot(values, dut_ref[h, :, here], 1, 0)
                dscore = (expo * (dexpo - c_ref[h : h + 1, here])).astype(BF)
                dv_add = dot(expo.astype(BF), du_ref[h, here, :], 1, 0)
                dk_add = dot(dscore, qh, 1, 0)
                dk = dk_add if dk is None else dk + dk_add
                dv = dv_add if dv is None else dv + dv_add
                rows = slice(h * HEAD_DIM, (h + 1) * HEAD_DIM)
                dq_add = dot(kt_ref[rows, there], dscore, 1, 0)
                dqt_ref[rows, here] = dq_add if j == 0 else dqt_ref[rows, here] + dq_add
        cosine, sine = both_heads(turn_ref[there, :])
        dq = (dqt_ref[:, there] * 0.125).T
        put(j, slice(0, PAIR), turn(dq, cosine, -sine))
        put(j, slice(PAIR, 2 * PAIR), turn(dk, cosine, -sine))
        put(j, slice(2 * PAIR, 3 * PAIR), dv)


def attn_backward(meta, q, k, v, dctx, ctxt, stat, turns):
    return pl.pallas_call(
        attn_backward_kernel,
        grid=(1,),
        in_specs=[SM] + [WHOLE] * 4 + [full(PAIR, SEQ), VM, WHOLE],
        out_specs=VM,
        out_shape=shape((SEQ, 3 * PAIR), BF),
        scratch_shapes=[
            pltpu.VMEM((PAIR, SEQ), F32),
            pltpu.VMEM((PAIR, SEQ), BF),
            pltpu.VMEM((2, SEQ, PAIR), BF),
            pltpu.VMEM((2, PAIR, SEQ), BF),
            pltpu.VMEM((2, SEQ, PAIR), BF),
            pltpu.VMEM((8, SEQ), F32),
        ],
        compiler_params=params(28),
        cost_estimate=cost(100),
        name="attn_backward",
    )(meta, *[keep_far(n) for n in (q, k, v, dctx, ctxt)], stat, keep_far(turns))


def lay_rows(ref, first, count):
    return jnp.concatenate([ref[pl.ds(first + r, 1), :] for r in range(count)], axis=1)


def by_half(double):
    return [
        pl.BlockSpec((double, D), lambda i, meta: (jnp.minimum(i, 1), 0)),
        pl.BlockSpec((double, D), lambda i, meta: (jnp.maximum(i - 2, 0), 0)),
    ]


def take_half(step, mine_ref, theirs_ref, now_ref):
    @pl.when(step < 2)
    def _():
        now_ref[...] = mine_ref[...]

    @pl.when(step >= 2)
    def _():
        now_ref[...] = theirs_ref[...]


def ffn_kernel(meta_ref, *refs):
    mine_ref, theirs_ref = refs[:2]
    n2_ref, xh_ref, ctx_ref, up_ref, down_ref, proj_ref, bias_ref, norm_ref = refs[2:10]
    out_mine_ref, out_theirs_ref, back_ref, dctx_ref, vec_ref, grad_ref = refs[10:16]
    dy_now, gup, gdown, gproj, total = refs[16:]
    step = pl.program_id(0)
    part = meta_ref[6]

    @pl.when(step == 0)
    def _():
        gup[...] = jnp.zeros_like(gup)
        gdown[...] = jnp.zeros_like(gdown)
        gproj[...] = jnp.zeros_like(gproj)
        total[...] = jnp.zeros_like(total)

    take_half(step, mine_ref, theirs_ref, dy_now)
    dy = dy_now[...]
    ctx = ctx_ref[...]
    dctx = dot(dy, proj_ref[...], 1, 1)
    for b in range(2):
        row = pl.multiple_of(meta_ref[8 + 2 * step + b] * ROWS, ROWS)
        dctx_ref[pl.ds(row, ROWS), :] = dctx[b * ROWS : (b + 1) * ROWS]
    gproj[...] += dot(ctx, dy, 0, 0)
    bias_up = lay_rows(bias_ref, 32 + 4 * part, 4)
    pre = dot(n2_ref[...], up_ref[...], 1, 0) + bias_up
    hidden, slope = gelu_parts(pre)
    hidden = hidden.astype(BF)
    dpre = (dot(dy, down_ref[...], 1, 0) * slope).astype(BF)
    out = (dot(ctx, proj_ref[...], 1, 0) + dot(hidden, down_ref[...], 1, 1)).astype(BF)

    @pl.when(step < 2)
    def _():
        out_mine_ref[...] = out

    @pl.when(step >= 2)
    def _():
        out_theirs_ref[...] = out

    back_ref[...] = (dot(dpre, up_ref[...], 1, 1) * norm_ref[2:3, :]).astype(BF)
    gdown[...] += dot(dy, hidden, 0, 0)
    gup[...] += dot(xh_ref[...], dpre, 0, 0)
    total[...] += jnp.broadcast_to(jnp.sum(dpre.astype(F32), axis=0, keepdims=True), total.shape)

    @pl.when(step == 3)
    def _():
        sums = total[...]
        raw = gup[...]
        gain = jnp.transpose(jnp.broadcast_to(norm_ref[2:3, :], (8, D)))[:, 0:1]
        shift = jnp.transpose(jnp.broadcast_to(norm_ref[3:4, :], (8, D)))[:, 0:1]
        product = (raw * up_ref[...].astype(F32)).astype(BF)
        gup[...] = raw * gain + shift * sums[0:1, :]
        for y in range(NY):
            for n in range(8):
                here = slice(n * 32, (n + 1) * 32)
                rows = slice(n * 128 + y * 32, n * 128 + (y + 1) * 32)
                grad_ref[y, here, 0:HID] = gup[rows, :].astype(BF)
                grad_ref[y, here, HID:] = gdown[rows, :].astype(BF)
            grad_ref[y, 256:288, :] = gproj[y * 32 : (y + 1) * 32, :].astype(BF)
        vec_ref[0:8, :] = dot(jnp.ones((8, HID), BF), product, 1, 1)
        vec_ref[8:16, :] = dot(sums.astype(BF), up_ref[...], 1, 1)
        vec_ref[16:24, 0:HID] = sums
        vec_ref[16:24, HID:] = jnp.zeros((8, D - HID), F32)


def feed_forward(meta, mine, theirs, n2, xh, ctx, up, down, proj, bias, norms):
    double = 2 * ROWS
    moving = lambda i, meta: (i, 0)
    fixed = lambda i, meta: (0, 0)
    once = pl.Buffered(1)
    return pl.pallas_call(
        ffn_kernel,
        grid_spec=pltpu.PrefetchScalarGridSpec(
            num_scalar_prefetch=1,
            grid=(4,),
            in_specs=by_half(double)
            + [
                pl.BlockSpec((double, D), moving),
                pl.BlockSpec((double, D), moving),
                pl.BlockSpec((double, PAIR), moving),
                pl.BlockSpec((D, HID), fixed, pipeline_mode=once),
                pl.BlockSpec((D, HID), fixed, pipeline_mode=once),
                pl.BlockSpec((PAIR, D), lambda i, meta: (2, 0), pipeline_mode=once),
                pl.BlockSpec((72, 128), fixed, pipeline_mode=once),
                pl.BlockSpec((4, D), fixed, pipeline_mode=once),
            ],
            out_specs=by_half(double)
            + [
                pl.BlockSpec((double, D), moving),
                pl.BlockSpec((SEQ, PAIR), fixed),
                VM,
                pl.BlockSpec((NY, 288, D), lambda i, meta: (0, 0, 0)),
            ],
            scratch_shapes=[
                pltpu.VMEM((double, D), BF),
                pltpu.VMEM((D, HID), F32),
                pltpu.VMEM((D, HID), F32),
                pltpu.VMEM((PAIR, D), F32),
                pltpu.VMEM((8, HID), F32),
            ],
        ),
        out_shape=[
            far((SEQ // 2, D), BF),
            far((SEQ // 2, D), BF),
            far((SEQ, D), BF),
            far((SEQ, PAIR), F32),
            shape((24, D), F32),
            far((NY, 288, D), BF),
        ],
        compiler_params=params(40),
        cost_estimate=cost(60),
        name="feed_forward",
    )(meta, mine, theirs, keep_far(n2), keep_far(xh), keep_far(ctx), up, down, proj, bias, norms)


def core_sum_kernel(mine_ref, theirs_ref, *sent_refs):
    step = pl.program_id(0)
    total = (mine_ref[...].astype(F32) + theirs_ref[...].astype(F32)).astype(BF)
    for k in range(NZ):

        @pl.when(step == k)
        def _():
            sent_refs[k][...] = total


def core_sum(mine, theirs):
    moving = lambda i: (i, 0)
    return pl.pallas_call(
        core_sum_kernel,
        grid=(NZ,),
        in_specs=[pl.BlockSpec((ROWS, D), moving)] * 2,
        out_specs=[pl.BlockSpec((ROWS, D), lambda i: (0, 0))] * NZ,
        out_shape=[shape((ROWS, D), BF)] * NZ,
        compiler_params=params(),
        cost_estimate=cost(0),
        name="core_sum",
    )(mine, theirs)


def fold_kernel(*refs):
    total = refs[0][...].astype(F32)
    for k in range(1, NZ):
        total = total + refs[k][...].astype(F32)
    refs[NZ][...] = total.astype(BF)


def fold(pieces):
    return pl.pallas_call(
        fold_kernel,
        in_specs=[VM] * NZ,
        out_specs=VM,
        out_shape=shape((ROWS, D), BF),
        compiler_params=params(),
        cost_estimate=cost(0),
        name="fold",
    )(*pieces)


def finish_out_kernel(x_ref, bias_ref, sum_ref, out_ref):
    bias = lay_rows(bias_ref, 24, 8) + lay_rows(bias_ref, 64, 8)
    out_ref[...] = (x_ref[...].astype(F32) + sum_ref[...].astype(F32) + bias).astype(BF)


def finish_out(x, bias, total):
    half = pl.BlockSpec((ROWS // 2, D), lambda i: (i, 0))
    return pl.pallas_call(
        finish_out_kernel,
        grid=(2,),
        in_specs=[half, pl.BlockSpec((72, 128), lambda i: (0, 0)), half],
        out_specs=half,
        out_shape=shape((ROWS, D), BF),
        compiler_params=params(),
        cost_estimate=cost(0),
        name="finish_out",
    )(keep_far(x), bias, total)


def finish_grad_kernel(x_ref, dy_ref, sum_ref, out_ref):
    w = sum_ref[...].astype(F32)
    x = x_ref[...].astype(F32)
    centred = x - jnp.mean(x, axis=-1, keepdims=True)
    rstd = lax.rsqrt(jnp.mean(centred * centred, axis=-1, keepdims=True) + EPS_NORM)
    xh = centred * rstd
    inner = w - jnp.mean(w, axis=-1, keepdims=True) - xh * jnp.mean(w * xh, axis=-1, keepdims=True)
    out_ref[...] = dy_ref[...].astype(F32) + rstd * inner


def finish_grad(x, dy, total):
    half = pl.BlockSpec((ROWS // 2, D), lambda i: (i, 0))
    return pl.pallas_call(
        finish_grad_kernel,
        grid=(2,),
        in_specs=[half] * 3,
        out_specs=half,
        out_shape=shape((ROWS, D), F32),
        compiler_params=params(),
        cost_estimate=cost(0),
        name="finish_grad",
    )(keep_far(x), keep_far(dy), total)


def reduce_y_kernel(where_ref, ffn_ref, *refs):
    low_ref = refs[4]
    total = ffn_ref[0].astype(F32)
    for n in range(1, NY):
        total = total + ffn_ref[n].astype(F32)
    low_ref[...] = total.astype(BF)
    x = where_ref[3] * NXL + where_ref[4]
    for k in range(4):
        target = jnp.bitwise_and(x + k, 3)
        half, low_x = target // 2, jnp.bitwise_and(target, 1)
        for ring in range(NZ):
            rows = pl.ds(pl.multiple_of((half * NZ + ring) * 32 + low_x * 16, 16), 16)
            refs[k][ring * 16 : (ring + 1) * 16, :] = low_ref[rows, :]
        refs[k][64:80, :] = low_ref[pl.ds(pl.multiple_of(256 + low_x * 16, 16), 16), :]


def reduce_y(where, ffn):
    return pl.pallas_call(
        reduce_y_kernel,
        grid=(1,),
        in_specs=[SM, full(NY, 288, D)],
        out_specs=[VM] * 4,
        out_shape=[shape((80, D), BF)] * 4,
        scratch_shapes=[pltpu.VMEM((288, D), BF)],
        compiler_params=params(),
        cost_estimate=cost(0),
        name="reduce_y",
    )(where, keep_far(ffn))


def reduce_x_kernel(where_ref, *refs):
    ffn_refs, qkv_ref, own_ref, sent_refs = refs[:4], refs[4], refs[5], refs[6:9]
    low_ref, low_qkv_ref = refs[9:]
    z = where_ref[1]
    total, total_qkv = ffn_refs[0][...].astype(F32), qkv_ref[0].astype(F32)
    for n in range(1, 4):
        total = total + ffn_refs[n][...].astype(F32)
    for n in range(1, 16):
        total_qkv = total_qkv + qkv_ref[n].astype(F32)
    low_ref[...] = total.astype(BF)
    low_qkv_ref[...] = total_qkv.astype(BF)
    for k in range(NZ):
        out_ref = own_ref if k == 0 else sent_refs[k - 1]
        rows = pl.ds(pl.multiple_of(jnp.bitwise_and(z + k, NZ - 1) * 16, 16), 16)
        out_ref[0:16, :] = low_ref[rows, :]
        out_ref[16:32, 0:512] = low_qkv_ref[rows, :]
        out_ref[16:32, 512:] = jnp.zeros((16, 512), BF)
    own_ref[32:48, :] = low_ref[64:80, :]


def reduce_x(where, ffn, qkv):
    return pl.pallas_call(
        reduce_x_kernel,
        grid=(1,),
        in_specs=[SM] + [VM] * 4 + [full(16, 64, 4 * PAIR)],
        out_specs=[VM] * 4,
        out_shape=[shape((48, D), BF)] + [shape((32, D), BF)] * 3,
        scratch_shapes=[pltpu.VMEM((80, D), BF), pltpu.VMEM((64, 4 * PAIR), BF)],
        compiler_params=params(),
        cost_estimate=cost(0),
        name="reduce_x",
    )(where, *ffn, keep_far(qkv))


UP, DOWN, PROJ, QKV, SMALL, WIDE = 0, 2048, 4096, 5120, 6656, 6784


def pack_kernel(where_ref, *refs):
    out_ref = refs[NZ]
    z = where_ref[1]
    small = jnp.zeros((16, 128), F32)
    for k in range(NZ):
        ring = jnp.bitwise_and(z + NZ - k, NZ - 1)
        ffn, qkv = refs[k][0:16, :], refs[k][16:32, :]
        small = small + qkv[:, 3 * PAIR : 4 * PAIR].astype(F32)
        for n in range(8):
            out_ref[n, :, pl.ds(pl.multiple_of(UP + ring * HID, HID), HID)] = ffn[:, :HID]
            out_ref[n, :, pl.ds(pl.multiple_of(DOWN + ring * HID, HID), HID)] = ffn[:, HID:]
            for part in range(3):
                place = pl.ds(pl.multiple_of(QKV + part * 512 + ring * PAIR, PAIR), PAIR)
                out_ref[n, :, place] = qkv[:, part * PAIR : (part + 1) * PAIR]
    for n in range(8):
        out_ref[n, :, PROJ:QKV] = refs[0][32:48, :]
        out_ref[n, :, SMALL:WIDE] = small.astype(BF)


def pack(where, own, others):
    return pl.pallas_call(
        pack_kernel,
        grid=(1,),
        in_specs=[SM] + [VM] * 4,
        out_specs=full(8, 16, WIDE),
        out_shape=far((8, 16, WIDE), BF),
        compiler_params=params(),
        cost_estimate=cost(0),
        name="pack",
    )(where, own, *others)


def merge_kernel(where_ref, mine_ref, theirs_ref, up_ref, down_ref, proj_ref, qkv_ref, small_ref):
    core = where_ref[0]
    native = where_ref[0] == where_ref[3]
    for side, ref in ((core, mine_ref), (1 - core, theirs_ref)):
        up_ref[:, pl.ds(pl.multiple_of(side * 2048, 2048), 2048)] = ref[:, UP:DOWN]
        down_ref[:, pl.ds(pl.multiple_of(side * 2048, 2048), 2048)] = ref[:, DOWN:PROJ]
        for part in range(3):
            place = pl.multiple_of(part * D + side * 512, 512)
            qkv_ref[:, pl.ds(place, 512)] = ref[:, QKV + part * 512 : QKV + (part + 1) * 512]

    @pl.when(native)
    def _():
        proj_ref[...] = mine_ref[:, PROJ:QKV]

    @pl.when(jnp.logical_not(native))
    def _():
        proj_ref[...] = theirs_ref[:, PROJ:QKV]

    for n in range(8):
        small_ref[2 * n : 2 * n + 2, :] = mine_ref[n * 16 : (n + 1) * 16, SMALL:WIDE].astype(F32)[
            0:2
        ] + theirs_ref[n * 16 : (n + 1) * 16, SMALL:WIDE].astype(F32)[0:2]


def merge(where, mine, theirs):
    return pl.pallas_call(
        merge_kernel,
        in_specs=[SM, VM, VM],
        out_specs=[VM] * 5,
        out_shape=[
            shape((128, FF), BF),
            shape((128, FF), BF),
            shape((128, D), BF),
            shape((128, 3 * D), BF),
            shape((16, 128), F32),
        ],
        compiler_params=params(),
        cost_estimate=cost(0),
        name="merge",
    )(where, mine, theirs)


def back_kernel(dqkv_ref, w_ref, ffn_ref, norm_ref, out_ref):
    dn1 = dot(dqkv_ref[...], w_ref[...], 1, 1)
    out_ref[...] = (dn1 * norm_ref[0:1, :] + ffn_ref[...].astype(F32)).astype(BF)


def back_theirs(dqkv, w, ffn_back, norms):
    moving = lambda i: (2 + i, 0)
    fixed = lambda i: (0, 0)
    return pl.pallas_call(
        back_kernel,
        grid=(2,),
        in_specs=[
            pl.BlockSpec((2 * ROWS, 3 * PAIR), moving),
            pl.BlockSpec((D, 3 * PAIR), fixed),
            pl.BlockSpec((2 * ROWS, D), moving),
            pl.BlockSpec((4, D), fixed),
        ],
        out_specs=pl.BlockSpec((2 * ROWS, D), lambda i: (i, 0)),
        out_shape=shape((SEQ // 2, D), BF),
        compiler_params=params(),
        cost_estimate=cost(0),
        name="back_theirs",
    )(dqkv, w, keep_far(ffn_back), norms)


def back_sum_kernel(dqkv_ref, w_ref, ffn_ref, norm_ref, other_ref, *out_refs):
    step = pl.program_id(0)
    dn1 = dot(dqkv_ref[...], w_ref[...], 1, 1)
    mine = (dn1 * norm_ref[0:1, :] + ffn_ref[...].astype(F32)).astype(BF)
    total = (mine.astype(F32) + other_ref[...].astype(F32)).astype(BF)
    for n in range(2):

        @pl.when(step == n)
        def _():
            out_refs[2 * n][...] = total[0:ROWS]
            out_refs[2 * n + 1][...] = total[ROWS:]


def back_sum(dqkv, w, ffn_back, norms, other):
    moving = lambda i: (i, 0)
    fixed = lambda i: (0, 0)
    return pl.pallas_call(
        back_sum_kernel,
        grid=(2,),
        in_specs=[
            pl.BlockSpec((2 * ROWS, 3 * PAIR), moving),
            pl.BlockSpec((D, 3 * PAIR), fixed),
            pl.BlockSpec((2 * ROWS, D), moving),
            pl.BlockSpec((4, D), fixed),
            pl.BlockSpec((2 * ROWS, D), moving),
        ],
        out_specs=[pl.BlockSpec((ROWS, D), fixed)] * NZ,
        out_shape=[far((ROWS, D), BF)] * NZ,
        compiler_params=params(),
        cost_estimate=cost(0),
        name="back_sum",
    )(dqkv, w, keep_far(ffn_back), norms, other)


def qkv_grad_kernel(meta_ref, xh_ref, dqkv_ref, w_ref, norm_ref, dy_ref, ffn_vec_ref, grad_ref, vec):
    part = meta_ref[6]
    dqkv = dqkv_ref[...]
    sums = jnp.broadcast_to(jnp.sum(dqkv.astype(F32), axis=0, keepdims=True), (8, 3 * PAIR))
    dy_sum = jnp.sum(dy_ref[...].astype(F32), axis=0, keepdims=True)
    raw = dot(xh_ref[...], dqkv, 0, 0)
    gain = jnp.transpose(jnp.broadcast_to(norm_ref[0:1, :], (8, D)))[:, 0:1]
    shift = jnp.transpose(jnp.broadcast_to(norm_ref[1:2, :], (8, D)))[:, 0:1]
    grad = (raw * gain + shift * sums[0:1, :]).astype(BF)
    for h in range(NXH):
        for p in range(8):
            for ring in range(NZ):
                first = (h * NZ + ring) * 128 + p * 16
                grad_ref[h * 8 + p, ring * 16 : (ring + 1) * 16, 0 : 3 * PAIR] = grad[first : first + 16]
    product = (raw * w_ref[...].astype(F32)).astype(BF)
    norm_rows = [
        dot(jnp.ones((8, 3 * PAIR), BF), product, 1, 1)[0:1],
        dot(sums.astype(BF), w_ref[...], 1, 1)[0:1],
        ffn_vec_ref[0:1, :],
        ffn_vec_ref[8:9, :],
    ]
    vec[...] = jnp.zeros_like(vec)

    def put(bias_row, values):
        place = bias_row + (bias_row // 9) * 7
        vec[pl.ds(place, 1), :] = values

    for n in range(3):
        put(n * 8 + part, sums[0:1, n * PAIR : (n + 1) * PAIR])
    for n in range(4):
        put(32 + part * 4 + n, ffn_vec_ref[16:17, n * 128 : (n + 1) * 128])
    for n in range(8):
        put(24 + n, dy_sum[:, n * 128 : (n + 1) * 128])
        put(64 + n, dy_sum[:, n * 128 : (n + 1) * 128])
        for r in range(4):
            vec[n * 16 + 9 + r : n * 16 + 10 + r, :] = norm_rows[r][:, n * 128 : (n + 1) * 128]
    for h in range(NXH):
        for p in range(8):
            for ring in range(NZ):
                first = (h * NZ + ring) * 16 + 2 * p
                grad_ref[h * 8 + p, ring * 16 : (ring + 1) * 16, 3 * PAIR :] = jnp.concatenate(
                    [vec[first : first + 2, :], jnp.zeros((14, 128), F32)], axis=0
                ).astype(BF)


def qkv_grad(meta, xh, dqkv, w, norms, dy, ffn_vec):
    return pl.pallas_call(
        qkv_grad_kernel,
        in_specs=[SM] + [VM] * 6,
        grid=(1,),
        out_specs=full(16, 64, 4 * PAIR),
        out_shape=far((16, 64, 4 * PAIR), BF),
        scratch_shapes=[pltpu.VMEM((128, 128), F32)],
        compiler_params=params(),
        cost_estimate=cost(0),
        name="qkv_grad",
    )(meta, xh, dqkv, w, norms, dy, ffn_vec)


def body(
    tokens, out_grad, segments, w_qkv, w_proj, w_up, w_down, norm_params, biases,
    prior_moment_qkv, prior_square_qkv, prior_moment_proj, prior_square_proj,
    prior_moment_up, prior_square_up, prior_moment_down, prior_square_down,
    prior_moment_norm, prior_square_norm, prior_moment_bias, prior_square_bias,
):
    rep, shard = lax.axis_index("rep"), lax.axis_index("shard")
    core, y = rep % NC, rep // (NC * NXL)
    where = jnp.stack([core, shard % NZ, y, shard // NZ, rep // NC % NXL]).astype(jnp.int32)

    x_mine = [permute(tokens, SPREAD[k]) for k in range(NZ)]
    docs = segments.astype(BF).reshape(2, 128)
    sent = send_weights(
        where, w_qkv, w_up, w_down, norm_params, biases.reshape(9, 128), docs, sibling(docs)
    )
    received = lax.all_to_all(sent, "shard", 0, 0, tiled=True)
    w_qkv_t, norms, bias, ffn_part, meta = assemble(where, received)
    turns = rotary_tables()
    x_joined = join(x_mine)
    dy_wide, _ = lax.optimization_barrier(
        (jnp.concatenate([out_grad, w_proj.astype(BF)], axis=0), x_joined)
    )
    dy_first = permute(dy_wide, SWAP)
    half = project_qkv(meta, x_joined, w_qkv_t, bias, norms, turns, None, 100)
    x_other = sibling(x_joined)
    n2, xh, q, k, v = project_qkv(meta, x_other, w_qkv_t, bias, norms, turns, half, 0)

    ffn_part = exchange(ffn_part, ALONG_Y)
    dy_block, _ = lax.optimization_barrier((dy_first[:ROWS], x_joined))
    dy_mine = around(dy_block)

    ctx, ctxt, stat = attn_forward(meta, q, k, v)
    ctx, dy_mine = lax.optimization_barrier((ctx, dy_mine))
    dy_joined = join(dy_mine)
    dy_joined, ffn_part = lax.optimization_barrier((dy_joined, ffn_part))
    w_up_t, w_down_t = assemble_ffn(ffn_part)
    dy_other = sibling(dy_joined)
    out_mine, out_theirs, ffn_back, dctx, ffn_vec, ffn_sent = feed_forward(
        meta, dy_joined, dy_other, n2, xh, ctx, w_up_t, w_down_t, dy_first, bias, norms
    )
    out_other = sibling(out_theirs)

    dqkv = attn_backward(meta, q, k, v, dctx, ctxt, stat, turns)
    qkv_sent = qkv_grad(meta, xh, dqkv, w_qkv_t, norms, out_grad, ffn_vec)
    out_pieces = back_around(core_sum(out_mine, out_other))
    out_sum = fold(out_pieces)
    dqkv, qkv_sent, out_sum, ffn_received = lax.optimization_barrier(
        (dqkv, qkv_sent, out_sum, exchange(ffn_sent, ALONG_Y))
    )

    ffn_parts = reduce_y(where, ffn_received)
    ffn_parts = [ffn_parts[0]] + [permute(ffn_parts[k], ROUND_X[k]) for k in (1, 2, 3)]
    qkv_received = exchange(qkv_sent, PLANE)
    dqkv, ffn_parts, qkv_received = lax.optimization_barrier((dqkv, ffn_parts, qkv_received))
    ffn_own, *ffn_others = reduce_x(where, ffn_parts, qkv_received)
    dqkv, ffn_own = lax.optimization_barrier((dqkv, ffn_own))
    w_theirs = back_theirs(dqkv, w_qkv_t, ffn_back, norms)
    block_out = finish_out(tokens, bias, permute(out_sum, SWAP))
    w_pieces = back_sum(dqkv, w_qkv_t, ffn_back, norms, sibling(w_theirs))
    ffn_others = [permute(b, ROUND_Z[k + 1]) for k, b in enumerate(ffn_others)]
    ffn_own, w_pieces = lax.optimization_barrier((ffn_own, w_pieces))
    mine_grad = exchange(pack(where, ffn_own, ffn_others), COPIES)
    mine_grad, block_out, w_sum = lax.optimization_barrier(
        (mine_grad, block_out, fold(back_around(w_pieces)))
    )
    mine_grad = mine_grad.reshape(128, WIDE)
    their_grad = sibling(mine_grad)
    g_up, g_down, g_proj, g_qkv, small = merge(where, mine_grad, their_grad)
    w_sum = permute(w_sum, SWAP)
    g_norm = small[9:13]
    g_bias = small[:9].reshape(1152)

    def matrix_step(weight, moment, square, grad):
        return adam_step(weight, moment, square, grad.astype(F32), RATE_MATRIX, DECAY)

    new_qkv = matrix_step(w_qkv, prior_moment_qkv, prior_square_qkv, g_qkv)
    new_proj = matrix_step(w_proj, prior_moment_proj, prior_square_proj, g_proj)
    new_up = matrix_step(w_up, prior_moment_up, prior_square_up, g_up)
    new_down = matrix_step(w_down, prior_moment_down, prior_square_down, g_down)
    w_sum, new_qkv = lax.optimization_barrier((w_sum, new_qkv))
    grad_tokens = finish_grad(tokens, out_grad, w_sum)
    new_norm = adam_step(norm_params, prior_moment_norm, prior_square_norm, g_norm, RATE_VECTOR, 0.0)
    new_bias = adam_step(biases, prior_moment_bias, prior_square_bias, g_bias, RATE_VECTOR, 0.0)
    return (block_out, grad_tokens, *new_qkv, *new_proj, *new_up, *new_down, *new_norm, *new_bias)


def solution(mesh):
    token = P(("rep", "shard"), None)
    row = P("shard", None)
    norm = P(None, "shard")
    flat = P("shard")
    in_specs = (
        (token, token, P(("rep", "shard")))
        + (row,) * 4
        + (norm, flat)
        + (row,) * 8
        + (norm, norm, flat, flat)
    )
    out_specs = (token, token) + (row,) * 12 + (norm,) * 3 + (flat,) * 3
    return jax.shard_map(body, mesh=mesh, in_specs=in_specs, out_specs=out_specs, check_vma=False)
```
